128 devices in a mesh: seq: 8 (over x, y_lo), tensor: 8 (over z, core), pool: 2 (over y_hi).
Axes of the slice: x: 4, y: 4 (y_hi: 2, y_lo: 2; y = y_hi * 2 + y_lo), z: 4, core: 2. Of those that a mesh axis runs over, the one named last changes fastest.
Arguments:
- pre_x: bfloat16 [8192, 8192], P(('seq', 'pool')), may hold values from -6 to 6
- w_query: bfloat16 [8192, 8192], P(None, 'tensor'), may hold values from -4 to 4
- w_key: bfloat16 [8192, 1024], P(None, 'tensor'), may hold values from -4 to 4
- w_value: bfloat16 [8192, 1024], P(None, 'tensor'), may hold values from -0.0625 to 0.0625
- dec_x: bfloat16 [4, 128, 8192], P(None, ('seq', 'pool'), 'tensor'), may hold values from -6 to 6
- cache: bfloat16 [2048, 16, 2, 1024], P(('seq', 'pool'), None, None, 'tensor'), may hold values from -6 to 6
- lengths: int32 [128], P(('seq', 'pool')), may hold values from 64 to 256, as said below
- page_table: int32 [128, 16], P(('seq', 'pool')), may hold values from 0 to 127, as said below
- dest_slots: int32 [16, 32], P(('seq', 'pool')), may hold values from 0 to 127, as said below
Outputs:
- pre_out: bfloat16 [8192, 8192], P(('seq', 'pool'), 'tensor')
- dec_out: bfloat16 [4, 128, 8192], P(None, ('seq', 'pool'), 'tensor')
The draws below stay inside these ranges and needn't reach their ends.
Inputs may be any that keep to these rules, and one draw needn't show every extreme that they name: `lengths`: every group of 8 rows has a row with the most. `page_table`: rows g * 8 to (g + 1) * 8 - 1 name pages of group g's pool; each of the group's 128 pages is named exactly once in the group's table. `dest_slots`: the slots of a group are distinct, and each is a page that the group's page table names within the live tokens of its row.
All inputs are finite; a program needn't handle non-finite values.
Results may differ from the reference program's by a relative error of at most 0.019.
Values may be sent and summed in bfloat16 or wider, within the bound.
A program may use at most 128 MiB of HBM per device.

```python
import jax
import jax.numpy as jnp
from jax import lax

D = 8192
KVH = 8
HD = 128
QH = 64
TOK_DEV = 512
PAGE = 16
MAXP = 16
ROWS_DEV = 8
STEPS = 4
SEQ_LEN = 8192
ROWS = 128
GROUPS = 16
PAGES_DEV = 128


def page_layout(key):
    groups = ROWS // ROWS_DEV
    new_count = TOK_DEV // PAGE

    def one_group(group):
        group_key = jax.random.fold_in(key, group)
        shuffled = jax.random.permutation(group_key, PAGES_DEV).astype(jnp.int32)
        row_order = jax.random.permutation(jax.random.fold_in(group_key, 7), ROWS_DEV).astype(jnp.int32)
        spot_high = row_order[0] * MAXP
        spot_low = row_order[1] * MAXP
        places = jnp.arange(PAGES_DEV, dtype=jnp.int32)
        highest = PAGES_DEV - 1
        held = shuffled[spot_high]
        shuffled = jnp.where(shuffled == highest, held, jnp.where(places == spot_high, highest, shuffled))
        held = shuffled[spot_low]
        shuffled = jnp.where(shuffled == 0, held, jnp.where(places == spot_low, 0, shuffled))
        table = shuffled.reshape(ROWS_DEV, MAXP)
        counter = jnp.arange(new_count, dtype=jnp.int32)
        slots = table[row_order[counter % ROWS_DEV], counter // ROWS_DEV]
        return (table, slots)
    tables, slots = jax.vmap(one_group)(jnp.arange(groups, dtype=jnp.int32))
    return (tables.reshape(ROWS, MAXP), slots)


def draw_page_table(key, part):
    layout = page_layout(key)
    return layout[0]


def draw_dest_slots(key, part):
    layout = page_layout(key)
    return layout[1]


def draw_lengths(key, part):
    key = jax.random.fold_in(key, 3)
    groups = ROWS // ROWS_DEV
    shortest = PAGE * ((TOK_DEV // PAGE + ROWS_DEV - 1) // ROWS_DEV)
    longest = MAXP * PAGE
    counts = jax.random.randint(key, (ROWS,), shortest, longest + 1, dtype=jnp.int32)
    chosen = jax.random.randint(jax.random.fold_in(key, 5), (groups,), 0, ROWS_DEV, dtype=jnp.int32)
    row_ids = jnp.arange(ROWS, dtype=jnp.int32)
    marked = row_ids % ROWS_DEV == chosen[row_ids // ROWS_DEV]
    return jnp.where(marked, longest, counts)


def draw_w_key(key, part):
    own_key = jax.random.fold_in(key, 11)
    regular = jnp.clip(jax.random.normal(own_key, (D, KVH * HD), jnp.float32), -6.0, 6.0) * D ** (-0.5)
    return regular.astype(jnp.bfloat16)


def draw_w_query(key, part):
    own_key = jax.random.fold_in(key, 13)
    regular = jnp.clip(jax.random.normal(own_key, (D, QH * HD), jnp.float32), -6.0, 6.0) * D ** (-0.5)
    return regular.astype(jnp.bfloat16)


def draw_pre_x(key, part):
    own_key = jax.random.fold_in(key, 21)
    return jnp.clip(jax.random.normal(own_key, (SEQ_LEN, D), jnp.float32), -6.0, 6.0).astype(jnp.bfloat16)


def draw_dec_x(key, part):
    own_key = jax.random.fold_in(key, 31)
    return jnp.clip(jax.random.normal(own_key, (STEPS, ROWS, D), jnp.float32), -6.0, 6.0).astype(jnp.bfloat16)


def steps_of(rng, extent, shards, low, high):
    factor_of, own = 1.0, jax.random.fold_in(rng, 6)
    for axis_at, parts in shards:
        heights = jnp.exp(jax.random.uniform(jax.random.fold_in(own, axis_at), (parts,), jnp.float32, low / len(shards), high / len(shards)))
        factor_of = factor_of * jnp.repeat(heights, extent[axis_at] // parts).reshape([-1 if axis == axis_at else 1 for axis in range(len(extent))])
    return factor_of


def scatter_about(rng, extent, width, reach, cuts=(), held_as=jnp.bfloat16):
    loudness = steps_of(rng, extent, cuts, -0.22, 0.18) if cuts else 1.0
    drawn = jax.random.normal(rng, extent, jnp.float32) * width * loudness
    return jnp.minimum(jnp.maximum(drawn, -reach), reach).astype(held_as)


def setup_inputs(seed: int = 0) -> dict:
    seeds = jax.random.split(jax.random.key(seed), 10)
    return {
        "pre_x": draw_pre_x(jax.random.fold_in(seeds[9], 71), 0),
        "w_query": draw_w_query(jax.random.fold_in(seeds[9], 71), 0),
        "w_key": draw_w_key(jax.random.fold_in(seeds[9], 71), 0),
        "w_value": scatter_about(seeds[3], (D, KVH * HD), D ** -0.5, 0.0625, ((1, 8),)),
        "dec_x": draw_dec_x(jax.random.fold_in(seeds[9], 71), 0),
        "cache": scatter_about(seeds[5], (GROUPS * PAGES_DEV, PAGE, 2, KVH * HD), 1.0, 6.0, ((0, 16), (3, 8))),
        "lengths": draw_lengths(jax.random.fold_in(seeds[9], 71), 0),
        "page_table": draw_page_table(jax.random.fold_in(seeds[9], 71), 0),
        "dest_slots": draw_dest_slots(jax.random.fold_in(seeds[9], 71), 0),
    }


def reference(pre_x, w_query, w_key, w_value, dec_x, cache, lengths, page_table, dest_slots):
    groups = ROWS // ROWS_DEV
    seq_total = pre_x.shape[0]
    share = QH // KVH
    score_scale = HD ** -0.5
    queries = jnp.dot(pre_x, w_query, preferred_element_type=jnp.float32).astype(jnp.bfloat16)
    queries = queries.reshape(seq_total, KVH, share, HD)
    key_rows = jnp.dot(pre_x, w_key, preferred_element_type=jnp.float32).astype(jnp.bfloat16)
    value_rows = jnp.dot(pre_x, w_value, preferred_element_type=jnp.float32).astype(jnp.bfloat16)
    key_heads = key_rows.reshape(seq_total, KVH, HD)
    value_heads = value_rows.reshape(seq_total, KVH, HD)
    blocks = seq_total // TOK_DEV
    key_pos = jnp.arange(seq_total, dtype=jnp.int32)

    def one_block(flat_index):
        head = flat_index // blocks
        block_index = flat_index % blocks
        q_block = lax.dynamic_slice_in_dim(queries, (block_index * TOK_DEV).astype(jnp.int32), TOK_DEV, 0)
        q_head = lax.dynamic_index_in_dim(q_block, head, 1, False)
        k_head = lax.dynamic_index_in_dim(key_heads, head, 1, False)
        v_head = lax.dynamic_index_in_dim(value_heads, head, 1, False)
        scores = jnp.einsum("tgd,kd->gtk", q_head.astype(jnp.float32), k_head.astype(jnp.float32)) * score_scale
        query_pos = block_index * TOK_DEV + jnp.arange(TOK_DEV, dtype=jnp.int32)
        allowed = key_pos[None, None, :] <= query_pos[None, :, None]
        scores = jnp.where(allowed, scores, -1e30)
        largest = jnp.max(scores, axis=-1)
        weights = jnp.where(allowed, jnp.exp(scores - largest[..., None]), 0.0)
        totals = jnp.sum(weights, axis=-1)
        rounded = lax.optimization_barrier(weights.astype(jnp.bfloat16)).astype(jnp.float32)
        mixed = jnp.einsum("gtk,kd->gtd", rounded, v_head.astype(jnp.float32)) / totals[..., None]
        return mixed.astype(jnp.bfloat16)

    pieces = lax.map(one_block, jnp.arange(KVH * blocks, dtype=jnp.int32))
    pre_out = pieces.reshape(KVH, blocks, share, TOK_DEV, HD).transpose(1, 3, 0, 2, 4).reshape(seq_total, QH * HD)

    per_group = TOK_DEV // (PAGE * groups)
    packed = jnp.stack([key_rows, value_rows], axis=1)
    packed = packed.reshape(groups, groups, per_group, PAGE, 2, KVH * HD)
    new_pages = packed.transpose(1, 0, 2, 3, 4, 5).reshape(groups, TOK_DEV // PAGE, PAGE, 2, KVH * HD)
    pool_all = cache.reshape(groups, PAGES_DEV, PAGE, 2, KVH * HD)
    pool_all = jax.vmap(lambda pages, slots, fresh: pages.at[slots].set(fresh))(pool_all, dest_slots, new_pages)

    flat_x = dec_x.reshape(STEPS * ROWS, D)
    dec_query = jnp.dot(flat_x, w_query, preferred_element_type=jnp.float32).astype(jnp.bfloat16)
    dec_query = dec_query.reshape(STEPS, ROWS, KVH, share, HD)
    dec_keys = jnp.dot(flat_x, w_key, preferred_element_type=jnp.float32).astype(jnp.bfloat16).reshape(STEPS, ROWS, KVH, HD)
    dec_values = jnp.dot(flat_x, w_value, preferred_element_type=jnp.float32).astype(jnp.bfloat16).reshape(STEPS, ROWS, KVH, HD)
    context_len = MAXP * PAGE
    causal = jnp.arange(STEPS, dtype=jnp.int32)[None, :] <= jnp.arange(STEPS, dtype=jnp.int32)[:, None]

    def one_row(row_index):
        group = row_index // ROWS_DEV
        pages_here = lax.dynamic_index_in_dim(pool_all, group, 0, False)
        table = lax.dynamic_index_in_dim(page_table, row_index, 0, False)
        context = pages_here[table].reshape(context_len, 2, KVH, HD).astype(jnp.float32)
        row_query = lax.dynamic_index_in_dim(dec_query, row_index, 1, False).astype(jnp.float32)
        row_keys = lax.dynamic_index_in_dim(dec_keys, row_index, 1, False).astype(jnp.float32)
        row_values = lax.dynamic_index_in_dim(dec_values, row_index, 1, False).astype(jnp.float32)
        live = jnp.arange(context_len, dtype=jnp.int32) < lengths[row_index]
        old_scores = jnp.einsum("shgd,khd->shgk", row_query, context[:, 0]) * score_scale
        old_scores = jnp.where(live[None, None, None, :], old_scores, -1e30)
        new_scores = jnp.einsum("shgd,thd->shgt", row_query, row_keys) * score_scale
        new_scores = jnp.where(causal[:, None, None, :], new_scores, -1e30)
        largest = jnp.maximum(jnp.max(old_scores, axis=-1), jnp.max(new_scores, axis=-1))
        old_weights = jnp.where(live[None, None, None, :], jnp.exp(old_scores - largest[..., None]), 0.0)
        new_weights = jnp.where(causal[:, None, None, :], jnp.exp(new_scores - largest[..., None]), 0.0)
        totals = jnp.sum(old_weights, axis=-1) + jnp.sum(new_weights, axis=-1)
        old_rounded = lax.optimization_barrier(old_weights.astype(jnp.bfloat16)).astype(jnp.float32)
        new_rounded = lax.optimization_barrier(new_weights.astype(jnp.bfloat16)).astype(jnp.float32)
        mixed = jnp.einsum("shgk,khd->shgd", old_rounded, context[:, 1]) + jnp.einsum("shgt,thd->shgd", new_rounded, row_values)
        mixed = mixed / totals[..., None]
        return mixed.reshape(STEPS, QH * HD).astype(jnp.bfloat16)

    dec_rows = lax.map(one_row, jnp.arange(ROWS, dtype=jnp.int32))
    dec_out = dec_rows.transpose(1, 0, 2)
    return pre_out, dec_out
```

```python
import functools

import jax
import jax.numpy as jnp
from jax import lax
from jax.experimental import pallas as pl
from jax.experimental.pallas import tpu as pltpu
from jax.sharding import PartitionSpec as P

MESH = pl.DeviceIdType.MESH
BF16 = jnp.bfloat16
F32 = jnp.float32

D = 8192
HD = 128
HEADS = 8
TOK = 512
GROUPS = 16
PAGE = 16
MAXP = 16
PAGES = 128
ROWS = 8
STEPS = 4
DEC = ROWS * STEPS
ALL = TOK + DEC
TILE_TOK = 64
TILES = TOK // TILE_TOK
TILE = TILE_TOK * HEADS
CACHE_ROWS = PAGES * PAGE * 2
NEW_ROWS = 512
SCALE = HD ** (-0.5) * 1.4426950408889634
LOW = -1e30
XC = 8
QK = 4
QN = 2
LENT = 4
TAKES = (4, 3, 3, 3, 2, 2, 1, 0)
JOIN = 3
EARLY = 9
TURNS = ((6,), (7, 8), (9, 10), (11,), (12,), (13,), (14,), (15,))

ORDER = (
    (0, 0), (3, 0), (1, 0), (0, 3), (0, 1), (2, 0), (3, 3), (3, 1),
    (1, 3), (1, 1), (2, 3), (2, 1), (0, 2), (3, 2), (1, 2), (2, 2),
)


def sends_after(event):
    near, far = event
    sends = []
    if near == 0 and far == 0:
        sends += [(0, "A+"), (0, "A-"), (1, "A+"), (1, "A-")]
    elif far == 0 and near == 3:
        sends += [(0, "A+")]
    elif far == 0 and near == 1:
        sends += [(1, "A-")]
    if far == 0:
        sends += [(0, "B+"), (0, "B-"), (1, "B+"), (1, "B-")]
    elif far == 3:
        sends += [(0, "B+")]
    elif far == 1:
        sends += [(1, "B-")]
    return sends


def seen_from(event, direction):
    near, far = event
    step = 1 if direction[1] == "+" else -1
    if direction[0] == "A":
        return ((near - step) % 4, far)
    return (near, (far - step) % 4)


SENDS = [(event, half, way) for event in ORDER for half, way in sends_after(event)]


def prefill(
    px, wq, wk, wv, dx,
    pre_out, dq_out, dkv_out, new_out,
    x_s, wkv_s, wq_s, kv_s, kt_s, va_s, of_s, q_s, pacc, acc, m_s, sa_s, sb_s,
    xsem, wksem, wvsem, qsem, dsem_own, dsend, drecv, ssem, rsem, qsend, qrecv, osend, orecv,
):
    seq, tensor, pool = lax.axis_index("seq"), lax.axis_index("tensor"), lax.axis_index("pool")
    x, y, core = seq // 2, pool * 2 + seq % 2, tensor % 2
    g = seq * 2 + pool
    low = g < 8
    other = 15 - g
    last = jnp.where(low, other, g)
    pair = jnp.where(low, g, other)
    count = sum(jnp.where(pair == k, TAKES[k], 0) for k in range(8))
    partner = {"seq": 7 - seq, "pool": 1 - pool}

    def place(near, far):
        ax, ay = (x + near) % 4, (y + far) % 4
        bx, by = (x + far) % 4, (y + near) % 4
        return jnp.where(core == 0, ax, bx), jnp.where(core == 0, ay, by)

    def slot_of(near, far):
        px_, py_ = place(near, far)
        return px_ * 4 + (py_ % 2) * 2 + py_ // 2

    def device(near, far):
        px_, py_ = place(near, far)
        return {"seq": px_ * 2 + py_ % 2, "pool": py_ // 2}

    ways = {"A+": device(1, 0), "A-": device(3, 0), "B+": device(0, 1), "B-": device(0, 3)}

    def x_copy(c):
        cols = pl.ds(pl.multiple_of(c * (D // XC), D // XC), D // XC)
        return pltpu.make_async_copy(px.at[:, cols], x_s.at[pl.ds(0, TOK), cols], xsem.at[c])

    def w_copy(c, ref, at, sem):
        rows = pl.ds(pl.multiple_of(c * (D // XC), D // XC), D // XC)
        return pltpu.make_async_copy(ref.at[rows, :], wkv_s.at[rows, pl.ds(at, HD)], sem.at[c])

    def q_copy(n, k):
        rows = pl.ds(k * (D // QK), D // QK)
        cols = pl.ds(n * (HEADS * HD // QN), HEADS * HD // QN)
        return pltpu.make_async_copy(wq.at[rows, cols], wq_s.at[rows, cols], qsem.at[n * QK + k])

    my_cols = pl.ds(pl.multiple_of(tensor * (D // 8), D // 8), D // 8)
    dec_own = pltpu.make_async_copy(dx, x_s.at[pl.ds(TOK, DEC), my_cols], dsem_own)

    for c in range(XC):
        x_copy(c).start()
        w_copy(c, wk, 0, wksem).start()
        w_copy(c, wv, HD, wvsem).start()
    dec_own.start()
    for n in range(QN):
        for k in range(QK):
            q_copy(n, k).start()

    barrier = pltpu.get_barrier_semaphore()
    for way in ways.values():
        pl.semaphore_signal(barrier, inc=1, device_id=way, device_id_type=MESH)
    pl.semaphore_signal(barrier, inc=1, device_id=partner, device_id_type=MESH)
    for k in range(1, 8):
        pl.semaphore_signal(
            barrier, inc=1, device_id={"tensor": (tensor + k) % 8}, device_id_type=MESH
        )
    pl.semaphore_wait(barrier, 12)

    def dec_copy(k):
        return pltpu.make_async_remote_copy(
            src_ref=dx,
            dst_ref=x_s.at[pl.ds(TOK, DEC), my_cols],
            send_sem=dsend.at[k - 1],
            recv_sem=drecv.at[k - 1],
            device_id={"tensor": (tensor + k) % 8},
            device_id_type=MESH,
        )

    def dec_arrival(k):
        cols = pl.ds(pl.multiple_of(((tensor + 8 - k) % 8) * (D // 8), D // 8), D // 8)
        return pltpu.make_async_remote_copy(
            src_ref=dx,
            dst_ref=x_s.at[pl.ds(TOK, DEC), cols],
            send_sem=dsend.at[k - 1],
            recv_sem=drecv.at[k - 1],
            device_id={"tensor": (tensor + k) % 8},
            device_id_type=MESH,
        )

    for k in range(1, 8):
        dec_copy(k).start()

    def kv_copy(number):
        event, half, way = SENDS[number]
        slot = slot_of(*event)
        near, far = seen_from(event, way)
        return pltpu.make_async_remote_copy(
            src_ref=kv_s.at[slot, half],
            dst_ref=kv_s.at[slot, half],
            send_sem=ssem.at[number],
            recv_sem=rsem.at[(near * 4 + far) * 2 + half],
            device_id=ways[way],
            device_id_type=MESH,
        )

    def pass_on(event):
        for number, (of, _, _) in enumerate(SENDS):
            if of == event:
                kv_copy(number).start()

    def arrive(event):
        near, far = event
        slot = slot_of(near, far)
        for half in range(2):
            pltpu.make_async_remote_copy(
                src_ref=kv_s.at[slot, half],
                dst_ref=kv_s.at[slot, half],
                send_sem=ssem.at[0],
                recv_sem=rsem.at[(near * 4 + far) * 2 + half],
                device_id=ways["A+"],
                device_id_type=MESH,
            ).wait_recv()
        pass_on(event)

    def lend(t, n):
        rows = pl.ds(n * (TILE // QN), TILE // QN)
        return pltpu.make_async_remote_copy(
            src_ref=q_s.at[TILES - LENT + t, rows],
            dst_ref=q_s.at[TILES + t + count - LENT, rows],
            send_sem=qsend.at[t * QN + n],
            recv_sem=qrecv.at[t * QN + n],
            device_id=partner,
            device_id_type=MESH,
        )

    def give_back(f):
        at = pl.ds(pl.multiple_of((TILES - count + f) * TILE_TOK, TILE_TOK), TILE_TOK)
        return pltpu.make_async_remote_copy(
            src_ref=of_s.at[f],
            dst_ref=pre_out.at[at, :],
            send_sem=osend.at[f],
            recv_sem=orecv.at[f],
            device_id=partner,
            device_id_type=MESH,
        )

    def lent(t):
        return count >= LENT - t

    def clear(j, carry):
        acc[j] = jnp.zeros((TILE, 2 * HD), F32)
        m_s[j] = jnp.full((TILE, HD), LOW, F32)
        return carry

    def fill(i, carry):
        va_s[i, :, HD:] = jnp.ones((TOK, HD), BF16)
        return carry

    lax.fori_loop(0, TILES + LENT, clear, 0)
    lax.fori_loop(0, GROUPS, fill, 0)

    def kv_step(c, carry):
        x_copy(c).wait()
        w_copy(c, wk, 0, wksem).wait()
        w_copy(c, wv, HD, wvsem).wait()
        at = pl.ds(pl.multiple_of(c * (D // XC), D // XC), D // XC)
        part = jnp.dot(x_s[0:TOK, at], wkv_s[at, :], preferred_element_type=F32)

        @pl.when(c == 0)
        def _():
            pacc[0:TOK, 0:256] = part

        @pl.when(c > 0)
        def _():
            pacc[0:TOK, 0:256] += part

        return carry

    lax.fori_loop(0, XC, kv_step, 0)
    kv_s[g, 0] = pacc[0:TOK, 0:HD].astype(BF16)
    kv_s[g, 1] = pacc[0:TOK, HD : 2 * HD].astype(BF16)
    pass_on(ORDER[0])

    dec_own.wait()
    for k in range(1, 8):
        dec_arrival(k).wait_recv()

    width = HEADS * HD // QN
    for n in range(QN):
        for k in range(QK):
            q_copy(n, k).wait()
            at = slice(k * (D // QK), (k + 1) * (D // QK))
            part = jnp.dot(
                x_s[:, at], wq_s[at, n * width : (n + 1) * width], preferred_element_type=F32
            )
            if k == 0:
                pacc[...] = part
            else:
                pacc[...] += part
        for hh in range(HEADS // QN):
            h = n * (HEADS // QN) + hh
            for j in range(TILES):
                q_s[j, h * TILE_TOK : (h + 1) * TILE_TOK, :] = (
                    pacc[j * TILE_TOK : (j + 1) * TILE_TOK, hh * HD : (hh + 1) * HD] * SCALE
                ).astype(BF16)
            dq_out[h * DEC : (h + 1) * DEC, :] = (
                pacc[TOK:ALL, hh * HD : (hh + 1) * HD] * SCALE
            ).astype(BF16)
        for t in range(LENT):

            @pl.when(jnp.logical_not(low) & lent(t))
            def _():
                lend(t, n).start()

        if n == 0:
            arrive(ORDER[1])
            arrive(ORDER[2])
    dkv = jnp.dot(x_s[TOK:ALL, :], wkv_s[...], preferred_element_type=F32)
    dkv_out[0] = dkv[:, 0:HD].astype(BF16)
    dkv_out[1] = dkv[:, HD : 2 * HD].astype(BF16)

    for event in ORDER[3:6]:
        arrive(event)

    def prepare(i, slot):
        kt_s[i] = kv_s[slot, 0].T
        va_s[i, :, 0:HD] = kv_s[slot, 1]

    def score(item, buf):
        j, i = item
        buf[...] = jnp.dot(q_s[j], kt_s[i], preferred_element_type=F32)

    def absorb(item, buf, masked):
        j, i = item
        cuts = [buf[:, k * HD : (k + 1) * HD] for k in range(TOK // HD)]
        if masked:
            first = jnp.where(j < TILES, j, j - count) * TILE_TOK
            row = (lax.broadcasted_iota(jnp.int32, (TILE, HD), 0) & (TILE_TOK - 1)) + first
            ahead = lax.broadcasted_iota(jnp.int32, (TILE, HD), 1) - row
            cuts = [jnp.where(ahead <= -k * HD, c, LOW) for k, c in enumerate(cuts)]
        old = m_s[j]
        best = functools.reduce(jnp.maximum, cuts)
        top = jnp.maximum(
            old, jnp.broadcast_to(jnp.max(best, axis=1, keepdims=True), (TILE, HD))
        )
        p = jnp.concatenate([jnp.exp2(c - top).astype(BF16) for c in cuts], axis=1)
        o = jnp.dot(p, va_s[i], preferred_element_type=F32)
        shrink = jnp.exp2(old - top)
        acc[j] = acc[j] * jnp.concatenate([shrink, shrink], axis=1) + o
        m_s[j] = top

    def run(n, item, masked):
        @pl.when(n > 0)
        def _():
            score(item(0), sa_s)

        def two(t, carry):
            score(item(2 * t + 1), sb_s)
            absorb(item(2 * t), sa_s, masked)
            score(item(jnp.minimum(2 * t + 2, n - 1)), sa_s)
            absorb(item(2 * t + 1), sb_s, masked)
            return carry

        lax.fori_loop(0, n // 2, two, 0)

        @pl.when(n % 2 == 1)
        def _():
            absorb(item(n - 1), sa_s, masked)

    own = jnp.where(low, TILES, TILES - count)
    every = jnp.where(low, TILES + count, own)

    prepare(0, g)
    run(own, lambda t: (t, 0), True)

    def slot_at(i):
        near = sum(jnp.where(i == e, ORDER[e][0], 0) for e in range(16))
        far = sum(jnp.where(i == e, ORDER[e][1], 0) for e in range(16))
        return slot_of(near, far)

    def block(i, carry):
        for turn, events in enumerate(TURNS):

            @pl.when(i == turn + 1)
            def _():
                for e in events:
                    arrive(ORDER[e])

        @pl.when(i == JOIN)
        def _():
            for t in range(LENT):
                for n in range(QN):

                    @pl.when(low & lent(t))
                    def _():
                        lend(t, n).wait_recv()

        slot = slot_at(i)
        joined = (i >= JOIN) & (i <= EARLY)

        @pl.when(slot <= last)
        def _():
            prepare(i, slot)

        start = jnp.where(slot < g, 0, TILES)
        stop = jnp.where(joined, every, own)
        n = jnp.where(slot < last, jnp.maximum(stop - start, 0), 0)
        run(n, lambda t: (start + t, i), False)

        @pl.when(joined & (slot == last))
        def _():
            run(every - TILES, lambda t: (TILES + t, i), True)

        return carry

    lax.fori_loop(1, EARLY + 1, block, 0)

    def prepare_late(i, carry):
        slot = slot_at(i)

        @pl.when(slot <= last)
        def _():
            prepare(i, slot)

        return carry

    lax.fori_loop(EARLY + 1, 16, prepare_late, 0)

    def finish(j, h):
        rows = slice(h * TILE_TOK, (h + 1) * TILE_TOK)
        return (acc[j, rows, 0:HD] / acc[j, rows, HD:]).astype(BF16)

    due = [e for e in range(16) if e < JOIN or e > EARLY]
    wanted = [jnp.where(slot_of(*ORDER[e]) < last, 1, 0) for e in due]
    before = [sum(wanted[:k], jnp.int32(0)) for k in range(len(due))]

    def due_at(t):
        return sum(
            jnp.where((wanted[k] == 1) & (before[k] == t), due[k], 0) for k in range(len(due))
        )

    def late(j, carry):
        run(before[-1] + wanted[-1], lambda t: (j, due_at(t)), False)
        for h in range(HEADS):
            of_s[j - TILES, :, h * HD : (h + 1) * HD] = finish(j, h)
        for f in range(LENT):

            @pl.when(j == TILES + f)
            def _():
                give_back(f).start()

        return carry

    lax.fori_loop(TILES, every, late, 0)

    def late_own(i, carry):
        run(jnp.where(slot_at(i) < g, own, 0), lambda t: (t, i), False)
        return carry

    lax.fori_loop(EARLY + 1, 16, late_own, 0)

    for j in range(TILES):

        @pl.when(j < own)
        def _():
            for h in range(HEADS):
                pre_out[j * TILE_TOK : (j + 1) * TILE_TOK, h * HD : (h + 1) * HD] = finish(j, h)

    mine = NEW_ROWS // GROUPS
    at = pl.ds(pl.multiple_of(g * mine, mine), mine)
    for src in range(GROUPS):
        for half in range(2):
            new_out[half, src * mine : (src + 1) * mine, :] = kv_s[src, half, at, :]

    for t in range(LENT):

        @pl.when((t < count) & low)
        def _():
            give_back(t).wait_send()

        @pl.when(lent(t) & jnp.logical_not(low))
        def _():
            for n in range(QN):
                lend(t, n).wait_send()

        @pl.when((t < count) & jnp.logical_not(low))
        def _():
            give_back(t).wait_recv()

    for k in range(1, 8):
        dec_copy(k).wait_send()
    for number in range(len(SENDS)):
        kv_copy(number).wait_send()


def decode(
    table, lens, dest, pre_in, cache, dq, dkv, new,
    pre_out, dec_out,
    cf_s, sd_s, sem,
):
    hand_on = pltpu.make_async_copy(pre_in, pre_out, sem)
    hand_on.start()
    cf_s[...] = cache[...].astype(F32)
    tokens = PAGES * PAGE

    lane = lax.broadcasted_iota(jnp.int32, (1, PAGES), 1)
    limits = []
    for r in range(ROWS):
        limit = jnp.zeros((1, PAGES), jnp.int32)
        for j in range(MAXP):
            left = jnp.clip(lens[r] - j * PAGE, 0, PAGE)
            limit = jnp.where(lane == table[r, j], left, limit)
        limits.append(limit)
    limit = jnp.concatenate(limits, axis=0).astype(F32)
    new_page = lax.broadcasted_iota(jnp.int32, (1, NEW_ROWS), 1) >> 4
    new_slot = jnp.zeros((1, NEW_ROWS), jnp.int32)
    replaced = jnp.zeros((1, PAGES), jnp.int32)
    for m in range(TOK // PAGE):
        new_slot = jnp.where(new_page == m, dest[0, m], new_slot)
        replaced = jnp.where(lane == dest[0, m], 1, replaced)
    old_limit = jnp.where(replaced == 1, 0.0, limit).astype(BF16)

    def bias(limit, page):
        total = page.shape[1]
        pick = jnp.where(
            lax.broadcasted_iota(jnp.int32, (PAGES, total), 0) == page, 1.0, 0.0
        ).astype(BF16)
        held = jnp.dot(limit, pick, preferred_element_type=F32)
        offset = lax.broadcasted_iota(jnp.int32, (1, total), 1) & (PAGE - 1)
        return jnp.where(offset.astype(F32) < held, 0.0, LOW)

    def scores(keys):
        return lax.dot_general(
            dq[...], keys, (((1,), (1,)), ((), ())), preferred_element_type=F32
        )

    def over_queries(mask):
        return jnp.broadcast_to(mask[None], (HEADS * STEPS, *mask.shape)).reshape(
            HEADS * DEC, mask.shape[1]
        )

    query_row = lax.broadcasted_iota(jnp.int32, (HEADS * DEC, DEC), 0)
    key_row = lax.broadcasted_iota(jnp.int32, (HEADS * DEC, DEC), 1)
    tok_ok = ((query_row & (ROWS - 1)) == (key_row & (ROWS - 1))) & (
        (key_row >> 3) <= ((query_row & (DEC - 1)) >> 3)
    )
    part = 512
    parts = tokens // part
    s_tok = jnp.where(tok_ok, scores(dkv[0]), LOW)
    top = jnp.max(s_tok, axis=1, keepdims=True)
    s_new = scores(new[0]) + over_queries(bias(limit.astype(BF16), new_slot))
    top = jnp.maximum(top, jnp.max(s_new, axis=1, keepdims=True))
    for i in range(parts):
        cols = slice(i * part, (i + 1) * part)
        page = (lax.broadcasted_iota(jnp.int32, (1, part), 1) >> 4) + i * (part // PAGE)
        keys = cf_s[pl.ds(2 * i * part, part, stride=2), :].astype(BF16)
        s_old = scores(keys) + over_queries(bias(old_limit, page))
        sd_s[:, cols] = s_old
        top = jnp.maximum(top, jnp.max(s_old, axis=1, keepdims=True))
    p = jnp.exp2(s_tok - top)
    total = jnp.sum(p, axis=1, keepdims=True)
    mixed = jnp.dot(p.astype(BF16), dkv[1], preferred_element_type=F32)
    p = jnp.exp2(s_new - top)
    total = total + jnp.sum(p, axis=1, keepdims=True)
    mixed = mixed + jnp.dot(p.astype(BF16), new[1], preferred_element_type=F32)
    for i in range(parts):
        p = jnp.exp2(sd_s[:, i * part : (i + 1) * part] - top)
        total = total + jnp.sum(p, axis=1, keepdims=True)
        values = cf_s[pl.ds(2 * i * part + 1, part, stride=2), :].astype(BF16)
        mixed = mixed + jnp.dot(p.astype(BF16), values, preferred_element_type=F32)
    mixed = mixed / total
    for h in range(HEADS):
        dec_out[:, h * HD : (h + 1) * HD] = mixed[h * DEC : (h + 1) * DEC, :].astype(BF16)
    hand_on.wait()


def per_device(pre_x, w_query, w_key, w_value, dec_x, cache, lengths, page_table, dest_slots):
    hbm = pl.BlockSpec(memory_space=pltpu.MemorySpace.HBM)
    vmem = pl.BlockSpec(memory_space=pltpu.MemorySpace.VMEM)
    smem = pl.BlockSpec(memory_space=pltpu.MemorySpace.SMEM)
    pre, dq, dkv, new = pl.pallas_call(
        prefill,
        out_shape=(
            jax.ShapeDtypeStruct((TOK, HEADS * HD), BF16),
            jax.ShapeDtypeStruct((HEADS * DEC, HD), BF16),
            jax.ShapeDtypeStruct((2, DEC, HD), BF16),
            jax.ShapeDtypeStruct((2, NEW_ROWS, HD), BF16),
        ),
        in_specs=[hbm] * 5,
        out_specs=(vmem,) * 4,
        scratch_shapes=[
            pltpu.VMEM((ALL, D), BF16),
            pltpu.VMEM((D, 2 * HD), BF16),
            pltpu.VMEM((D, HEADS * HD), BF16),
            pltpu.VMEM((GROUPS, 2, TOK, HD), BF16),
            pltpu.VMEM((GROUPS, HD, TOK), BF16),
            pltpu.VMEM((GROUPS, TOK, 2 * HD), BF16),
            pltpu.VMEM((LENT, TILE_TOK, HEADS * HD), BF16),
            pltpu.VMEM((TILES + LENT, TILE, HD), BF16),
            pltpu.VMEM((ALL, HEADS * HD // QN), F32),
            pltpu.VMEM((TILES + LENT, TILE, 2 * HD), F32),
            pltpu.VMEM((TILES + LENT, TILE, HD), F32),
            pltpu.VMEM((TILE, TOK), F32),
            pltpu.VMEM((TILE, TOK), F32),
            pltpu.SemaphoreType.DMA((XC,)),
            pltpu.SemaphoreType.DMA((XC,)),
            pltpu.SemaphoreType.DMA((XC,)),
            pltpu.SemaphoreType.DMA((QN * QK,)),
            pltpu.SemaphoreType.DMA,
            pltpu.SemaphoreType.DMA((7,)),
            pltpu.SemaphoreType.DMA((7,)),
            pltpu.SemaphoreType.DMA((len(SENDS),)),
            pltpu.SemaphoreType.DMA((32,)),
            pltpu.SemaphoreType.DMA((LENT * QN,)),
            pltpu.SemaphoreType.DMA((LENT * QN,)),
            pltpu.SemaphoreType.DMA((LENT,)),
            pltpu.SemaphoreType.DMA((LENT,)),
        ],
        compiler_params=pltpu.CompilerParams(
            collective_id=0, has_side_effects=True, vmem_limit_bytes=63 * 1024 * 1024
        ),
    )(pre_x, w_query, w_key, w_value, dec_x.reshape(DEC, D // 8))
    pre_out, dec_out = pl.pallas_call(
        decode,
        out_shape=(
            jax.ShapeDtypeStruct((TOK, HEADS * HD), BF16),
            jax.ShapeDtypeStruct((DEC, HEADS * HD), BF16),
        ),
        in_specs=[smem] * 3 + [hbm] + [vmem] * 4,
        out_specs=(hbm, vmem),
        scratch_shapes=[
            pltpu.VMEM((CACHE_ROWS, HD), F32),
            pltpu.VMEM((HEADS * DEC, PAGES * PAGE), F32),
            pltpu.SemaphoreType.DMA,
        ],
        compiler_params=pltpu.CompilerParams(vmem_limit_bytes=63 * 1024 * 1024),
    )(page_table, lengths, dest_slots, pre, cache.reshape(CACHE_ROWS, HD), dq, dkv, new)
    return pre_out, dec_out.reshape(STEPS, ROWS, HEADS * HD)


def solution(mesh):
    in_specs = (
        P(("seq", "pool"), None),
        P(None, "tensor"),
        P(None, "tensor"),
        P(None, "tensor"),
        P(None, ("seq", "pool"), "tensor"),
        P(("seq", "pool"), None, None, "tensor"),
        P(("seq", "pool")),
        P(("seq", "pool"), None),
        P(("seq", "pool"), None),
    )
    out_specs = (P(("seq", "pool"), "tensor"), P(None, ("seq", "pool"), "tensor"))
    return jax.shard_map(
        per_device, mesh=mesh, in_specs=in_specs, out_specs=out_specs, check_vma=False
    )
```

```python
import functools

import jax
import jax.numpy as jnp
from jax import lax
from jax.experimental import pallas as pl
from jax.experimental.pallas import tpu as pltpu
from jax.sharding import PartitionSpec as P

MESH = pl.DeviceIdType.MESH
BF16 = jnp.bfloat16
F32 = jnp.float32

D = 8192
HD = 128
HEADS = 8
TOK = 512
GROUPS = 16
PAGE = 16
MAXP = 16
PAGES = 128
ROWS = 8
STEPS = 4
DEC = ROWS * STEPS
ALL = TOK + DEC
TILE_TOK = 64
TILES = TOK // TILE_TOK
TILE = TILE_TOK * HEADS
CACHE_ROWS = PAGES * PAGE * 2
NEW_ROWS = 512
SCALE = HD ** (-0.5) * 1.4426950408889634
LOW = -1e30
XC = 8
QK = 4
QN = 2
LENT = 4
TAKES = (4, 3, 3, 2, 2, 1, 1, 0)
PAIRS = GROUPS // 2
CHUNK = 16
TURNS = ((), (6, 7), (8, 9), (10, 11), (12, 13, 14, 15))

ORDER = (
    (0, 0), (3, 0), (1, 0), (0, 3), (0, 1), (2, 0), (3, 3), (3, 1),
    (1, 3), (1, 1), (2, 3), (2, 1), (0, 2), (3, 2), (1, 2), (2, 2),
)


def sends_after(event):
    near, far = event
    sends = []
    if near == 0 and far == 0:
        sends += [(0, "A+"), (0, "A-"), (1, "A+"), (1, "A-")]
    elif far == 0 and near == 3:
        sends += [(0, "A+")]
    elif far == 0 and near == 1:
        sends += [(1, "A-")]
    if far == 0:
        sends += [(0, "B+"), (0, "B-"), (1, "B+"), (1, "B-")]
    elif far == 3:
        sends += [(0, "B+")]
    elif far == 1:
        sends += [(1, "B-")]
    return sends


def seen_from(event, direction):
    near, far = event
    step = 1 if direction[1] == "+" else -1
    if direction[0] == "A":
        return ((near - step) % 4, far)
    return (near, (far - step) % 4)


SENDS = [(event, half, way) for event in ORDER for half, way in sends_after(event)]


def prefill(
    px, wq, wk, wv, dx,
    pre_out, dq_out, dkv_out, new_out,
    x_s, wkv_s, wq_s, kv_s, kt_s, va_s, of_s, q_s, pacc, acc, m_s, sa_s, sb_s, pa_s, pb_s,
    xsem, wksem, wvsem, qsem, dsem_own, dsend, drecv, ssem, rsem, qsend, qrecv, osend, orecv,
):
    seq, tensor, pool = lax.axis_index("seq"), lax.axis_index("tensor"), lax.axis_index("pool")
    x, y, core = seq // 2, pool * 2 + seq % 2, tensor % 2
    g = seq * 2 + pool
    low = g < 8
    other = 15 - g
    last = jnp.where(low, other, g)
    pair = jnp.where(low, g, other)
    count = sum(jnp.where(pair == k, TAKES[k], 0) for k in range(8))
    partner = {"seq": 7 - seq, "pool": 1 - pool}

    def place(near, far):
        ax, ay = (x + near) % 4, (y + far) % 4
        bx, by = (x + far) % 4, (y + near) % 4
        return jnp.where(core == 0, ax, bx), jnp.where(core == 0, ay, by)

    def slot_of(near, far):
        px_, py_ = place(near, far)
        return px_ * 4 + (py_ % 2) * 2 + py_ // 2

    def device(near, far):
        px_, py_ = place(near, far)
        return {"seq": px_ * 2 + py_ % 2, "pool": py_ // 2}

    ways = {"A+": device(1, 0), "A-": device(3, 0), "B+": device(0, 1), "B-": device(0, 3)}

    def x_copy(c):
        cols = pl.ds(pl.multiple_of(c * (D // XC), D // XC), D // XC)
        return pltpu.make_async_copy(px.at[:, cols], x_s.at[pl.ds(0, TOK), cols], xsem.at[c])

    def w_copy(c, ref, at, sem):
        rows = pl.ds(pl.multiple_of(c * (D // XC), D // XC), D // XC)
        return pltpu.make_async_copy(ref.at[rows, :], wkv_s.at[rows, pl.ds(at, HD)], sem.at[c])

    def q_copy(n, k):
        rows = pl.ds(k * (D // QK), D // QK)
        cols = pl.ds(n * (HEADS * HD // QN), HEADS * HD // QN)
        return pltpu.make_async_copy(wq.at[rows, cols], wq_s.at[rows, cols], qsem.at[n * QK + k])

    my_cols = pl.ds(pl.multiple_of(tensor * (D // 8), D // 8), D // 8)
    dec_own = pltpu.make_async_copy(dx, x_s.at[pl.ds(TOK, DEC), my_cols], dsem_own)

    for c in range(XC):
        x_copy(c).start()
        w_copy(c, wk, 0, wksem).start()
        w_copy(c, wv, HD, wvsem).start()
    dec_own.start()
    for n in range(QN):
        for k in range(QK):
            q_copy(n, k).start()

    barrier = pltpu.get_barrier_semaphore()
    for way in ways.values():
        pl.semaphore_signal(barrier, inc=1, device_id=way, device_id_type=MESH)
    pl.semaphore_signal(barrier, inc=1, device_id=partner, device_id_type=MESH)
    for k in range(1, 8):
        pl.semaphore_signal(
            barrier, inc=1, device_id={"tensor": (tensor + k) % 8}, device_id_type=MESH
        )
    pl.semaphore_wait(barrier, 12)

    def dec_copy(k):
        return pltpu.make_async_remote_copy(
            src_ref=dx,
            dst_ref=x_s.at[pl.ds(TOK, DEC), my_cols],
            send_sem=dsend.at[k - 1],
            recv_sem=drecv.at[k - 1],
            device_id={"tensor": (tensor + k) % 8},
            device_id_type=MESH,
        )

    def dec_arrival(k):
        cols = pl.ds(pl.multiple_of(((tensor + 8 - k) % 8) * (D // 8), D // 8), D // 8)
        return pltpu.make_async_remote_copy(
            src_ref=dx,
            dst_ref=x_s.at[pl.ds(TOK, DEC), cols],
            send_sem=dsend.at[k - 1],
            recv_sem=drecv.at[k - 1],
            device_id={"tensor": (tensor + k) % 8},
            device_id_type=MESH,
        )

    for k in range(1, 8):
        dec_copy(k).start()

    def kv_copy(number):
        event, half, way = SENDS[number]
        slot = slot_of(*event)
        near, far = seen_from(event, way)
        return pltpu.make_async_remote_copy(
            src_ref=kv_s.at[slot, half],
            dst_ref=kv_s.at[slot, half],
            send_sem=ssem.at[number],
            recv_sem=rsem.at[(near * 4 + far) * 2 + half],
            device_id=ways[way],
            device_id_type=MESH,
        )

    def pass_on(event):
        for number, (of, _, _) in enumerate(SENDS):
            if of == event:
                kv_copy(number).start()

    def arrive(event):
        near, far = event
        slot = slot_of(near, far)
        for half in range(2):
            pltpu.make_async_remote_copy(
                src_ref=kv_s.at[slot, half],
                dst_ref=kv_s.at[slot, half],
                send_sem=ssem.at[0],
                recv_sem=rsem.at[(near * 4 + far) * 2 + half],
                device_id=ways["A+"],
                device_id_type=MESH,
            ).wait_recv()
        pass_on(event)

    def lend(t, n):
        rows = pl.ds(n * (TILE // QN), TILE // QN)
        return pltpu.make_async_remote_copy(
            src_ref=q_s.at[TILES - LENT + t, rows],
            dst_ref=q_s.at[TILES + t + count - LENT, rows],
            send_sem=qsend.at[t * QN + n],
            recv_sem=qrecv.at[t * QN + n],
            device_id=partner,
            device_id_type=MESH,
        )

    def give_back(f):
        at = pl.ds(pl.multiple_of((TILES - count + f) * TILE_TOK, TILE_TOK), TILE_TOK)
        return pltpu.make_async_remote_copy(
            src_ref=of_s.at[f],
            dst_ref=pre_out.at[at, :],
            send_sem=osend.at[f],
            recv_sem=orecv.at[f],
            device_id=partner,
            device_id_type=MESH,
        )

    def lent(t):
        return count >= LENT - t

    def clear(j, carry):
        acc[j] = jnp.zeros((TILE, 2 * HD), F32)
        m_s[j] = jnp.full((TILE, HD), LOW, F32)
        return carry

    def fill(i, carry):
        va_s[i, :, HD:] = jnp.ones((2 * TOK, HD), BF16)
        return carry

    lax.fori_loop(0, TILES + LENT, clear, 0)
    lax.fori_loop(0, PAIRS, fill, 0)

    def kv_step(c, carry):
        x_copy(c).wait()
        w_copy(c, wk, 0, wksem).wait()
        w_copy(c, wv, HD, wvsem).wait()
        at = pl.ds(pl.multiple_of(c * (D // XC), D // XC), D // XC)
        part = jnp.dot(x_s[0:TOK, at], wkv_s[at, :], preferred_element_type=F32)

        @pl.when(c == 0)
        def _():
            pacc[0:TOK, 0:256] = part

        @pl.when(c > 0)
        def _():
            pacc[0:TOK, 0:256] += part

        return carry

    lax.fori_loop(0, XC, kv_step, 0)
    kv_s[g, 0] = pacc[0:TOK, 0:HD].astype(BF16)
    kv_s[g, 1] = pacc[0:TOK, HD : 2 * HD].astype(BF16)
    pass_on(ORDER[0])

    dec_own.wait()
    for k in range(1, 8):
        dec_arrival(k).wait_recv()

    width = HEADS * HD // QN
    for n in range(QN):
        for k in range(QK):
            q_copy(n, k).wait()
            at = slice(k * (D // QK), (k + 1) * (D // QK))
            part = jnp.dot(
                x_s[:, at], wq_s[at, n * width : (n + 1) * width], preferred_element_type=F32
            )
            if k == 0:
                pacc[...] = part
            else:
                pacc[...] += part
        for hh in range(HEADS // QN):
            h = n * (HEADS // QN) + hh
            for j in range(TILES):
                q_s[j, h * TILE_TOK : (h + 1) * TILE_TOK, :] = (
                    pacc[j * TILE_TOK : (j + 1) * TILE_TOK, hh * HD : (hh + 1) * HD] * SCALE
                ).astype(BF16)
            dq_out[h * DEC : (h + 1) * DEC, :] = (
                pacc[TOK:ALL, hh * HD : (hh + 1) * HD] * SCALE
            ).astype(BF16)
        for t in range(LENT):

            @pl.when(jnp.logical_not(low) & lent(t))
            def _():
                lend(t, n).start()

        if n == 0:
            arrive(ORDER[1])
            arrive(ORDER[2])
    dkv = jnp.dot(x_s[TOK:ALL, :], wkv_s[...], preferred_element_type=F32)
    dkv_out[0] = dkv[:, 0:HD].astype(BF16)
    dkv_out[1] = dkv[:, HD : 2 * HD].astype(BF16)

    for event in ORDER[3:6]:
        arrive(event)

    def prepare(slot):
        side = pl.ds(pl.multiple_of((slot % 2) * TOK, TOK), TOK)
        kt_s[slot // 2, :, side] = kv_s[slot, 0].T
        va_s[slot // 2, side, 0:HD] = kv_s[slot, 1]

    def part_of(item):
        j, block, whole = item
        if whole:
            return j, block, slice(0, 2 * TOK), 2 * TOK
        return j, block // 2, pl.ds(pl.multiple_of((block % 2) * TOK, TOK), TOK), TOK

    def score(item, buf):
        j, two, side, width = part_of(item)
        buf[:, 0:width] = jnp.dot(q_s[j], kt_s[two, :, side], preferred_element_type=F32)

    def absorb(item, buf, weights, ahead):
        j, two, side, width = part_of(item)
        if ahead is not None:
            first = jnp.where(j < TILES, j, j - count) * TILE_TOK + ahead
            lead = lax.broadcasted_iota(jnp.int32, (CHUNK, HD), 1) - lax.broadcasted_iota(
                jnp.int32, (CHUNK, HD), 0
            )
        for c in range(TILE // CHUNK):
            rows = slice(c * CHUNK, (c + 1) * CHUNK)
            cuts = [buf[rows, k * HD : (k + 1) * HD] for k in range(width // HD)]
            if ahead is not None:
                cuts = [
                    jnp.where(lead <= first + (c * CHUNK % TILE_TOK - k * HD), cut, LOW)
                    for k, cut in enumerate(cuts)
                ]
            old = m_s[j, rows, :]
            best = functools.reduce(jnp.maximum, cuts)
            top = jnp.maximum(
                old, jnp.broadcast_to(jnp.max(best, axis=1, keepdims=True), (CHUNK, HD))
            )
            for k, cut in enumerate(cuts):
                weights[rows, k * HD : (k + 1) * HD] = jnp.exp2(cut - top).astype(BF16)
            shrink = jnp.exp2(old - top)
            m_s[j, rows, :] = top
            acc[j, rows, 0:HD] = acc[j, rows, 0:HD] * shrink
            acc[j, rows, HD:] = acc[j, rows, HD:] * shrink
        acc[j] += jnp.dot(weights[:, 0:width], va_s[two, side, :], preferred_element_type=F32)

    def run(n, item, ahead=None):
        @pl.when(n > 0)
        def _():
            score(item(0), sa_s)

        def two(t, carry):
            score(item(2 * t + 1), sb_s)
            absorb(item(2 * t), sa_s, pa_s, ahead)
            score(item(jnp.minimum(2 * t + 2, n - 1)), sa_s)
            absorb(item(2 * t + 1), sb_s, pb_s, ahead)
            return carry

        lax.fori_loop(0, n // 2, two, 0)

        @pl.when(n % 2 == 1)
        def _():
            absorb(item(n - 1), sa_s, pa_s, ahead)

    own = jnp.where(low, TILES, TILES - count)
    taken = jnp.where(low, count, 0)

    prepare(g)
    run(own, lambda t: (t, g, False), 0)

    def finish(j, h):
        rows = slice(h * TILE_TOK, (h + 1) * TILE_TOK)
        return (acc[j, rows, 0:HD] / acc[j, rows, HD:]).astype(BF16)

    def pair_at(i):
        half = i // 4
        step = jnp.where(core == 0, i % 4, i // 2)
        across = jnp.where(core == 0, 1 - half, 1 - i % 2)
        near = jnp.where(step == 0, 0, jnp.where(step == 1, 3, step - 1))
        return ((x + near) % 4) * 2 + (y + across) % 2

    def prepare_pair(i):
        for side in range(2):
            slot = 2 * pair_at(i) + side

            @pl.when(slot <= last)
            def _():
                prepare(slot)

    def turn(i, carry):
        for at, events in enumerate(TURNS):

            @pl.when(i == at)
            def _():
                for e in events:
                    arrive(ORDER[e])

        @pl.when(i < PAIRS // 2)
        def _():
            prepare_pair(i)

        @pl.when(i == PAIRS // 2)
        def _():
            def rest(k, carry):
                prepare_pair(k)
                return carry

            lax.fori_loop(PAIRS // 2, PAIRS, rest, 0)
            for t in range(LENT):
                for n in range(QN):

                    @pl.when(low & lent(t))
                    def _():
                        lend(t, n).wait_recv()

            def single(k, carry):
                start = jnp.where(k == 2, 0, TILES)
                odd = jnp.where(k == 2, g, last) % 2
                n = jnp.where(k == 0, taken, odd * jnp.where(k == 1, taken, own))
                block = jnp.where(k == 0, last, jnp.where(k == 1, last, g) - 1)
                run(n, lambda t: (start + t, block, False), jnp.where(k == 0, 0, TOK))
                return carry

            lax.fori_loop(0, 3, single, 0)

            def away(j, carry):
                run(last // 2, lambda t: (j, t, True))
                for h in range(HEADS):
                    of_s[j - TILES, :, h * HD : (h + 1) * HD] = finish(j, h)
                for f in range(LENT):

                    @pl.when(j == TILES + f)
                    def _():
                        give_back(f).start()

                return carry

            lax.fori_loop(TILES, TILES + taken, away, 0)

        two = pair_at(i)
        run(jnp.where(two < g // 2, own, 0), lambda t: (t, two, True))
        return carry

    lax.fori_loop(0, PAIRS, turn, 0)

    for j in range(TILES):

        @pl.when(j < own)
        def _():
            for h in range(HEADS):
                pre_out[j * TILE_TOK : (j + 1) * TILE_TOK, h * HD : (h + 1) * HD] = finish(j, h)

    mine = NEW_ROWS // GROUPS
    at = pl.ds(pl.multiple_of(g * mine, mine), mine)
    for src in range(GROUPS):
        for half in range(2):
            new_out[half, src * mine : (src + 1) * mine, :] = kv_s[src, half, at, :]

    for t in range(LENT):

        @pl.when((t < count) & low)
        def _():
            give_back(t).wait_send()

        @pl.when(lent(t) & jnp.logical_not(low))
        def _():
            for n in range(QN):
                lend(t, n).wait_send()

        @pl.when((t < count) & jnp.logical_not(low))
        def _():
            give_back(t).wait_recv()

    for k in range(1, 8):
        dec_copy(k).wait_send()
    for number in range(len(SENDS)):
        kv_copy(number).wait_send()


def decode(
    table, lens, dest, pre_in, cache, dq, dkv, new,
    pre_out, dec_out,
    pre_s, pool_s, mix_s, page_s, dq_s, out_s, in_sem, out_sem, pool_sem,
):
    half = TOK // 2

    def take(k):
        rows = pl.ds(k * half, half)
        return pltpu.make_async_copy(pre_in.at[rows, :], pre_s.at[rows, :], in_sem.at[k])

    def hand_on(k):
        rows = pl.ds(k * half, half)
        return pltpu.make_async_copy(pre_s.at[rows, :], pre_out.at[rows, :], out_sem.at[k])

    pool = pltpu.make_async_copy(cache, page_s, pool_sem)
    pool.start()
    for k in range(2):
        take(k).start()

    mix_s[pl.ds(0, NEW_ROWS, stride=2), :] = new[0].astype(F32)
    mix_s[pl.ds(1, NEW_ROWS, stride=2), :] = new[1].astype(F32)
    pool.wait()
    for m in range(TOK // PAGE):
        at = pl.ds(pl.multiple_of(dest[0, m] * 2 * PAGE, 2 * PAGE), 2 * PAGE)
        page_s[at, :] = mix_s[m * 2 * PAGE : (m + 1) * 2 * PAGE, :].astype(BF16)
    dq_s[...] = dq[...].astype(F32)
    for r in range(ROWS):
        for j in range(MAXP):
            at = pl.ds(pl.multiple_of(table[r, j] * 2 * PAGE, 2 * PAGE), 2 * PAGE)
            pool_s[r, j * 2 * PAGE : (j + 1) * 2 * PAGE, :] = page_s[at, :]

    for k in range(2):
        take(k).wait()
        hand_on(k).start()

    wide = 2 * MAXP * PAGE
    queries = HEADS * STEPS
    column = lax.broadcasted_iota(jnp.int32, (queries, wide), 1)
    query = lax.broadcasted_iota(jnp.int32, (queries, DEC), 0)
    token = lax.broadcasted_iota(jnp.int32, (queries, DEC), 1)
    so_far = (token >> 3) <= (query & (STEPS - 1))
    for r in range(ROWS):
        q = dq_s[pl.ds(r, queries, stride=ROWS), :].astype(BF16)

        def scores(keys):
            return lax.dot_general(q, keys, (((1,), (1,)), ((), ())), preferred_element_type=F32)

        live = ((column & 1) == 0) & (column < 2 * lens[r])
        s_old = jnp.where(live, scores(pool_s[r]), LOW)
        s_new = jnp.where(so_far & ((token & (ROWS - 1)) == r), scores(dkv[0]), LOW)
        top = jnp.maximum(
            jnp.max(s_old, axis=1, keepdims=True), jnp.max(s_new, axis=1, keepdims=True)
        )
        p_old = jnp.exp2(s_old - top)
        p_new = jnp.exp2(s_new - top)
        total = jnp.sum(p_old, axis=1, keepdims=True) + jnp.sum(p_new, axis=1, keepdims=True)
        p_old = jnp.concatenate(
            [pltpu.roll(p_old[:, k * HD : (k + 1) * HD], 1, 1) for k in range(wide // HD)], axis=1
        ).astype(BF16)
        mixed = jnp.dot(p_old, pool_s[r], preferred_element_type=F32) + jnp.dot(
            p_new.astype(BF16), dkv[1], preferred_element_type=F32
        )
        out_s[pl.ds(r, queries, stride=ROWS), :] = mixed / total
    for h in range(HEADS):
        dec_out[:, h * HD : (h + 1) * HD] = out_s[h * DEC : (h + 1) * DEC, :].astype(BF16)
    for k in range(2):
        hand_on(k).wait()


def per_device(pre_x, w_query, w_key, w_value, dec_x, cache, lengths, page_table, dest_slots):
    hbm = pl.BlockSpec(memory_space=pltpu.MemorySpace.HBM)
    vmem = pl.BlockSpec(memory_space=pltpu.MemorySpace.VMEM)
    smem = pl.BlockSpec(memory_space=pltpu.MemorySpace.SMEM)
    pre, dq, dkv, new = pl.pallas_call(
        prefill,
        out_shape=(
            jax.ShapeDtypeStruct((TOK, HEADS * HD), BF16),
            jax.ShapeDtypeStruct((HEADS * DEC, HD), BF16),
            jax.ShapeDtypeStruct((2, DEC, HD), BF16),
            jax.ShapeDtypeStruct((2, NEW_ROWS, HD), BF16),
        ),
        in_specs=[hbm] * 5,
        out_specs=(vmem,) * 4,
        scratch_shapes=[
            pltpu.VMEM((ALL, D), BF16),
            pltpu.VMEM((D, 2 * HD), BF16),
            pltpu.VMEM((D, HEADS * HD), BF16),
            pltpu.VMEM((GROUPS, 2, TOK, HD), BF16),
            pltpu.VMEM((PAIRS, HD, 2 * TOK), BF16),
            pltpu.VMEM((PAIRS, 2 * TOK, 2 * HD), BF16),
            pltpu.VMEM((LENT, TILE_TOK, HEADS * HD), BF16),
            pltpu.VMEM((TILES + LENT, TILE, HD), BF16),
            pltpu.VMEM((ALL, HEADS * HD // QN), F32),
            pltpu.VMEM((TILES + LENT, TILE, 2 * HD), F32),
            pltpu.VMEM((TILES + LENT, TILE, HD), F32),
            pltpu.VMEM((TILE, 2 * TOK), F32),
            pltpu.VMEM((TILE, 2 * TOK), F32),
            pltpu.VMEM((TILE, 2 * TOK), BF16),
            pltpu.VMEM((TILE, 2 * TOK), BF16),
            pltpu.SemaphoreType.DMA((XC,)),
            pltpu.SemaphoreType.DMA((XC,)),
            pltpu.SemaphoreType.DMA((XC,)),
            pltpu.SemaphoreType.DMA((QN * QK,)),
            pltpu.SemaphoreType.DMA,
            pltpu.SemaphoreType.DMA((7,)),
            pltpu.SemaphoreType.DMA((7,)),
            pltpu.SemaphoreType.DMA((len(SENDS),)),
            pltpu.SemaphoreType.DMA((32,)),
            pltpu.SemaphoreType.DMA((LENT * QN,)),
            pltpu.SemaphoreType.DMA((LENT * QN,)),
            pltpu.SemaphoreType.DMA((LENT,)),
            pltpu.SemaphoreType.DMA((LENT,)),
        ],
        compiler_params=pltpu.CompilerParams(
            collective_id=0, has_side_effects=True, vmem_limit_bytes=63 * 1024 * 1024
        ),
    )(pre_x, w_query, w_key, w_value, dec_x.reshape(DEC, D // 8))
    pre_out, dec_out = pl.pallas_call(
        decode,
        out_shape=(
            jax.ShapeDtypeStruct((TOK, HEADS * HD), BF16),
            jax.ShapeDtypeStruct((DEC, HEADS * HD), BF16),
        ),
        in_specs=[smem] * 3 + [hbm] * 2 + [vmem] * 3,
        out_specs=(hbm, vmem),
        scratch_shapes=[
            pltpu.VMEM((TOK, HEADS * HD), BF16),
            pltpu.VMEM((ROWS, 2 * MAXP * PAGE, HD), BF16),
            pltpu.VMEM((2 * NEW_ROWS, HD), F32),
            pltpu.VMEM((CACHE_ROWS, HD), BF16),
            pltpu.VMEM((HEADS * DEC, HD), F32),
            pltpu.VMEM((HEADS * DEC, HD), F32),
            pltpu.SemaphoreType.DMA((2,)),
            pltpu.SemaphoreType.DMA((2,)),
            pltpu.SemaphoreType.DMA,
        ],
        compiler_params=pltpu.CompilerParams(vmem_limit_bytes=63 * 1024 * 1024),
    )(page_table, lengths, dest_slots, pre, cache.reshape(CACHE_ROWS, HD), dq, dkv, new)
    return pre_out, dec_out.reshape(STEPS, ROWS, HEADS * HD)


def solution(mesh):
    in_specs = (
        P(("seq", "pool"), None),
        P(None, "tensor"),
        P(None, "tensor"),
        P(None, "tensor"),
        P(None, ("seq", "pool"), "tensor"),
        P(("seq", "pool"), None, None, "tensor"),
        P(("seq", "pool")),
        P(("seq", "pool"), None),
        P(("seq", "pool"), None),
    )
    out_specs = (P(("seq", "pool"), "tensor"), P(None, ("seq", "pool"), "tensor"))
    return jax.shard_map(
        per_device, mesh=mesh, in_specs=in_specs, out_specs=out_specs, check_vma=False
    )
```

```python
import functools

import jax
import jax.numpy as jnp
from jax import lax
from jax.experimental import pallas as pl
from jax.experimental.pallas import tpu as pltpu
from jax.sharding import PartitionSpec as P

MESH = pl.DeviceIdType.MESH
BF16 = jnp.bfloat16
F32 = jnp.float32

D = 8192
HD = 128
HEADS = 8
TOK = 512
GROUPS = 16
PAGE = 16
MAXP = 16
PAGES = 128
ROWS = 8
STEPS = 4
DEC = ROWS * STEPS
ALL = TOK + DEC
TILE_TOK = 64
TILES = TOK // TILE_TOK
TILE = TILE_TOK * HEADS
CACHE_ROWS = PAGES * PAGE * 2
NEW_ROWS = 512
SCALE = HD ** (-0.5) * 1.4426950408889634
LOW = -1e30
XC = 8
QK = 2
QN = 4
LENT = 4
TAKES = (4, 3, 3, 2, 2, 1, 1, 0)
PAIRS = GROUPS // 2
CHUNK = 16
HALF = TILE // 2
SHIFT = 4.0
POLLS = {2: (1, 2), 4: (5,), 5: (3, 4), 7: (6, 7)}

ORDER = (
    (0, 0), (3, 0), (1, 0), (0, 3), (0, 1), (2, 0), (3, 3), (3, 1),
    (1, 3), (1, 1), (2, 3), (2, 1), (0, 2), (3, 2), (1, 2), (2, 2),
)


def sends_after(event):
    near, far = event
    sends = []
    if near == 0 and far == 0:
        sends += [(0, "A+"), (0, "A-"), (1, "A+"), (1, "A-")]
    elif far == 0 and near == 3:
        sends += [(0, "A+")]
    elif far == 0 and near == 1:
        sends += [(1, "A-")]
    if far == 0:
        sends += [(0, "B+"), (0, "B-"), (1, "B+"), (1, "B-")]
    elif far == 3:
        sends += [(0, "B+")]
    elif far == 1:
        sends += [(1, "B-")]
    return sends


def seen_from(event, direction):
    near, far = event
    step = 1 if direction[1] == "+" else -1
    if direction[0] == "A":
        return ((near - step) % 4, far)
    return (near, (far - step) % 4)


SENDS = [(event, half, way) for event in ORDER for half, way in sends_after(event)]


def prefill(
    px, wq, wk, wv, dx,
    pre_out, dq_out, dkv_out, new_out,
    x_s, wkv_s, wq_s, kv_s, kt_s, va_s, of_s, q_s, pacc, acc, m_s, sa_s, sb_s, pa_s, pb_s, ha_s, hb_s,
    xsem, wksem, wvsem, qsem, dsem_own, dsend, drecv, ssem, rsem, qsend, qrecv, osend, orecv,
):
    seq, tensor, pool = lax.axis_index("seq"), lax.axis_index("tensor"), lax.axis_index("pool")
    x, y, core = seq // 2, pool * 2 + seq % 2, tensor % 2
    g = seq * 2 + pool
    low = g < 8
    other = 15 - g
    last = jnp.where(low, other, g)
    pair = jnp.where(low, g, other)
    count = sum(jnp.where(pair == k, TAKES[k], 0) for k in range(8))
    partner = {"seq": 7 - seq, "pool": 1 - pool}

    def place(near, far):
        ax, ay = (x + near) % 4, (y + far) % 4
        bx, by = (x + far) % 4, (y + near) % 4
        return jnp.where(core == 0, ax, bx), jnp.where(core == 0, ay, by)

    def slot_of(near, far):
        px_, py_ = place(near, far)
        return px_ * 4 + (py_ % 2) * 2 + py_ // 2

    def device(near, far):
        px_, py_ = place(near, far)
        return {"seq": px_ * 2 + py_ % 2, "pool": py_ // 2}

    ways = {"A+": device(1, 0), "A-": device(3, 0), "B+": device(0, 1), "B-": device(0, 3)}

    def x_copy(c):
        cols = pl.ds(pl.multiple_of(c * (D // XC), D // XC), D // XC)
        return pltpu.make_async_copy(px.at[:, cols], x_s.at[pl.ds(0, TOK), cols], xsem.at[c])

    def w_copy(c, ref, at, sem):
        rows = pl.ds(pl.multiple_of(c * (D // XC), D // XC), D // XC)
        return pltpu.make_async_copy(ref.at[rows, :], wkv_s.at[rows, pl.ds(at, HD)], sem.at[c])

    def q_copy(n, k):
        rows = pl.ds(k * (D // QK), D // QK)
        cols = pl.ds(n * (HEADS * HD // QN), HEADS * HD // QN)
        return pltpu.make_async_copy(wq.at[rows, cols], wq_s.at[rows, cols], qsem.at[n * QK + k])

    my_cols = pl.ds(pl.multiple_of(tensor * (D // 8), D // 8), D // 8)
    dec_own = pltpu.make_async_copy(dx, x_s.at[pl.ds(TOK, DEC), my_cols], dsem_own)

    for c in range(XC):
        x_copy(c).start()
        w_copy(c, wk, 0, wksem).start()
        w_copy(c, wv, HD, wvsem).start()
    dec_own.start()
    for n in range(QN):
        for k in range(QK):
            q_copy(n, k).start()

    barrier = pltpu.get_barrier_semaphore()
    for way in ways.values():
        pl.semaphore_signal(barrier, inc=1, device_id=way, device_id_type=MESH)
    pl.semaphore_signal(barrier, inc=1, device_id=partner, device_id_type=MESH)
    for k in range(1, 8):
        pl.semaphore_signal(
            barrier, inc=1, device_id={"tensor": (tensor + k) % 8}, device_id_type=MESH
        )
    pl.semaphore_wait(barrier, 12)

    def dec_copy(k):
        return pltpu.make_async_remote_copy(
            src_ref=dx,
            dst_ref=x_s.at[pl.ds(TOK, DEC), my_cols],
            send_sem=dsend.at[k - 1],
            recv_sem=drecv.at[k - 1],
            device_id={"tensor": (tensor + k) % 8},
            device_id_type=MESH,
        )

    def dec_arrival(k):
        cols = pl.ds(pl.multiple_of(((tensor + 8 - k) % 8) * (D // 8), D // 8), D // 8)
        return pltpu.make_async_remote_copy(
            src_ref=dx,
            dst_ref=x_s.at[pl.ds(TOK, DEC), cols],
            send_sem=dsend.at[k - 1],
            recv_sem=drecv.at[k - 1],
            device_id={"tensor": (tensor + k) % 8},
            device_id_type=MESH,
        )

    for k in range(1, 8):
        dec_copy(k).start()

    def kv_copy(number):
        event, half, way = SENDS[number]
        slot = slot_of(*event)
        near, far = seen_from(event, way)
        return pltpu.make_async_remote_copy(
            src_ref=kv_s.at[slot, half],
            dst_ref=kv_s.at[slot, half],
            send_sem=ssem.at[number],
            recv_sem=rsem.at[(near * 4 + far) * 2 + half],
            device_id=ways[way],
            device_id_type=MESH,
        )

    def pass_on(event):
        for number, (of, _, _) in enumerate(SENDS):
            if of == event:
                kv_copy(number).start()

    def arrive(event):
        near, far = event
        slot = slot_of(near, far)
        for half in range(2):
            pltpu.make_async_remote_copy(
                src_ref=kv_s.at[slot, half],
                dst_ref=kv_s.at[slot, half],
                send_sem=ssem.at[0],
                recv_sem=rsem.at[(near * 4 + far) * 2 + half],
                device_id=ways["A+"],
                device_id_type=MESH,
            ).wait_recv()
        pass_on(event)

    def lend(t, n):
        rows = pl.ds(n * (TILE // QN), TILE // QN)
        return pltpu.make_async_remote_copy(
            src_ref=q_s.at[TILES - LENT + t, rows],
            dst_ref=q_s.at[TILES + t + count - LENT, rows],
            send_sem=qsend.at[t * QN + n],
            recv_sem=qrecv.at[t * QN + n],
            device_id=partner,
            device_id_type=MESH,
        )

    def give_back(f):
        at = pl.ds(pl.multiple_of((TILES - count + f) * TILE_TOK, TILE_TOK), TILE_TOK)
        return pltpu.make_async_remote_copy(
            src_ref=of_s.at[f],
            dst_ref=pre_out.at[at, :],
            send_sem=osend.at[f],
            recv_sem=orecv.at[f],
            device_id=partner,
            device_id_type=MESH,
        )

    def lent(t):
        return count >= LENT - t

    def clear(j, carry):
        acc[j] = jnp.zeros((TILE, 2 * HD), F32)
        m_s[j] = jnp.full((TILE, HD), LOW, F32)
        return carry

    def fill(i, carry):
        va_s[i, :, HD:] = jnp.ones((2 * TOK, HD), BF16)
        return carry

    lax.fori_loop(0, TILES + LENT, clear, 0)
    lax.fori_loop(0, PAIRS, fill, 0)

    def kv_step(c, carry):
        x_copy(c).wait()
        w_copy(c, wk, 0, wksem).wait()
        w_copy(c, wv, HD, wvsem).wait()
        at = pl.ds(pl.multiple_of(c * (D // XC), D // XC), D // XC)
        part = jnp.dot(x_s[0:TOK, at], wkv_s[at, :], preferred_element_type=F32)

        @pl.when(c == 0)
        def _():
            pacc[0:TOK, 0:256] = part

        @pl.when(c > 0)
        def _():
            pacc[0:TOK, 0:256] += part

        return carry

    lax.fori_loop(0, XC, kv_step, 0)
    kv_s[g, 0] = pacc[0:TOK, 0:HD].astype(BF16)
    kv_s[g, 1] = pacc[0:TOK, HD : 2 * HD].astype(BF16)
    pass_on(ORDER[0])

    dec_own.wait()
    for k in range(1, 8):
        dec_arrival(k).wait_recv()

    width = HEADS * HD // QN
    for n in range(QN):
        for k in range(QK):
            q_copy(n, k).wait()
            at = slice(k * (D // QK), (k + 1) * (D // QK))
            part = jnp.dot(
                x_s[:, at], wq_s[at, n * width : (n + 1) * width], preferred_element_type=F32
            )
            if k == 0:
                pacc[...] = part
            else:
                pacc[...] += part
            for e in POLLS.get(n * QK + k, ()):
                arrive(ORDER[e])
        for hh in range(HEADS // QN):
            h = n * (HEADS // QN) + hh
            for j in range(TILES):
                q_s[j, h * TILE_TOK : (h + 1) * TILE_TOK, :] = (
                    pacc[j * TILE_TOK : (j + 1) * TILE_TOK, hh * HD : (hh + 1) * HD] * SCALE
                ).astype(BF16)
            dq_out[h * DEC : (h + 1) * DEC, :] = (
                pacc[TOK:ALL, hh * HD : (hh + 1) * HD] * SCALE
            ).astype(BF16)
        for t in range(LENT):

            @pl.when(jnp.logical_not(low) & lent(t))
            def _():
                lend(t, n).start()

    dkv = jnp.dot(x_s[TOK:ALL, :], wkv_s[...], preferred_element_type=F32)
    dkv_out[0] = dkv[:, 0:HD].astype(BF16)
    dkv_out[1] = dkv[:, HD : 2 * HD].astype(BF16)

    def prepare(slot):
        side = pl.ds(pl.multiple_of((slot % 2) * TOK, TOK), TOK)
        kt_s[slot // 2, :, side] = kv_s[slot, 0].T
        va_s[slot // 2, side, 0:HD] = kv_s[slot, 1]

    def part_of(item):
        j, block, whole = item
        if whole:
            return j, block, slice(0, 2 * TOK), 2 * TOK
        return j, block // 2, pl.ds(pl.multiple_of((block % 2) * TOK, TOK), TOK), TOK

    def weave(*streams):
        steps = [
            ((k + 0.5) / len(stream), number, step)
            for number, stream in enumerate(streams)
            for k, step in enumerate(stream)
        ]
        for _, _, step in sorted(steps, key=lambda at: at[:2]):
            step()

    bufs = ((sa_s, pa_s, ha_s), (sb_s, pb_s, hb_s))

    def score(item, half):
        j, two, side, width = part_of(item)
        buf = bufs[half][0]
        rows = slice(half * HALF, (half + 1) * HALF)
        at = 0 if width == 2 * TOK else pl.multiple_of((item[1] % 2) * TOK, TOK)

        def step(n):
            keys = kt_s[two, :, pl.ds(at + n * 2 * HD, 2 * HD)]
            buf[:, n * 2 * HD : (n + 1) * 2 * HD] = jnp.dot(
                q_s[j, rows, :], keys, preferred_element_type=F32
            )

        return [functools.partial(step, n) for n in range(width // (2 * HD))]

    def weigh(item, half, ahead):
        j, two, side, width = part_of(item)
        buf, weights, shrinks = bufs[half]
        if ahead is not None:
            first = jnp.where(j < TILES, j, j - count) * TILE_TOK + ahead
            lead = lax.broadcasted_iota(jnp.int32, (CHUNK, HD), 1) - lax.broadcasted_iota(
                jnp.int32, (CHUNK, HD), 0
            )

        def step(c):
            rows = slice(c * CHUNK, (c + 1) * CHUNK)
            whole = slice(half * HALF + c * CHUNK, half * HALF + (c + 1) * CHUNK)
            cuts = [buf[rows, k * HD : (k + 1) * HD] for k in range(width // HD)]
            if ahead is not None:
                cuts = [
                    jnp.where(lead <= first + (c * CHUNK % TILE_TOK - k * HD), cut, LOW)
                    for k, cut in enumerate(cuts)
                ]
            old = m_s[j, whole, :]
            best = functools.reduce(jnp.maximum, cuts)
            top = jnp.maximum(
                old, jnp.broadcast_to(jnp.max(best, axis=1, keepdims=True) - SHIFT, (CHUNK, HD))
            )
            for k, cut in enumerate(cuts):
                weights[rows, k * HD : (k + 1) * HD] = jnp.exp2((cut - top).astype(BF16))
            shrinks[rows, :] = jnp.exp2(old - top)
            m_s[j, whole, :] = top

        return [functools.partial(step, c) for c in range(HALF // CHUNK)]

    def collect(item, half):
        j, two, side, width = part_of(item)
        _, weights, shrinks = bufs[half]

        o = jnp.dot(weights[:, 0:width], va_s[two, side, :], preferred_element_type=F32)
        for c in range(HALF // CHUNK):
            rows = slice(c * CHUNK, (c + 1) * CHUNK)
            whole = slice(half * HALF + c * CHUNK, half * HALF + (c + 1) * CHUNK)
            shrink = shrinks[rows, :]
            acc[j, whole, 0:HD] = acc[j, whole, 0:HD] * shrink + o[rows, 0:HD]
            acc[j, whole, HD:] = acc[j, whole, HD:] * shrink + o[rows, HD:]

    def run(n, item, ahead=None):
        @pl.when(n > 0)
        def _():
            weave(score(item(0), 0))
            weave(score(item(0), 1), weigh(item(0), 0, ahead))

            def one(t, carry):
                now, later = item(t), item(t + 1)
                collect(now, 0)
                weave(score(later, 0), weigh(now, 1, ahead))
                collect(now, 1)
                weave(score(later, 1), weigh(later, 0, ahead))
                return carry

            lax.fori_loop(0, n - 1, one, 0)
            collect(item(n - 1), 0)
            weave(weigh(item(n - 1), 1, ahead))
            collect(item(n - 1), 1)

    own = jnp.where(low, TILES, TILES - count)
    taken = jnp.where(low, count, 0)

    prepare(g)
    def begin(k, carry):
        run(own // 2 + k * (own % 2), lambda t: (t + k * (own // 2), g, False), 0)
        for at, events in enumerate(((8, 9), (10, 11))):

            @pl.when(k == at)
            def _():
                for e in events:
                    arrive(ORDER[e])

        return carry

    lax.fori_loop(0, 2, begin, 0)

    def finish(j, h):
        rows = slice(h * TILE_TOK, (h + 1) * TILE_TOK)
        return (acc[j, rows, 0:HD] / acc[j, rows, HD:]).astype(BF16)

    def pair_at(i):
        half = i // 4
        step = jnp.where(core == 0, i % 4, i // 2)
        across = jnp.where(core == 0, 1 - half, 1 - i % 2)
        near = jnp.where(step == 0, 0, jnp.where(step == 1, 3, step - 1))
        return ((x + near) % 4) * 2 + (y + across) % 2

    def prepare_pair(i):
        for side in range(2):
            slot = 2 * pair_at(i) + side

            @pl.when(slot <= last)
            def _():
                prepare(slot)

    def turn(i, carry):
        @pl.when(i < PAIRS // 2)
        def _():
            prepare_pair(i)

        @pl.when(i == PAIRS // 2)
        def _():
            for e in (12, 13, 14, 15):
                arrive(ORDER[e])

            def rest(k, carry):
                prepare_pair(k)
                return carry

            lax.fori_loop(PAIRS // 2, PAIRS, rest, 0)
            for t in range(LENT):
                for n in range(QN):

                    @pl.when(low & lent(t))
                    def _():
                        lend(t, n).wait_recv()

            def single(k, carry):
                start = jnp.where(k == 2, 0, TILES)
                odd = jnp.where(k == 2, g, last) % 2
                n = jnp.where(k == 0, taken, odd * jnp.where(k == 1, taken, own))
                block = jnp.where(k == 0, last, jnp.where(k == 1, last, g) - 1)
                run(n, lambda t: (start + t, block, False), jnp.where(k == 0, 0, TOK))
                return carry

            lax.fori_loop(0, 3, single, 0)

            def away(j, carry):
                run(last // 2, lambda t: (j, t, True))
                for h in range(HEADS):
                    of_s[j - TILES, :, h * HD : (h + 1) * HD] = finish(j, h)
                for f in range(LENT):

                    @pl.when(j == TILES + f)
                    def _():
                        give_back(f).start()

                return carry

            lax.fori_loop(TILES, TILES + taken, away, 0)

        two = pair_at(i)
        run(jnp.where(two < g // 2, own, 0), lambda t: (t, two, True))
        return carry

    lax.fori_loop(0, PAIRS, turn, 0)

    for j in range(TILES):

        @pl.when(j < own)
        def _():
            for h in range(HEADS):
                pre_out[j * TILE_TOK : (j + 1) * TILE_TOK, h * HD : (h + 1) * HD] = finish(j, h)

    mine = NEW_ROWS // GROUPS
    at = pl.ds(pl.multiple_of(g * mine, mine), mine)
    for src in range(GROUPS):
        for half in range(2):
            new_out[half, src * mine : (src + 1) * mine, :] = kv_s[src, half, at, :]

    for t in range(LENT):

        @pl.when((t < count) & low)
        def _():
            give_back(t).wait_send()

        @pl.when(lent(t) & jnp.logical_not(low))
        def _():
            for n in range(QN):
                lend(t, n).wait_send()

        @pl.when((t < count) & jnp.logical_not(low))
        def _():
            give_back(t).wait_recv()

    for k in range(1, 8):
        dec_copy(k).wait_send()
    for number in range(len(SENDS)):
        kv_copy(number).wait_send()


def decode(
    table, lens, dest, pre_in, cache, dq, dkv, new,
    pre_out, dec_out,
    pre_s, pool_s, mix_s, page_s, dq_s, out_s, in_sem, out_sem, pool_sem,
):
    half = TOK // 2

    def take(k):
        rows = pl.ds(k * half, half)
        return pltpu.make_async_copy(pre_in.at[rows, :], pre_s.at[rows, :], in_sem.at[k])

    def hand_on(k):
        rows = pl.ds(k * half, half)
        return pltpu.make_async_copy(pre_s.at[rows, :], pre_out.at[rows, :], out_sem.at[k])

    pool = pltpu.make_async_copy(cache, page_s, pool_sem)
    pool.start()
    for k in range(2):
        take(k).start()

    mix_s[pl.ds(0, NEW_ROWS, stride=2), :] = new[0].astype(F32)
    mix_s[pl.ds(1, NEW_ROWS, stride=2), :] = new[1].astype(F32)
    pool.wait()
    for m in range(TOK // PAGE):
        at = pl.ds(pl.multiple_of(dest[0, m] * 2 * PAGE, 2 * PAGE), 2 * PAGE)
        page_s[at, :] = mix_s[m * 2 * PAGE : (m + 1) * 2 * PAGE, :].astype(BF16)
    dq_s[...] = dq[...].astype(F32)
    for r in range(ROWS):
        for j in range(MAXP):
            at = pl.ds(pl.multiple_of(table[r, j] * 2 * PAGE, 2 * PAGE), 2 * PAGE)
            pool_s[r, j * 2 * PAGE : (j + 1) * 2 * PAGE, :] = page_s[at, :]

    for k in range(2):
        take(k).wait()
        hand_on(k).start()

    wide = 2 * MAXP * PAGE
    queries = HEADS * STEPS
    column = lax.broadcasted_iota(jnp.int32, (queries, wide), 1)
    query = lax.broadcasted_iota(jnp.int32, (queries, DEC), 0)
    token = lax.broadcasted_iota(jnp.int32, (queries, DEC), 1)
    so_far = (token >> 3) <= (query & (STEPS - 1))
    for r in range(ROWS):
        q = dq_s[pl.ds(r, queries, stride=ROWS), :].astype(BF16)

        def scores(keys):
            return lax.dot_general(q, keys, (((1,), (1,)), ((), ())), preferred_element_type=F32)

        live = ((column & 1) == 0) & (column < 2 * lens[r])
        s_old = jnp.where(live, scores(pool_s[r]), LOW)
        s_new = jnp.where(so_far & ((token & (ROWS - 1)) == r), scores(dkv[0]), LOW)
        top = jnp.maximum(
            jnp.max(s_old, axis=1, keepdims=True), jnp.max(s_new, axis=1, keepdims=True)
        )
        p_old = jnp.exp2(s_old - top)
        p_new = jnp.exp2(s_new - top)
        total = jnp.sum(p_old, axis=1, keepdims=True) + jnp.sum(p_new, axis=1, keepdims=True)
        p_old = jnp.concatenate(
            [pltpu.roll(p_old[:, k * HD : (k + 1) * HD], 1, 1) for k in range(wide // HD)], axis=1
        ).astype(BF16)
        mixed = jnp.dot(p_old, pool_s[r], preferred_element_type=F32) + jnp.dot(
            p_new.astype(BF16), dkv[1], preferred_element_type=F32
        )
        out_s[pl.ds(r, queries, stride=ROWS), :] = mixed / total
    for h in range(HEADS):
        dec_out[:, h * HD : (h + 1) * HD] = out_s[h * DEC : (h + 1) * DEC, :].astype(BF16)
    for k in range(2):
        hand_on(k).wait()


def per_device(pre_x, w_query, w_key, w_value, dec_x, cache, lengths, page_table, dest_slots):
    hbm = pl.BlockSpec(memory_space=pltpu.MemorySpace.HBM)
    vmem = pl.BlockSpec(memory_space=pltpu.MemorySpace.VMEM)
    smem = pl.BlockSpec(memory_space=pltpu.MemorySpace.SMEM)
    pre, dq, dkv, new = pl.pallas_call(
        prefill,
        out_shape=(
            jax.ShapeDtypeStruct((TOK, HEADS * HD), BF16),
            jax.ShapeDtypeStruct((HEADS * DEC, HD), BF16),
            jax.ShapeDtypeStruct((2, DEC, HD), BF16),
            jax.ShapeDtypeStruct((2, NEW_ROWS, HD), BF16),
        ),
        in_specs=[hbm] * 5,
        out_specs=(vmem,) * 4,
        scratch_shapes=[
            pltpu.VMEM((ALL, D), BF16),
            pltpu.VMEM((D, 2 * HD), BF16),
            pltpu.VMEM((D, HEADS * HD), BF16),
            pltpu.VMEM((GROUPS, 2, TOK, HD), BF16),
            pltpu.VMEM((PAIRS, HD, 2 * TOK), BF16),
            pltpu.VMEM((PAIRS, 2 * TOK, 2 * HD), BF16),
            pltpu.VMEM((LENT, TILE_TOK, HEADS * HD), BF16),
            pltpu.VMEM((TILES + LENT, TILE, HD), BF16),
            pltpu.VMEM((ALL, HEADS * HD // QN), F32),
            pltpu.VMEM((TILES + LENT, TILE, 2 * HD), F32),
            pltpu.VMEM((TILES + LENT, TILE, HD), F32),
            pltpu.VMEM((HALF, 2 * TOK), F32),
            pltpu.VMEM((HALF, 2 * TOK), F32),
            pltpu.VMEM((HALF, 2 * TOK), BF16),
            pltpu.VMEM((HALF, 2 * TOK), BF16),
            pltpu.VMEM((HALF, HD), F32),
            pltpu.VMEM((HALF, HD), F32),
            pltpu.SemaphoreType.DMA((XC,)),
            pltpu.SemaphoreType.DMA((XC,)),
            pltpu.SemaphoreType.DMA((XC,)),
            pltpu.SemaphoreType.DMA((QN * QK,)),
            pltpu.SemaphoreType.DMA,
            pltpu.SemaphoreType.DMA((7,)),
            pltpu.SemaphoreType.DMA((7,)),
            pltpu.SemaphoreType.DMA((len(SENDS),)),
            pltpu.SemaphoreType.DMA((32,)),
            pltpu.SemaphoreType.DMA((LENT * QN,)),
            pltpu.SemaphoreType.DMA((LENT * QN,)),
            pltpu.SemaphoreType.DMA((LENT,)),
            pltpu.SemaphoreType.DMA((LENT,)),
        ],
        compiler_params=pltpu.CompilerParams(
            collective_id=0, has_side_effects=True, vmem_limit_bytes=63 * 1024 * 1024
        ),
    )(pre_x, w_query, w_key, w_value, dec_x.reshape(DEC, D // 8))
    pre_out, dec_out = pl.pallas_call(
        decode,
        out_shape=(
            jax.ShapeDtypeStruct((TOK, HEADS * HD), BF16),
            jax.ShapeDtypeStruct((DEC, HEADS * HD), BF16),
        ),
        in_specs=[smem] * 3 + [hbm] * 2 + [vmem] * 3,
        out_specs=(hbm, vmem),
        scratch_shapes=[
            pltpu.VMEM((TOK, HEADS * HD), BF16),
            pltpu.VMEM((ROWS, 2 * MAXP * PAGE, HD), BF16),
            pltpu.VMEM((2 * NEW_ROWS, HD), F32),
            pltpu.VMEM((CACHE_ROWS, HD), BF16),
            pltpu.VMEM((HEADS * DEC, HD), F32),
            pltpu.VMEM((HEADS * DEC, HD), F32),
            pltpu.SemaphoreType.DMA((2,)),
            pltpu.SemaphoreType.DMA((2,)),
            pltpu.SemaphoreType.DMA,
        ],
        compiler_params=pltpu.CompilerParams(vmem_limit_bytes=63 * 1024 * 1024),
    )(page_table, lengths, dest_slots, pre, cache.reshape(CACHE_ROWS, HD), dq, dkv, new)
    return pre_out, dec_out.reshape(STEPS, ROWS, HEADS * HD)


def solution(mesh):
    in_specs = (
        P(("seq", "pool"), None),
        P(None, "tensor"),
        P(None, "tensor"),
        P(None, "tensor"),
        P(None, ("seq", "pool"), "tensor"),
        P(("seq", "pool"), None, None, "tensor"),
        P(("seq", "pool")),
        P(("seq", "pool"), None),
        P(("seq", "pool"), None),
    )
    out_specs = (P(("seq", "pool"), "tensor"), P(None, ("seq", "pool"), "tensor"))
    return jax.shard_map(
        per_device, mesh=mesh, in_specs=in_specs, out_specs=out_specs, check_vma=False
    )
```

```python
import functools

import jax
import jax.numpy as jnp
from jax import lax
from jax.experimental import pallas as pl
from jax.experimental.pallas import tpu as pltpu
from jax.sharding import PartitionSpec as P

MESH = pl.DeviceIdType.MESH
BF16 = jnp.bfloat16
F32 = jnp.float32

D = 8192
HD = 128
HEADS = 8
TOK = 512
GROUPS = 16
PAGE = 16
MAXP = 16
PAGES = 128
ROWS = 8
STEPS = 4
DEC = ROWS * STEPS
ALL = TOK + DEC
TILE_TOK = 64
TILES = TOK // TILE_TOK
TILE = TILE_TOK * HEADS
CACHE_ROWS = PAGES * PAGE * 2
NEW_ROWS = 512
SCALE = HD ** (-0.5) * 1.4426950408889634
LOW = -1e30
XC = 8
QK = 4
QN = 2
LENT = 4
TAKES = (3, 3, 3, 3, 2, 2, 1, 0)
PAIRS = GROUPS // 2
CHUNK = 16
POLLS = {5: (1, 2), 7: (3, 4, 5)}
TURNS = {1: (6, 7, 8, 9), 2: (10, 11), 4: (12, 13, 14, 15)}
JOIN, PART = 2, 6

ORDER = (
    (0, 0), (3, 0), (1, 0), (0, 3), (0, 1), (2, 0), (3, 3), (3, 1),
    (1, 3), (1, 1), (2, 3), (2, 1), (0, 2), (3, 2), (1, 2), (2, 2),
)


def sends_after(event):
    near, far = event
    sends = []
    if near == 0 and far == 0:
        sends += [(0, "A+"), (0, "A-"), (1, "A+"), (1, "A-")]
    elif far == 0 and near == 3:
        sends += [(0, "A+")]
    elif far == 0 and near == 1:
        sends += [(1, "A-")]
    if far == 0:
        sends += [(0, "B+"), (0, "B-"), (1, "B+"), (1, "B-")]
    elif far == 3:
        sends += [(0, "B+")]
    elif far == 1:
        sends += [(1, "B-")]
    return sends


def seen_from(event, direction):
    near, far = event
    step = 1 if direction[1] == "+" else -1
    if direction[0] == "A":
        return ((near - step) % 4, far)
    return (near, (far - step) % 4)


SENDS = [(event, half, way) for event in ORDER for half, way in sends_after(event)]


def prefill(
    px, wq, wk, wv, dx,
    pre_out, dq_out, dkv_out, new_out,
    x_s, wkv_s, wq_s, kv_s, kt_s, va_s, of_s, q_s, pacc, acc, m_s, sa_s, sb_s, pa_s, pb_s,
    xsem, wksem, wvsem, qsem, dsem_own, dsend, drecv, ssem, rsem, qsend, qrecv, osend, orecv,
):
    seq, tensor, pool = lax.axis_index("seq"), lax.axis_index("tensor"), lax.axis_index("pool")
    x, y, core = seq // 2, pool * 2 + seq % 2, tensor % 2
    g = seq * 2 + pool
    low = g < 8
    other = 15 - g
    last = jnp.where(low, other, g)
    pair = jnp.where(low, g, other)
    count = sum(jnp.where(pair == k, TAKES[k], 0) for k in range(8))
    partner = {"seq": 7 - seq, "pool": 1 - pool}

    def place(near, far):
        ax, ay = (x + near) % 4, (y + far) % 4
        bx, by = (x + far) % 4, (y + near) % 4
        return jnp.where(core == 0, ax, bx), jnp.where(core == 0, ay, by)

    def slot_of(near, far):
        px_, py_ = place(near, far)
        return px_ * 4 + (py_ % 2) * 2 + py_ // 2

    def device(near, far):
        px_, py_ = place(near, far)
        return {"seq": px_ * 2 + py_ % 2, "pool": py_ // 2}

    ways = {"A+": device(1, 0), "A-": device(3, 0), "B+": device(0, 1), "B-": device(0, 3)}

    def x_copy(c):
        cols = pl.ds(pl.multiple_of(c * (D // XC), D // XC), D // XC)
        return pltpu.make_async_copy(px.at[:, cols], x_s.at[pl.ds(0, TOK), cols], xsem.at[c])

    def w_copy(c, ref, at, sem):
        rows = pl.ds(pl.multiple_of(c * (D // XC), D // XC), D // XC)
        return pltpu.make_async_copy(ref.at[rows, :], wkv_s.at[rows, pl.ds(at, HD)], sem.at[c])

    def q_copy(n, k):
        rows = pl.ds(k * (D // QK), D // QK)
        cols = pl.ds(n * (HEADS * HD // QN), HEADS * HD // QN)
        return pltpu.make_async_copy(wq.at[rows, cols], wq_s.at[rows, cols], qsem.at[n * QK + k])

    my_cols = pl.ds(pl.multiple_of(tensor * (D // 8), D // 8), D // 8)
    dec_own = pltpu.make_async_copy(dx, x_s.at[pl.ds(TOK, DEC), my_cols], dsem_own)

    for c in range(XC):
        x_copy(c).start()
        w_copy(c, wk, 0, wksem).start()
        w_copy(c, wv, HD, wvsem).start()
    dec_own.start()

    barrier = pltpu.get_barrier_semaphore()
    for way in ways.values():
        pl.semaphore_signal(barrier, inc=1, device_id=way, device_id_type=MESH)
    pl.semaphore_signal(barrier, inc=1, device_id=partner, device_id_type=MESH)
    for k in range(1, 8):
        pl.semaphore_signal(
            barrier, inc=1, device_id={"tensor": (tensor + k) % 8}, device_id_type=MESH
        )
    pl.semaphore_wait(barrier, 12)

    def dec_copy(k):
        return pltpu.make_async_remote_copy(
            src_ref=dx,
            dst_ref=x_s.at[pl.ds(TOK, DEC), my_cols],
            send_sem=dsend.at[k - 1],
            recv_sem=drecv.at[k - 1],
            device_id={"tensor": (tensor + k) % 8},
            device_id_type=MESH,
        )

    def dec_arrival(k):
        cols = pl.ds(pl.multiple_of(((tensor + 8 - k) % 8) * (D // 8), D // 8), D // 8)
        return pltpu.make_async_remote_copy(
            src_ref=dx,
            dst_ref=x_s.at[pl.ds(TOK, DEC), cols],
            send_sem=dsend.at[k - 1],
            recv_sem=drecv.at[k - 1],
            device_id={"tensor": (tensor + k) % 8},
            device_id_type=MESH,
        )

    for k in range(1, 8):
        dec_copy(k).start()

    def kv_copy(number):
        event, half, way = SENDS[number]
        slot = slot_of(*event)
        near, far = seen_from(event, way)
        return pltpu.make_async_remote_copy(
            src_ref=kv_s.at[slot, half],
            dst_ref=kv_s.at[slot, half],
            send_sem=ssem.at[number],
            recv_sem=rsem.at[(near * 4 + far) * 2 + half],
            device_id=ways[way],
            device_id_type=MESH,
        )

    def pass_on(event):
        for number, (of, _, _) in enumerate(SENDS):
            if of == event:
                kv_copy(number).start()

    def arrive(event):
        near, far = event
        slot = slot_of(near, far)
        for half in range(2):
            pltpu.make_async_remote_copy(
                src_ref=kv_s.at[slot, half],
                dst_ref=kv_s.at[slot, half],
                send_sem=ssem.at[0],
                recv_sem=rsem.at[(near * 4 + far) * 2 + half],
                device_id=ways["A+"],
                device_id_type=MESH,
            ).wait_recv()
        pass_on(event)

    def lend(t, n):
        rows = pl.ds(n * (TILE // QN), TILE // QN)
        return pltpu.make_async_remote_copy(
            src_ref=q_s.at[TILES - LENT + t, rows],
            dst_ref=q_s.at[TILES + t + count - LENT, rows],
            send_sem=qsend.at[t * QN + n],
            recv_sem=qrecv.at[t * QN + n],
            device_id=partner,
            device_id_type=MESH,
        )

    def give_back(f):
        at = pl.ds(pl.multiple_of((TILES - count + f) * TILE_TOK, TILE_TOK), TILE_TOK)
        return pltpu.make_async_remote_copy(
            src_ref=of_s.at[f],
            dst_ref=pre_out.at[at, :],
            send_sem=osend.at[f],
            recv_sem=orecv.at[f],
            device_id=partner,
            device_id_type=MESH,
        )

    def lent(t):
        return count >= LENT - t

    def clear(j, carry):
        acc[j] = jnp.zeros((TILE, 2 * HD), F32)
        m_s[j] = jnp.full((TILE, HD), LOW, F32)
        return carry

    def fill(i, carry):
        va_s[i, :, HD:] = jnp.ones((2 * TOK, HD), BF16)
        return carry

    lax.fori_loop(0, TILES + LENT, clear, 0)
    lax.fori_loop(0, PAIRS, fill, 0)

    def kv_step(c, carry):
        x_copy(c).wait()
        w_copy(c, wk, 0, wksem).wait()
        w_copy(c, wv, HD, wvsem).wait()
        for k in range(QN * QK):

            @pl.when(c == 4 + k // 2)
            def _():
                q_copy(k // QK, k % QK).start()

        at = pl.ds(pl.multiple_of(c * (D // XC), D // XC), D // XC)
        part = jnp.dot(x_s[0:TOK, at], wkv_s[at, :], preferred_element_type=F32)

        @pl.when(c == 0)
        def _():
            pacc[0:TOK, 0:256] = part

        @pl.when(c > 0)
        def _():
            pacc[0:TOK, 0:256] += part

        return carry

    lax.fori_loop(0, XC, kv_step, 0)
    kv_s[g, 0] = pacc[0:TOK, 0:HD].astype(BF16)
    kv_s[g, 1] = pacc[0:TOK, HD : 2 * HD].astype(BF16)
    pass_on(ORDER[0])

    dec_own.wait()
    for k in range(1, 8):
        dec_arrival(k).wait_recv()

    width = HEADS * HD // QN
    for n in range(QN):
        for k in range(QK):
            q_copy(n, k).wait()
            at = slice(k * (D // QK), (k + 1) * (D // QK))
            part = jnp.dot(
                x_s[:, at], wq_s[at, n * width : (n + 1) * width], preferred_element_type=F32
            )
            if k == 0:
                pacc[...] = part
            else:
                pacc[...] += part
            for e in POLLS.get(n * QK + k, ()):
                arrive(ORDER[e])
        for hh in range(HEADS // QN):
            h = n * (HEADS // QN) + hh
            for j in range(TILES):
                q_s[j, h * TILE_TOK : (h + 1) * TILE_TOK, :] = (
                    pacc[j * TILE_TOK : (j + 1) * TILE_TOK, hh * HD : (hh + 1) * HD] * SCALE
                ).astype(BF16)
            dq_out[h * DEC : (h + 1) * DEC, :] = (
                pacc[TOK:ALL, hh * HD : (hh + 1) * HD] * SCALE
            ).astype(BF16)
        for t in range(LENT):

            @pl.when(jnp.logical_not(low) & lent(t))
            def _():
                lend(t, n).start()

    dkv = jnp.dot(x_s[TOK:ALL, :], wkv_s[...], preferred_element_type=F32)
    dkv_out[0] = dkv[:, 0:HD].astype(BF16)
    dkv_out[1] = dkv[:, HD : 2 * HD].astype(BF16)

    def prepare(slot):
        side = pl.ds(pl.multiple_of((slot % 2) * TOK, TOK), TOK)
        kt_s[slot // 2, :, side] = kv_s[slot, 0].T
        va_s[slot // 2, side, 0:HD] = kv_s[slot, 1]

    def part_of(item):
        j, block, whole = item
        if whole:
            return j, block, slice(0, 2 * TOK), 2 * TOK
        return j, block // 2, pl.ds(pl.multiple_of((block % 2) * TOK, TOK), TOK), TOK

    def score(item, buf):
        j, two, side, width = part_of(item)
        buf[:, 0:width] = jnp.dot(q_s[j], kt_s[two, :, side], preferred_element_type=F32)

    def absorb(item, buf, weights, ahead):
        j, two, side, width = part_of(item)
        if ahead is not None:
            first = jnp.where(j < TILES, j, j - count) * TILE_TOK + ahead
            lead = lax.broadcasted_iota(jnp.int32, (CHUNK, HD), 1) - lax.broadcasted_iota(
                jnp.int32, (CHUNK, HD), 0
            )
        for c in range(TILE // CHUNK):
            rows = slice(c * CHUNK, (c + 1) * CHUNK)
            cuts = [buf[rows, k * HD : (k + 1) * HD] for k in range(width // HD)]
            if ahead is not None:
                cuts = [
                    jnp.where(lead <= first + (c * CHUNK % TILE_TOK - k * HD), cut, LOW)
                    for k, cut in enumerate(cuts)
                ]
            old = m_s[j, rows, :]
            best = functools.reduce(jnp.maximum, cuts)
            top = jnp.maximum(
                old, jnp.broadcast_to(jnp.max(best, axis=1, keepdims=True), (CHUNK, HD))
            )
            for k, cut in enumerate(cuts):
                weights[rows, k * HD : (k + 1) * HD] = jnp.exp2(cut - top).astype(BF16)
            shrink = jnp.exp2(old - top)
            m_s[j, rows, :] = top
            acc[j, rows, 0:HD] = acc[j, rows, 0:HD] * shrink
            acc[j, rows, HD:] = acc[j, rows, HD:] * shrink
        acc[j] += jnp.dot(weights[:, 0:width], va_s[two, side, :], preferred_element_type=F32)

    def run(n, item, ahead=None):
        @pl.when(n > 0)
        def _():
            score(item(0), sa_s)

        def two(t, carry):
            score(item(2 * t + 1), sb_s)
            absorb(item(2 * t), sa_s, pa_s, ahead)
            score(item(jnp.minimum(2 * t + 2, n - 1)), sa_s)
            absorb(item(2 * t + 1), sb_s, pb_s, ahead)
            return carry

        lax.fori_loop(0, n // 2, two, 0)

        @pl.when(n % 2 == 1)
        def _():
            absorb(item(n - 1), sa_s, pa_s, ahead)

    own = jnp.where(low, TILES, TILES - count)
    taken = jnp.where(low, count, 0)

    prepare(g)
    run(own, lambda t: (t, g, False), 0)

    def finish(j, h):
        rows = slice(h * TILE_TOK, (h + 1) * TILE_TOK)
        return (acc[j, rows, 0:HD] / acc[j, rows, HD:]).astype(BF16)

    def pair_at(i):
        half = i // 4
        step = jnp.where(core == 0, i % 4, i // 2)
        across = jnp.where(core == 0, 1 - half, 1 - i % 2)
        near = jnp.where(step == 0, 0, jnp.where(step == 1, 3, step - 1))
        return ((x + near) % 4) * 2 + (y + across) % 2

    def prepare_pair(i):
        for side in range(2):
            slot = 2 * pair_at(i) + side

            @pl.when(slot <= last)
            def _():
                prepare(slot)

    due = [i for i in range(PAIRS) if i < JOIN or i >= PART]
    wanted = [jnp.where(pair_at(i) < last // 2, 1, 0) for i in due]
    before = [sum(wanted[:k], jnp.int32(0)) for k in range(len(due))]

    def due_at(t):
        return sum(
            jnp.where((wanted[k] == 1) & (before[k] == t), pair_at(due[k]), 0)
            for k in range(len(due))
        )

    def turn(i, carry):
        for at, events in TURNS.items():

            @pl.when(i == at)
            def _():
                for e in events:
                    arrive(ORDER[e])

        @pl.when(i == JOIN)
        def _():
            for t in range(LENT):
                for n in range(QN):

                    @pl.when(low & lent(t))
                    def _():
                        lend(t, n).wait_recv()

        prepare_pair(i)

        @pl.when(i == PART)
        def _():
            prepare_pair(PART + 1)

            def single(k, carry):
                start = jnp.where(k == 2, 0, TILES)
                odd = jnp.where(k == 2, g, last) % 2
                n = jnp.where(k == 0, taken, odd * jnp.where(k == 1, taken, own))
                block = jnp.where(k == 0, last, jnp.where(k == 1, last, g) - 1)
                run(n, lambda t: (start + t, block, False), jnp.where(k == 0, 0, TOK))
                return carry

            lax.fori_loop(0, 3, single, 0)

            def away(j, carry):
                run(before[-1] + wanted[-1], lambda t: (j, due_at(t), True))
                for h in range(HEADS):
                    of_s[j - TILES, :, h * HD : (h + 1) * HD] = finish(j, h)
                for f in range(LENT):

                    @pl.when(j == TILES + f)
                    def _():
                        give_back(f).start()

                return carry

            lax.fori_loop(TILES, TILES + taken, away, 0)

        two = pair_at(i)
        joined = (i >= JOIN) & (i < PART) & (two < last // 2)
        start = jnp.where(two < g // 2, 0, TILES)
        stop = jnp.where(joined & low, TILES + taken, own)
        run(jnp.maximum(stop - start, 0), lambda t: (start + t, two, True))
        return carry

    lax.fori_loop(0, PAIRS, turn, 0)

    for j in range(TILES):

        @pl.when(j < own)
        def _():
            for h in range(HEADS):
                pre_out[j * TILE_TOK : (j + 1) * TILE_TOK, h * HD : (h + 1) * HD] = finish(j, h)

    mine = NEW_ROWS // GROUPS
    at = pl.ds(pl.multiple_of(g * mine, mine), mine)
    for src in range(GROUPS):
        for half in range(2):
            new_out[half, src * mine : (src + 1) * mine, :] = kv_s[src, half, at, :]

    for t in range(LENT):

        @pl.when((t < count) & low)
        def _():
            give_back(t).wait_send()

        @pl.when(lent(t) & jnp.logical_not(low))
        def _():
            for n in range(QN):
                lend(t, n).wait_send()

        @pl.when((t < count) & jnp.logical_not(low))
        def _():
            give_back(t).wait_recv()

    for k in range(1, 8):
        dec_copy(k).wait_send()
    for number in range(len(SENDS)):
        kv_copy(number).wait_send()


def decode(
    table, lens, dest, pre_in, cache, dq, dkv, new,
    pre_out, dec_out,
    pre_s, pool_s, mix_s, page_s, dq_s, out_s, in_sem, out_sem, pool_sem,
):
    half = TOK // 2

    def take(k):
        rows = pl.ds(k * half, half)
        return pltpu.make_async_copy(pre_in.at[rows, :], pre_s.at[rows, :], in_sem.at[k])

    def hand_on(k):
        rows = pl.ds(k * half, half)
        return pltpu.make_async_copy(pre_s.at[rows, :], pre_out.at[rows, :], out_sem.at[k])

    pool = pltpu.make_async_copy(cache, page_s, pool_sem)
    pool.start()
    for k in range(2):
        take(k).start()

    mix_s[pl.ds(0, NEW_ROWS, stride=2), :] = new[0].astype(F32)
    mix_s[pl.ds(1, NEW_ROWS, stride=2), :] = new[1].astype(F32)
    pool.wait()
    for m in range(TOK // PAGE):
        at = pl.ds(pl.multiple_of(dest[0, m] * 2 * PAGE, 2 * PAGE), 2 * PAGE)
        page_s[at, :] = mix_s[m * 2 * PAGE : (m + 1) * 2 * PAGE, :].astype(BF16)
    dq_s[...] = dq[...].astype(F32)
    for r in range(ROWS):
        for j in range(MAXP):
            at = pl.ds(pl.multiple_of(table[r, j] * 2 * PAGE, 2 * PAGE), 2 * PAGE)
            pool_s[r, j * 2 * PAGE : (j + 1) * 2 * PAGE, :] = page_s[at, :]

    for k in range(2):
        take(k).wait()
        hand_on(k).start()

    wide = 2 * MAXP * PAGE
    queries = HEADS * STEPS
    column = lax.broadcasted_iota(jnp.int32, (queries, wide), 1)
    query = lax.broadcasted_iota(jnp.int32, (queries, DEC), 0)
    token = lax.broadcasted_iota(jnp.int32, (queries, DEC), 1)
    so_far = (token >> 3) <= (query & (STEPS - 1))
    s_old, s_new = [], []
    for r in range(ROWS):
        q = dq_s[pl.ds(r, queries, stride=ROWS), :].astype(BF16)

        def scores(keys):
            return lax.dot_general(q, keys, (((1,), (1,)), ((), ())), preferred_element_type=F32)

        live = ((column & 1) == 0) & (column < 2 * lens[r])
        s_old.append(jnp.where(live, scores(pool_s[r]), LOW))
        s_new.append(jnp.where(so_far & ((token & (ROWS - 1)) == r), scores(dkv[0]), LOW))
    tops = [
        jnp.maximum(jnp.max(a, axis=1, keepdims=True), jnp.max(b, axis=1, keepdims=True))
        for a, b in zip(s_old, s_new)
    ]
    p_old = [jnp.exp2(a - top) for a, top in zip(s_old, tops)]
    p_new = [jnp.exp2(b - top) for b, top in zip(s_new, tops)]
    totals = [
        jnp.sum(a, axis=1, keepdims=True) + jnp.sum(b, axis=1, keepdims=True)
        for a, b in zip(p_old, p_new)
    ]
    p_old = [
        jnp.concatenate(
            [pltpu.roll(a[:, k * HD : (k + 1) * HD], 1, 1) for k in range(wide // HD)], axis=1
        ).astype(BF16)
        for a in p_old
    ]
    for r in range(ROWS):
        mixed = jnp.dot(p_old[r], pool_s[r], preferred_element_type=F32) + jnp.dot(
            p_new[r].astype(BF16), dkv[1], preferred_element_type=F32
        )
        out_s[pl.ds(r, queries, stride=ROWS), :] = mixed / totals[r]
    for h in range(HEADS):
        dec_out[:, h * HD : (h + 1) * HD] = out_s[h * DEC : (h + 1) * DEC, :].astype(BF16)
    for k in range(2):
        hand_on(k).wait()


def per_device(pre_x, w_query, w_key, w_value, dec_x, cache, lengths, page_table, dest_slots):
    hbm = pl.BlockSpec(memory_space=pltpu.MemorySpace.HBM)
    vmem = pl.BlockSpec(memory_space=pltpu.MemorySpace.VMEM)
    smem = pl.BlockSpec(memory_space=pltpu.MemorySpace.SMEM)
    pre, dq, dkv, new = pl.pallas_call(
        prefill,
        out_shape=(
            jax.ShapeDtypeStruct((TOK, HEADS * HD), BF16),
            jax.ShapeDtypeStruct((HEADS * DEC, HD), BF16),
            jax.ShapeDtypeStruct((2, DEC, HD), BF16),
            jax.ShapeDtypeStruct((2, NEW_ROWS, HD), BF16),
        ),
        in_specs=[hbm] * 5,
        out_specs=(vmem,) * 4,
        scratch_shapes=[
            pltpu.VMEM((ALL, D), BF16),
            pltpu.VMEM((D, 2 * HD), BF16),
            pltpu.VMEM((D, HEADS * HD), BF16),
            pltpu.VMEM((GROUPS, 2, TOK, HD), BF16),
            pltpu.VMEM((PAIRS, HD, 2 * TOK), BF16),
            pltpu.VMEM((PAIRS, 2 * TOK, 2 * HD), BF16),
            pltpu.VMEM((LENT, TILE_TOK, HEADS * HD), BF16),
            pltpu.VMEM((TILES + LENT, TILE, HD), BF16),
            pltpu.VMEM((ALL, HEADS * HD // QN), F32),
            pltpu.VMEM((TILES + LENT, TILE, 2 * HD), F32),
            pltpu.VMEM((TILES + LENT, TILE, HD), F32),
            pltpu.VMEM((TILE, 2 * TOK), F32),
            pltpu.VMEM((TILE, 2 * TOK), F32),
            pltpu.VMEM((TILE, 2 * TOK), BF16),
            pltpu.VMEM((TILE, 2 * TOK), BF16),
            pltpu.SemaphoreType.DMA((XC,)),
            pltpu.SemaphoreType.DMA((XC,)),
            pltpu.SemaphoreType.DMA((XC,)),
            pltpu.SemaphoreType.DMA((QN * QK,)),
            pltpu.SemaphoreType.DMA,
            pltpu.SemaphoreType.DMA((7,)),
            pltpu.SemaphoreType.DMA((7,)),
            pltpu.SemaphoreType.DMA((len(SENDS),)),
            pltpu.SemaphoreType.DMA((32,)),
            pltpu.SemaphoreType.DMA((LENT * QN,)),
            pltpu.SemaphoreType.DMA((LENT * QN,)),
            pltpu.SemaphoreType.DMA((LENT,)),
            pltpu.SemaphoreType.DMA((LENT,)),
        ],
        compiler_params=pltpu.CompilerParams(
            collective_id=0, has_side_effects=True, vmem_limit_bytes=63 * 1024 * 1024
        ),
    )(pre_x, w_query, w_key, w_value, dec_x.reshape(DEC, D // 8))
    pre_out, dec_out = pl.pallas_call(
        decode,
        out_shape=(
            jax.ShapeDtypeStruct((TOK, HEADS * HD), BF16),
            jax.ShapeDtypeStruct((DEC, HEADS * HD), BF16),
        ),
        in_specs=[smem] * 3 + [hbm] * 2 + [vmem] * 3,
        out_specs=(hbm, vmem),
        scratch_shapes=[
            pltpu.VMEM((TOK, HEADS * HD), BF16),
            pltpu.VMEM((ROWS, 2 * MAXP * PAGE, HD), BF16),
            pltpu.VMEM((2 * NEW_ROWS, HD), F32),
            pltpu.VMEM((CACHE_ROWS, HD), BF16),
            pltpu.VMEM((HEADS * DEC, HD), F32),
            pltpu.VMEM((HEADS * DEC, HD), F32),
            pltpu.SemaphoreType.DMA((2,)),
            pltpu.SemaphoreType.DMA((2,)),
            pltpu.SemaphoreType.DMA,
        ],
        compiler_params=pltpu.CompilerParams(vmem_limit_bytes=63 * 1024 * 1024),
    )(page_table, lengths, dest_slots, pre, cache.reshape(CACHE_ROWS, HD), dq, dkv, new)
    return pre_out, dec_out.reshape(STEPS, ROWS, HEADS * HD)


def solution(mesh):
    in_specs = (
        P(("seq", "pool"), None),
        P(None, "tensor"),
        P(None, "tensor"),
        P(None, "tensor"),
        P(None, ("seq", "pool"), "tensor"),
        P(("seq", "pool"), None, None, "tensor"),
        P(("seq", "pool")),
        P(("seq", "pool"), None),
        P(("seq", "pool"), None),
    )
    out_specs = (P(("seq", "pool"), "tensor"), P(None, ("seq", "pool"), "tensor"))
    return jax.shard_map(
        per_device, mesh=mesh, in_specs=in_specs, out_specs=out_specs, check_vma=False
    )
```

```python
import functools

import jax
import jax.numpy as jnp
from jax import lax
from jax.experimental import pallas as pl
from jax.experimental.pallas import tpu as pltpu
from jax.sharding import PartitionSpec as P

MESH = pl.DeviceIdType.MESH
BF16 = jnp.bfloat16
F32 = jnp.float32

D = 8192
HD = 128
HEADS = 8
TOK = 512
GROUPS = 16
PAGE = 16
MAXP = 16
PAGES = 128
ROWS = 8
STEPS = 4
DEC = ROWS * STEPS
ALL = TOK + DEC
TILE_TOK = 64
TILES = TOK // TILE_TOK
TILE = TILE_TOK * HEADS
CACHE_ROWS = PAGES * PAGE * 2
NEW_ROWS = 512
SCALE = HD ** (-0.5) * 1.4426950408889634
LOW = -1e30
XC = 8
QK = 4
QN = 2
LENT = 4
TAKES = (3, 3, 3, 3, 2, 2, 1, 0)
PAIRS = GROUPS // 2
CHUNK = 16
POLLS = {5: (1, 2), 7: (3, 4, 5)}
JOIN, MISSED, PART, ENDS = 2, 4, 6, 10
TURNS = {1: (6, 7, 8, 9, 10, 11), PART: (12, 13, 14, 15)}
SHIFT = 4.0

ORDER = (
    (0, 0), (3, 0), (1, 0), (0, 3), (0, 1), (2, 0), (3, 3), (3, 1),
    (1, 3), (1, 1), (2, 3), (2, 1), (0, 2), (3, 2), (1, 2), (2, 2),
)


def sends_after(event):
    near, far = event
    sends = []
    if near == 0 and far == 0:
        sends += [(0, "A+"), (0, "A-"), (1, "A+"), (1, "A-")]
    elif far == 0 and near == 3:
        sends += [(0, "A+")]
    elif far == 0 and near == 1:
        sends += [(1, "A-")]
    if far == 0:
        sends += [(0, "B+"), (0, "B-"), (1, "B+"), (1, "B-")]
    elif far == 3:
        sends += [(0, "B+")]
    elif far == 1:
        sends += [(1, "B-")]
    return sends


def seen_from(event, direction):
    near, far = event
    step = 1 if direction[1] == "+" else -1
    if direction[0] == "A":
        return ((near - step) % 4, far)
    return (near, (far - step) % 4)


SENDS = [(event, half, way) for event in ORDER for half, way in sends_after(event)]


def prefill(
    px, wq, wk, wv, dx,
    pre_out, dq_out, dkv_out, new_out,
    x_s, wkv_s, wq_s, kv_s, kt_s, va_s, of_s, q_s, pacc, acc, m_s, sa_s, sb_s, pa_s, pb_s,
    xsem, wksem, wvsem, qsem, dsem_own, dsend, drecv, ssem, rsem, qsend, qrecv, osend, orecv,
):
    seq, tensor, pool = lax.axis_index("seq"), lax.axis_index("tensor"), lax.axis_index("pool")
    x, y, core = seq // 2, pool * 2 + seq % 2, tensor % 2
    g = seq * 2 + pool
    low = g < 8
    other = 15 - g
    last = jnp.where(low, other, g)
    pair = jnp.where(low, g, other)
    count = sum(jnp.where(pair == k, TAKES[k], 0) for k in range(8))
    partner = {"seq": 7 - seq, "pool": 1 - pool}

    def place(near, far):
        ax, ay = (x + near) % 4, (y + far) % 4
        bx, by = (x + far) % 4, (y + near) % 4
        return jnp.where(core == 0, ax, bx), jnp.where(core == 0, ay, by)

    def slot_of(near, far):
        px_, py_ = place(near, far)
        return px_ * 4 + (py_ % 2) * 2 + py_ // 2

    def device(near, far):
        px_, py_ = place(near, far)
        return {"seq": px_ * 2 + py_ % 2, "pool": py_ // 2}

    ways = {"A+": device(1, 0), "A-": device(3, 0), "B+": device(0, 1), "B-": device(0, 3)}

    def x_copy(c):
        cols = pl.ds(pl.multiple_of(c * (D // XC), D // XC), D // XC)
        return pltpu.make_async_copy(px.at[:, cols], x_s.at[pl.ds(0, TOK), cols], xsem.at[c])

    def w_copy(c, ref, at, sem):
        rows = pl.ds(pl.multiple_of(c * (D // XC), D // XC), D // XC)
        return pltpu.make_async_copy(ref.at[rows, :], wkv_s.at[rows, pl.ds(at, HD)], sem.at[c])

    def q_copy(n, k):
        rows = pl.ds(k * (D // QK), D // QK)
        cols = pl.ds(n * (HEADS * HD // QN), HEADS * HD // QN)
        return pltpu.make_async_copy(wq.at[rows, cols], wq_s.at[rows, cols], qsem.at[n * QK + k])

    my_cols = pl.ds(pl.multiple_of(tensor * (D // 8), D // 8), D // 8)
    dec_own = pltpu.make_async_copy(dx, x_s.at[pl.ds(TOK, DEC), my_cols], dsem_own)

    for c in range(XC):
        x_copy(c).start()
        w_copy(c, wk, 0, wksem).start()
        w_copy(c, wv, HD, wvsem).start()
    dec_own.start()

    barrier = pltpu.get_barrier_semaphore()
    for way in ways.values():
        pl.semaphore_signal(barrier, inc=1, device_id=way, device_id_type=MESH)
    pl.semaphore_signal(barrier, inc=1, device_id=partner, device_id_type=MESH)
    for k in range(1, 8):
        pl.semaphore_signal(
            barrier, inc=1, device_id={"tensor": (tensor + k) % 8}, device_id_type=MESH
        )
    pl.semaphore_wait(barrier, 12)

    def dec_copy(k):
        return pltpu.make_async_remote_copy(
            src_ref=dx,
            dst_ref=x_s.at[pl.ds(TOK, DEC), my_cols],
            send_sem=dsend.at[k - 1],
            recv_sem=drecv.at[k - 1],
            device_id={"tensor": (tensor + k) % 8},
            device_id_type=MESH,
        )

    def dec_arrival(k):
        cols = pl.ds(pl.multiple_of(((tensor + 8 - k) % 8) * (D // 8), D // 8), D // 8)
        return pltpu.make_async_remote_copy(
            src_ref=dx,
            dst_ref=x_s.at[pl.ds(TOK, DEC), cols],
            send_sem=dsend.at[k - 1],
            recv_sem=drecv.at[k - 1],
            device_id={"tensor": (tensor + k) % 8},
            device_id_type=MESH,
        )

    for k in range(1, 8):
        dec_copy(k).start()

    def kv_copy(number):
        event, half, way = SENDS[number]
        slot = slot_of(*event)
        near, far = seen_from(event, way)
        return pltpu.make_async_remote_copy(
            src_ref=kv_s.at[slot, half],
            dst_ref=kv_s.at[slot, half],
            send_sem=ssem.at[number],
            recv_sem=rsem.at[(near * 4 + far) * 2 + half],
            device_id=ways[way],
            device_id_type=MESH,
        )

    def pass_on(event):
        for number, (of, _, _) in enumerate(SENDS):
            if of == event:
                kv_copy(number).start()

    def arrive(event):
        near, far = event
        slot = slot_of(near, far)
        for half in range(2):
            pltpu.make_async_remote_copy(
                src_ref=kv_s.at[slot, half],
                dst_ref=kv_s.at[slot, half],
                send_sem=ssem.at[0],
                recv_sem=rsem.at[(near * 4 + far) * 2 + half],
                device_id=ways["A+"],
                device_id_type=MESH,
            ).wait_recv()
        pass_on(event)

    def lend(t, n):
        rows = pl.ds(n * (TILE // QN), TILE // QN)
        return pltpu.make_async_remote_copy(
            src_ref=q_s.at[TILES - LENT + t, rows],
            dst_ref=q_s.at[TILES + t + count - LENT, rows],
            send_sem=qsend.at[t * QN + n],
            recv_sem=qrecv.at[t * QN + n],
            device_id=partner,
            device_id_type=MESH,
        )

    def give_back(f):
        at = pl.ds(pl.multiple_of((TILES - count + f) * TILE_TOK, TILE_TOK), TILE_TOK)
        return pltpu.make_async_remote_copy(
            src_ref=of_s.at[f],
            dst_ref=pre_out.at[at, :],
            send_sem=osend.at[f],
            recv_sem=orecv.at[f],
            device_id=partner,
            device_id_type=MESH,
        )

    def lent(t):
        return count >= LENT - t

    def clear(j, carry):
        acc[j] = jnp.zeros((TILE, 2 * HD), F32)
        m_s[j] = jnp.full((TILE, HD), LOW, F32)
        return carry

    def fill(i, carry):
        va_s[i, :, HD:] = jnp.ones((2 * TOK, HD), BF16)
        return carry

    lax.fori_loop(0, TILES + LENT, clear, 0)
    lax.fori_loop(0, PAIRS, fill, 0)

    def kv_step(c, carry):
        x_copy(c).wait()
        w_copy(c, wk, 0, wksem).wait()
        w_copy(c, wv, HD, wvsem).wait()
        for k in range(QN * QK):

            @pl.when(c == 4 + k // 2)
            def _():
                q_copy(k // QK, k % QK).start()

        at = pl.ds(pl.multiple_of(c * (D // XC), D // XC), D // XC)
        part = jnp.dot(x_s[0:TOK, at], wkv_s[at, :], preferred_element_type=F32)

        @pl.when(c == 0)
        def _():
            pacc[0:TOK, 0:256] = part

        @pl.when(c > 0)
        def _():
            pacc[0:TOK, 0:256] += part

        return carry

    lax.fori_loop(0, XC, kv_step, 0)
    kv_s[g, 0] = pacc[0:TOK, 0:HD].astype(BF16)
    kv_s[g, 1] = pacc[0:TOK, HD : 2 * HD].astype(BF16)
    pass_on(ORDER[0])

    dec_own.wait()
    for k in range(1, 8):
        dec_arrival(k).wait_recv()

    width = HEADS * HD // QN
    for n in range(QN):
        for k in range(QK):
            q_copy(n, k).wait()
            at = slice(k * (D // QK), (k + 1) * (D // QK))
            part = jnp.dot(
                x_s[:, at], wq_s[at, n * width : (n + 1) * width], preferred_element_type=F32
            )
            if k == 0:
                pacc[...] = part
            else:
                pacc[...] += part
            for e in POLLS.get(n * QK + k, ()):
                arrive(ORDER[e])
        for hh in range(HEADS // QN):
            h = n * (HEADS // QN) + hh
            for j in range(TILES):
                q_s[j, h * TILE_TOK : (h + 1) * TILE_TOK, :] = (
                    pacc[j * TILE_TOK : (j + 1) * TILE_TOK, hh * HD : (hh + 1) * HD] * SCALE
                ).astype(BF16)
            dq_out[h * DEC : (h + 1) * DEC, :] = (
                pacc[TOK:ALL, hh * HD : (hh + 1) * HD] * SCALE
            ).astype(BF16)
        for t in range(LENT):

            @pl.when(jnp.logical_not(low) & lent(t))
            def _():
                lend(t, n).start()

    dkv = jnp.dot(x_s[TOK:ALL, :], wkv_s[...], preferred_element_type=F32)
    dkv_out[0] = dkv[:, 0:HD].astype(BF16)
    dkv_out[1] = dkv[:, HD : 2 * HD].astype(BF16)

    def prepare(slot):
        side = pl.ds(pl.multiple_of((slot % 2) * TOK, TOK), TOK)
        kt_s[slot // 2, :, side] = kv_s[slot, 0].T
        va_s[slot // 2, side, 0:HD] = kv_s[slot, 1]

    def part_of(item):
        j, block, whole = item
        if whole:
            return j, block, slice(0, 2 * TOK), 2 * TOK
        return j, block // 2, pl.ds(pl.multiple_of((block % 2) * TOK, TOK), TOK), TOK

    def score(item, buf):
        j, two, side, width = part_of(item)
        buf[:, 0:width] = jnp.dot(q_s[j], kt_s[two, :, side], preferred_element_type=F32)

    def absorb(item, buf, weights, ahead):
        j, two, side, width = part_of(item)
        if ahead is not None:
            first = jnp.where(j < TILES, j, j - count) * TILE_TOK + ahead
            lead = lax.broadcasted_iota(jnp.int32, (CHUNK, HD), 1) - lax.broadcasted_iota(
                jnp.int32, (CHUNK, HD), 0
            )
        for c in range(TILE // CHUNK):
            rows = slice(c * CHUNK, (c + 1) * CHUNK)
            cuts = [buf[rows, k * HD : (k + 1) * HD] for k in range(width // HD)]
            if ahead is not None:
                cuts = [
                    jnp.where(lead <= first + (c * CHUNK % TILE_TOK - k * HD), cut, LOW)
                    for k, cut in enumerate(cuts)
                ]
            old = m_s[j, rows, :]
            best = functools.reduce(jnp.maximum, cuts)
            top = jnp.maximum(
                old, jnp.broadcast_to(jnp.max(best, axis=1, keepdims=True) - SHIFT, (CHUNK, HD))
            )
            for k, cut in enumerate(cuts):
                weights[rows, k * HD : (k + 1) * HD] = jnp.exp2((cut - top).astype(BF16))
            shrink = jnp.exp2(old - top)
            m_s[j, rows, :] = top
            acc[j, rows, 0:HD] = acc[j, rows, 0:HD] * shrink
            acc[j, rows, HD:] = acc[j, rows, HD:] * shrink
        acc[j] += jnp.dot(weights[:, 0:width], va_s[two, side, :], preferred_element_type=F32)

    def run(n, item, ahead=None):
        @pl.when(n > 0)
        def _():
            score(item(0), sa_s)

        def two(t, carry):
            score(item(2 * t + 1), sb_s)
            absorb(item(2 * t), sa_s, pa_s, ahead)
            score(item(jnp.minimum(2 * t + 2, n - 1)), sa_s)
            absorb(item(2 * t + 1), sb_s, pb_s, ahead)
            return carry

        lax.fori_loop(0, n // 2, two, 0)

        @pl.when(n % 2 == 1)
        def _():
            absorb(item(n - 1), sa_s, pa_s, ahead)

    own = jnp.where(low, TILES, TILES - count)
    taken = jnp.where(low, count, 0)

    prepare(g)
    run(own, lambda t: (t, g, False), 0)

    def finish(j, h):
        rows = slice(h * TILE_TOK, (h + 1) * TILE_TOK)
        return (acc[j, rows, 0:HD] / acc[j, rows, HD:]).astype(BF16)

    def pair_at(i):
        half = i // 4
        step = jnp.where(core == 0, i % 4, i // 2)
        across = jnp.where(core == 0, 1 - half, 1 - i % 2)
        near = jnp.where(step == 0, 0, jnp.where(step == 1, 3, step - 1))
        return ((x + near) % 4) * 2 + (y + across) % 2

    def prepare_pair(i):
        for side in range(2):
            slot = 2 * pair_at(i) + side

            @pl.when(slot <= last)
            def _():
                prepare(slot)

    due = range(PAIRS // 2, PAIRS)
    wanted = [jnp.where(pair_at(i) < last // 2, 1, 0) for i in due]
    before = [sum(wanted[:k], jnp.int32(0)) for k in range(len(due))]

    def due_at(t):
        return sum(
            jnp.where((wanted[k] == 1) & (before[k] == t), pair_at(due[k]), 0)
            for k in range(len(due))
        )

    def turn(s, carry):
        for at, events in TURNS.items():

            @pl.when(s == at)
            def _():
                for e in events:
                    arrive(ORDER[e])

        i = jnp.where(s < MISSED, s, jnp.where(s < PART, s - MISSED, s - PART + PAIRS // 2))

        @pl.when(s < MISSED)
        def _():
            prepare_pair(i)

        @pl.when(s == JOIN)
        def _():
            for t in range(LENT):
                for n in range(QN):

                    @pl.when(low & lent(t))
                    def _():
                        lend(t, n).wait_recv()

        @pl.when((s == MISSED) & (taken > 0))
        def _():
            def single(k, carry):
                block = last - k
                prepare(block)
                run(taken, lambda t: (TILES + t, block, False), k * TOK)
                return carry

            lax.fori_loop(0, 1 + last % 2, single, 0)

        @pl.when(s == PART)
        def _():
            def rest(k, carry):
                prepare_pair(k)
                return carry

            lax.fori_loop(PAIRS // 2, PAIRS, rest, 0)

            def away(j, carry):
                run(before[-1] + wanted[-1], lambda t: (j, due_at(t), True))
                for h in range(HEADS):
                    of_s[j - TILES, :, h * HD : (h + 1) * HD] = finish(j, h)
                for f in range(LENT):

                    @pl.when(j == TILES + f)
                    def _():
                        give_back(f).start()

                return carry

            lax.fori_loop(TILES, TILES + taken, away, 0)
            run(own * (g % 2), lambda t: (t, g - 1, False))

        two = pair_at(i)
        join = (s >= JOIN) & (s < PART) & (two < last // 2)
        start = jnp.where((two < g // 2) & ((s < MISSED) | (s >= PART)), 0, TILES)
        stop = jnp.where(join & low, TILES + taken, jnp.where(start == 0, own, 0))
        run(jnp.maximum(stop - start, 0), lambda t: (start + t, two, True))
        return carry

    lax.fori_loop(0, ENDS, turn, 0)

    for j in range(TILES):

        @pl.when(j < own)
        def _():
            for h in range(HEADS):
                pre_out[j * TILE_TOK : (j + 1) * TILE_TOK, h * HD : (h + 1) * HD] = finish(j, h)

    mine = NEW_ROWS // GROUPS
    at = pl.ds(pl.multiple_of(g * mine, mine), mine)
    for src in range(GROUPS):
        for half in range(2):
            new_out[half, src * mine : (src + 1) * mine, :] = kv_s[src, half, at, :]

    for t in range(LENT):

        @pl.when((t < count) & low)
        def _():
            give_back(t).wait_send()

        @pl.when(lent(t) & jnp.logical_not(low))
        def _():
            for n in range(QN):
                lend(t, n).wait_send()

        @pl.when((t < count) & jnp.logical_not(low))
        def _():
            give_back(t).wait_recv()

    for k in range(1, 8):
        dec_copy(k).wait_send()
    for number in range(len(SENDS)):
        kv_copy(number).wait_send()


def decode(
    table, lens, dest, pre_in, cache, dq, dkv, new,
    pre_out, dec_out,
    pre_s, pool_s, mix_s, page_s, dq_s, out_s, in_sem, out_sem, pool_sem,
):
    half = TOK // 2

    def take(k):
        rows = pl.ds(k * half, half)
        return pltpu.make_async_copy(pre_in.at[rows, :], pre_s.at[rows, :], in_sem.at[k])

    def hand_on(k):
        rows = pl.ds(k * half, half)
        return pltpu.make_async_copy(pre_s.at[rows, :], pre_out.at[rows, :], out_sem.at[k])

    pool = pltpu.make_async_copy(cache, page_s, pool_sem)
    pool.start()
    for k in range(2):
        take(k).start()

    mix_s[pl.ds(0, NEW_ROWS, stride=2), :] = new[0].astype(F32)
    mix_s[pl.ds(1, NEW_ROWS, stride=2), :] = new[1].astype(F32)
    pool.wait()
    for m in range(TOK // PAGE):
        at = pl.ds(pl.multiple_of(dest[0, m] * 2 * PAGE, 2 * PAGE), 2 * PAGE)
        page_s[at, :] = mix_s[m * 2 * PAGE : (m + 1) * 2 * PAGE, :].astype(BF16)
    dq_s[...] = dq[...].astype(F32)
    for r in range(ROWS):
        for j in range(MAXP):
            at = pl.ds(pl.multiple_of(table[r, j] * 2 * PAGE, 2 * PAGE), 2 * PAGE)
            pool_s[r, j * 2 * PAGE : (j + 1) * 2 * PAGE, :] = page_s[at, :]

    for k in range(2):
        take(k).wait()
        hand_on(k).start()

    wide = 2 * MAXP * PAGE
    queries = HEADS * STEPS
    column = lax.broadcasted_iota(jnp.int32, (queries, wide), 1)
    query = lax.broadcasted_iota(jnp.int32, (queries, DEC), 0)
    token = lax.broadcasted_iota(jnp.int32, (queries, DEC), 1)
    so_far = (token >> 3) <= (query & (STEPS - 1))
    s_old, s_new = [], []
    for r in range(ROWS):
        q = dq_s[pl.ds(r, queries, stride=ROWS), :].astype(BF16)

        def scores(keys):
            return lax.dot_general(q, keys, (((1,), (1,)), ((), ())), preferred_element_type=F32)

        live = ((column & 1) == 0) & (column < 2 * lens[r])
        s_old.append(jnp.where(live, scores(pool_s[r]), LOW))
        s_new.append(jnp.where(so_far & ((token & (ROWS - 1)) == r), scores(dkv[0]), LOW))
    tops = [
        jnp.maximum(jnp.max(a, axis=1, keepdims=True), jnp.max(b, axis=1, keepdims=True))
        for a, b in zip(s_old, s_new)
    ]
    p_old = [jnp.exp2(a - top) for a, top in zip(s_old, tops)]
    p_new = [jnp.exp2(b - top) for b, top in zip(s_new, tops)]
    totals = [
        jnp.sum(a, axis=1, keepdims=True) + jnp.sum(b, axis=1, keepdims=True)
        for a, b in zip(p_old, p_new)
    ]
    p_old = [
        jnp.concatenate(
            [pltpu.roll(a[:, k * HD : (k + 1) * HD], 1, 1) for k in range(wide // HD)], axis=1
        ).astype(BF16)
        for a in p_old
    ]
    for r in range(ROWS):
        mixed = jnp.dot(p_old[r], pool_s[r], preferred_element_type=F32) + jnp.dot(
            p_new[r].astype(BF16), dkv[1], preferred_element_type=F32
        )
        out_s[pl.ds(r, queries, stride=ROWS), :] = mixed / totals[r]
    for h in range(HEADS):
        dec_out[:, h * HD : (h + 1) * HD] = out_s[h * DEC : (h + 1) * DEC, :].astype(BF16)
    for k in range(2):
        hand_on(k).wait()


def per_device(pre_x, w_query, w_key, w_value, dec_x, cache, lengths, page_table, dest_slots):
    hbm = pl.BlockSpec(memory_space=pltpu.MemorySpace.HBM)
    vmem = pl.BlockSpec(memory_space=pltpu.MemorySpace.VMEM)
    smem = pl.BlockSpec(memory_space=pltpu.MemorySpace.SMEM)
    pre, dq, dkv, new = pl.pallas_call(
        prefill,
        out_shape=(
            jax.ShapeDtypeStruct((TOK, HEADS * HD), BF16),
            jax.ShapeDtypeStruct((HEADS * DEC, HD), BF16),
            jax.ShapeDtypeStruct((2, DEC, HD), BF16),
            jax.ShapeDtypeStruct((2, NEW_ROWS, HD), BF16),
        ),
        in_specs=[hbm] * 5,
        out_specs=(vmem,) * 4,
        scratch_shapes=[
            pltpu.VMEM((ALL, D), BF16),
            pltpu.VMEM((D, 2 * HD), BF16),
            pltpu.VMEM((D, HEADS * HD), BF16),
            pltpu.VMEM((GROUPS, 2, TOK, HD), BF16),
            pltpu.VMEM((PAIRS, HD, 2 * TOK), BF16),
            pltpu.VMEM((PAIRS, 2 * TOK, 2 * HD), BF16),
            pltpu.VMEM((LENT, TILE_TOK, HEADS * HD), BF16),
            pltpu.VMEM((TILES + LENT, TILE, HD), BF16),
            pltpu.VMEM((ALL, HEADS * HD // QN), F32),
            pltpu.VMEM((TILES + LENT, TILE, 2 * HD), F32),
            pltpu.VMEM((TILES + LENT, TILE, HD), F32),
            pltpu.VMEM((TILE, 2 * TOK), F32),
            pltpu.VMEM((TILE, 2 * TOK), F32),
            pltpu.VMEM((TILE, 2 * TOK), BF16),
            pltpu.VMEM((TILE, 2 * TOK), BF16),
            pltpu.SemaphoreType.DMA((XC,)),
            pltpu.SemaphoreType.DMA((XC,)),
            pltpu.SemaphoreType.DMA((XC,)),
            pltpu.SemaphoreType.DMA((QN * QK,)),
            pltpu.SemaphoreType.DMA,
            pltpu.SemaphoreType.DMA((7,)),
            pltpu.SemaphoreType.DMA((7,)),
            pltpu.SemaphoreType.DMA((len(SENDS),)),
            pltpu.SemaphoreType.DMA((32,)),
            pltpu.SemaphoreType.DMA((LENT * QN,)),
            pltpu.SemaphoreType.DMA((LENT * QN,)),
            pltpu.SemaphoreType.DMA((LENT,)),
            pltpu.SemaphoreType.DMA((LENT,)),
        ],
        compiler_params=pltpu.CompilerParams(
            collective_id=0, has_side_effects=True, vmem_limit_bytes=63 * 1024 * 1024
        ),
    )(pre_x, w_query, w_key, w_value, dec_x.reshape(DEC, D // 8))
    pre_out, dec_out = pl.pallas_call(
        decode,
        out_shape=(
            jax.ShapeDtypeStruct((TOK, HEADS * HD), BF16),
            jax.ShapeDtypeStruct((DEC, HEADS * HD), BF16),
        ),
        in_specs=[smem] * 3 + [hbm] * 2 + [vmem] * 3,
        out_specs=(hbm, vmem),
        scratch_shapes=[
            pltpu.VMEM((TOK, HEADS * HD), BF16),
            pltpu.VMEM((ROWS, 2 * MAXP * PAGE, HD), BF16),
            pltpu.VMEM((2 * NEW_ROWS, HD), F32),
            pltpu.VMEM((CACHE_ROWS, HD), BF16),
            pltpu.VMEM((HEADS * DEC, HD), F32),
            pltpu.VMEM((HEADS * DEC, HD), F32),
            pltpu.SemaphoreType.DMA((2,)),
            pltpu.SemaphoreType.DMA((2,)),
            pltpu.SemaphoreType.DMA,
        ],
        compiler_params=pltpu.CompilerParams(vmem_limit_bytes=63 * 1024 * 1024),
    )(page_table, lengths, dest_slots, pre, cache.reshape(CACHE_ROWS, HD), dq, dkv, new)
    return pre_out, dec_out.reshape(STEPS, ROWS, HEADS * HD)


def solution(mesh):
    in_specs = (
        P(("seq", "pool"), None),
        P(None, "tensor"),
        P(None, "tensor"),
        P(None, "tensor"),
        P(None, ("seq", "pool"), "tensor"),
        P(("seq", "pool"), None, None, "tensor"),
        P(("seq", "pool")),
        P(("seq", "pool"), None),
        P(("seq", "pool"), None),
    )
    out_specs = (P(("seq", "pool"), "tensor"), P(None, ("seq", "pool"), "tensor"))
    return jax.shard_map(
        per_device, mesh=mesh, in_specs=in_specs, out_specs=out_specs, check_vma=False
    )
```

```python
import functools

import jax
import jax.numpy as jnp
from jax import lax
from jax.experimental import pallas as pl
from jax.experimental.pallas import tpu as pltpu
from jax.sharding import PartitionSpec as P

MESH = pl.DeviceIdType.MESH
BF16 = jnp.bfloat16
F32 = jnp.float32

D = 8192
HD = 128
HEADS = 8
TOK = 512
GROUPS = 16
PAGE = 16
MAXP = 16
PAGES = 128
ROWS = 8
STEPS = 4
DEC = ROWS * STEPS
ALL = TOK + DEC
TILES = HEADS
TILE = TOK
CACHE_ROWS = PAGES * PAGE * 2
NEW_ROWS = 512
SCALE = HD ** (-0.5) * 1.4426950408889634
LOW = -1e30
XC = 8
QK = 4
QN = 2
LENT = 4
TAKES = (3, 3, 3, 3, 2, 2, 1, 0)
PAIRS = GROUPS // 2
CHUNK = 16
POLLS = {5: (1, 2), 7: (3, 4, 5)}
JOIN, MISSED, PART, ENDS = 2, 4, 6, 10
TURNS = {1: (6, 7, 8, 9, 10, 11), PART: (12, 13, 14, 15)}

ORDER = (
    (0, 0), (3, 0), (1, 0), (0, 3), (0, 1), (2, 0), (3, 3), (3, 1),
    (1, 3), (1, 1), (2, 3), (2, 1), (0, 2), (3, 2), (1, 2), (2, 2),
)


def sends_after(event):
    near, far = event
    sends = []
    if near == 0 and far == 0:
        sends += [(0, "A+"), (0, "A-"), (1, "A+"), (1, "A-")]
    elif far == 0 and near == 3:
        sends += [(0, "A+")]
    elif far == 0 and near == 1:
        sends += [(1, "A-")]
    if far == 0:
        sends += [(0, "B+"), (0, "B-"), (1, "B+"), (1, "B-")]
    elif far == 3:
        sends += [(0, "B+")]
    elif far == 1:
        sends += [(1, "B-")]
    return sends


def seen_from(event, direction):
    near, far = event
    step = 1 if direction[1] == "+" else -1
    if direction[0] == "A":
        return ((near - step) % 4, far)
    return (near, (far - step) % 4)


SENDS = [(event, half, way) for event in ORDER for half, way in sends_after(event)]


def prefill(
    px, wq, wk, wv, dx,
    pre_out, dq_out, dkv_out, new_out,
    x_s, wkv_s, wq_s, kv_s, kt_s, va_s, of_s, q_s, pacc, acc, m_s, sa_s, sb_s, pa_s, pb_s,
    xsem, wksem, wvsem, qsem, dsem_own, dsend, drecv, ssem, rsem, qsend, qrecv, osend, orecv,
):
    seq, tensor, pool = lax.axis_index("seq"), lax.axis_index("tensor"), lax.axis_index("pool")
    x, y, core = seq // 2, pool * 2 + seq % 2, tensor % 2
    g = seq * 2 + pool
    low = g < 8
    other = 15 - g
    last = jnp.where(low, other, g)
    pair = jnp.where(low, g, other)
    count = sum(jnp.where(pair == k, TAKES[k], 0) for k in range(8))
    partner = {"seq": 7 - seq, "pool": 1 - pool}

    def place(near, far):
        ax, ay = (x + near) % 4, (y + far) % 4
        bx, by = (x + far) % 4, (y + near) % 4
        return jnp.where(core == 0, ax, bx), jnp.where(core == 0, ay, by)

    def slot_of(near, far):
        px_, py_ = place(near, far)
        return px_ * 4 + (py_ % 2) * 2 + py_ // 2

    def device(near, far):
        px_, py_ = place(near, far)
        return {"seq": px_ * 2 + py_ % 2, "pool": py_ // 2}

    ways = {"A+": device(1, 0), "A-": device(3, 0), "B+": device(0, 1), "B-": device(0, 3)}

    def x_copy(c):
        cols = pl.ds(pl.multiple_of(c * (D // XC), D // XC), D // XC)
        return pltpu.make_async_copy(px.at[:, cols], x_s.at[pl.ds(0, TOK), cols], xsem.at[c])

    def w_copy(c, ref, at, sem):
        rows = pl.ds(pl.multiple_of(c * (D // XC), D // XC), D // XC)
        return pltpu.make_async_copy(ref.at[rows, :], wkv_s.at[rows, pl.ds(at, HD)], sem.at[c])

    def q_copy(n, k):
        rows = pl.ds(k * (D // QK), D // QK)
        cols = pl.ds(n * (HEADS * HD // QN), HEADS * HD // QN)
        return pltpu.make_async_copy(wq.at[rows, cols], wq_s.at[rows, cols], qsem.at[n * QK + k])

    my_cols = pl.ds(pl.multiple_of(tensor * (D // 8), D // 8), D // 8)
    dec_own = pltpu.make_async_copy(dx, x_s.at[pl.ds(TOK, DEC), my_cols], dsem_own)

    for c in range(XC):
        x_copy(c).start()
        w_copy(c, wk, 0, wksem).start()
        w_copy(c, wv, HD, wvsem).start()
    dec_own.start()

    barrier = pltpu.get_barrier_semaphore()
    for way in ways.values():
        pl.semaphore_signal(barrier, inc=1, device_id=way, device_id_type=MESH)
    pl.semaphore_signal(barrier, inc=1, device_id=partner, device_id_type=MESH)
    for k in range(1, 8):
        pl.semaphore_signal(
            barrier, inc=1, device_id={"tensor": (tensor + k) % 8}, device_id_type=MESH
        )
    pl.semaphore_wait(barrier, 12)

    def dec_copy(k):
        return pltpu.make_async_remote_copy(
            src_ref=dx,
            dst_ref=x_s.at[pl.ds(TOK, DEC), my_cols],
            send_sem=dsend.at[k - 1],
            recv_sem=drecv.at[k - 1],
            device_id={"tensor": (tensor + k) % 8},
            device_id_type=MESH,
        )

    def dec_arrival(k):
        cols = pl.ds(pl.multiple_of(((tensor + 8 - k) % 8) * (D // 8), D // 8), D // 8)
        return pltpu.make_async_remote_copy(
            src_ref=dx,
            dst_ref=x_s.at[pl.ds(TOK, DEC), cols],
            send_sem=dsend.at[k - 1],
            recv_sem=drecv.at[k - 1],
            device_id={"tensor": (tensor + k) % 8},
            device_id_type=MESH,
        )

    for k in range(1, 8):
        dec_copy(k).start()

    def kv_copy(number):
        event, half, way = SENDS[number]
        slot = slot_of(*event)
        near, far = seen_from(event, way)
        return pltpu.make_async_remote_copy(
            src_ref=kv_s.at[slot, half],
            dst_ref=kv_s.at[slot, half],
            send_sem=ssem.at[number],
            recv_sem=rsem.at[(near * 4 + far) * 2 + half],
            device_id=ways[way],
            device_id_type=MESH,
        )

    def pass_on(event):
        for number, (of, _, _) in enumerate(SENDS):
            if of == event:
                kv_copy(number).start()

    def arrive(event):
        near, far = event
        slot = slot_of(near, far)
        for half in range(2):
            pltpu.make_async_remote_copy(
                src_ref=kv_s.at[slot, half],
                dst_ref=kv_s.at[slot, half],
                send_sem=ssem.at[0],
                recv_sem=rsem.at[(near * 4 + far) * 2 + half],
                device_id=ways["A+"],
                device_id_type=MESH,
            ).wait_recv()
        pass_on(event)

    def lend(t):
        return pltpu.make_async_remote_copy(
            src_ref=q_s.at[t],
            dst_ref=q_s.at[TILES + t],
            send_sem=qsend.at[t],
            recv_sem=qrecv.at[t],
            device_id=partner,
            device_id_type=MESH,
        )

    def give_back(t):
        return pltpu.make_async_remote_copy(
            src_ref=of_s.at[t],
            dst_ref=pre_out.at[:, pl.ds(t * HD, HD)],
            send_sem=osend.at[t],
            recv_sem=orecv.at[t],
            device_id=partner,
            device_id_type=MESH,
        )

    def clear(j, carry):
        acc[j] = jnp.zeros((TILE, 2 * HD), F32)
        m_s[j] = jnp.full((TILE, HD), LOW, F32)
        return carry

    def fill(i, carry):
        va_s[i, :, HD:] = jnp.ones((2 * TOK, HD), BF16)
        return carry

    lax.fori_loop(0, TILES + LENT, clear, 0)
    lax.fori_loop(0, PAIRS, fill, 0)

    def kv_step(c, carry):
        x_copy(c).wait()
        w_copy(c, wk, 0, wksem).wait()
        w_copy(c, wv, HD, wvsem).wait()
        for k in range(QN * QK):

            @pl.when(c == 4 + k // 2)
            def _():
                q_copy(k // QK, k % QK).start()

        at = pl.ds(pl.multiple_of(c * (D // XC), D // XC), D // XC)
        part = jnp.dot(x_s[0:TOK, at], wkv_s[at, :], preferred_element_type=F32)

        @pl.when(c == 0)
        def _():
            pacc[0:TOK, 0:256] = part

        @pl.when(c > 0)
        def _():
            pacc[0:TOK, 0:256] += part

        return carry

    lax.fori_loop(0, XC, kv_step, 0)
    kv_s[g, 0] = pacc[0:TOK, 0:HD].astype(BF16)
    kv_s[g, 1] = pacc[0:TOK, HD : 2 * HD].astype(BF16)
    pass_on(ORDER[0])

    dec_own.wait()
    for k in range(1, 8):
        dec_arrival(k).wait_recv()

    width = HEADS * HD // QN
    for n in range(QN):
        for k in range(QK):
            q_copy(n, k).wait()
            at = slice(k * (D // QK), (k + 1) * (D // QK))
            part = jnp.dot(
                x_s[:, at], wq_s[at, n * width : (n + 1) * width], preferred_element_type=F32
            )
            if k == 0:
                pacc[...] = part
            else:
                pacc[...] += part
            for e in POLLS.get(n * QK + k, ()):
                arrive(ORDER[e])
        for hh in range(HEADS // QN):
            h = n * (HEADS // QN) + hh
            q_s[h] = (pacc[0:TOK, hh * HD : (hh + 1) * HD] * SCALE).astype(BF16)
            dq_out[h * DEC : (h + 1) * DEC, :] = (
                pacc[TOK:ALL, hh * HD : (hh + 1) * HD] * SCALE
            ).astype(BF16)
        if n == 0:
            for t in range(LENT):

                @pl.when(jnp.logical_not(low) & (t < count))
                def _():
                    lend(t).start()

    dkv = jnp.dot(x_s[TOK:ALL, :], wkv_s[...], preferred_element_type=F32)
    dkv_out[0] = dkv[:, 0:HD].astype(BF16)
    dkv_out[1] = dkv[:, HD : 2 * HD].astype(BF16)

    def prepare(slot):
        side = pl.ds(pl.multiple_of((slot % 2) * TOK, TOK), TOK)
        kt_s[slot // 2, :, side] = kv_s[slot, 0].T
        va_s[slot // 2, side, 0:HD] = kv_s[slot, 1]

    def part_of(item):
        j, block, whole = item
        if whole:
            return j, block, slice(0, 2 * TOK), 2 * TOK
        return j, block // 2, pl.ds(pl.multiple_of((block % 2) * TOK, TOK), TOK), TOK

    def score(item, buf):
        j, two, side, width = part_of(item)
        buf[:, 0:width] = jnp.dot(q_s[j], kt_s[two, :, side], preferred_element_type=F32)

    def absorb(item, buf, weights, ahead):
        j, two, side, width = part_of(item)
        if ahead is not None:
            lead = lax.broadcasted_iota(jnp.int32, (CHUNK, HD), 1) - lax.broadcasted_iota(
                jnp.int32, (CHUNK, HD), 0
            )
        for c in range(TILE // CHUNK):
            rows = slice(c * CHUNK, (c + 1) * CHUNK)
            cuts = [buf[rows, k * HD : (k + 1) * HD] for k in range(width // HD)]
            if ahead is not None:
                cuts = [
                    jnp.where(lead <= c * CHUNK - k * HD + ahead, cut, LOW)
                    for k, cut in enumerate(cuts)
                ]
            if isinstance(ahead, int):
                clear_from = (ahead + (c + 1) * CHUNK - 1) // HD + 1
                for k in range(clear_from, len(cuts)):
                    weights[rows, k * HD : (k + 1) * HD] = jnp.zeros((CHUNK, HD), BF16)
                cuts = cuts[:clear_from]
            old = m_s[j, rows, :]
            best = functools.reduce(jnp.maximum, cuts)
            top = jnp.maximum(
                old, jnp.broadcast_to(jnp.max(best, axis=1, keepdims=True), (CHUNK, HD))
            )
            for k, cut in enumerate(cuts):
                weights[rows, k * HD : (k + 1) * HD] = jnp.exp2(cut - top).astype(BF16)
            shrink = jnp.exp2(old - top)
            m_s[j, rows, :] = top
            acc[j, rows, 0:HD] = acc[j, rows, 0:HD] * shrink
            acc[j, rows, HD:] = acc[j, rows, HD:] * shrink
        acc[j] += jnp.dot(weights[:, 0:width], va_s[two, side, :], preferred_element_type=F32)

    def run(n, item, ahead=None):
        @pl.when(n > 0)
        def _():
            score(item(0), sa_s)

        def two(t, carry):
            score(item(2 * t + 1), sb_s)
            absorb(item(2 * t), sa_s, pa_s, ahead)
            score(item(jnp.minimum(2 * t + 2, n - 1)), sa_s)
            absorb(item(2 * t + 1), sb_s, pb_s, ahead)
            return carry

        lax.fori_loop(0, n // 2, two, 0)

        @pl.when(n % 2 == 1)
        def _():
            absorb(item(n - 1), sa_s, pa_s, ahead)

    first = jnp.where(low, 0, count)
    own = TILES - first
    taken = jnp.where(low, count, 0)

    prepare(g)
    run(own, lambda t: (first + t, g, False), 0)

    def finish(j):
        return (acc[j, :, 0:HD] / acc[j, :, HD:]).astype(BF16)

    def pair_at(i):
        half = i // 4
        step = jnp.where(core == 0, i % 4, i // 2)
        across = jnp.where(core == 0, 1 - half, 1 - i % 2)
        near = jnp.where(step == 0, 0, jnp.where(step == 1, 3, step - 1))
        return ((x + near) % 4) * 2 + (y + across) % 2

    def prepare_pair(i):
        for side in range(2):
            slot = 2 * pair_at(i) + side

            @pl.when(slot <= last)
            def _():
                prepare(slot)

    due = range(PAIRS // 2, PAIRS)
    wanted = [jnp.where(pair_at(i) < last // 2, 1, 0) for i in due]
    before = [sum(wanted[:k], jnp.int32(0)) for k in range(len(due))]

    def due_at(t):
        return sum(
            jnp.where((wanted[k] == 1) & (before[k] == t), pair_at(due[k]), 0)
            for k in range(len(due))
        )

    def turn(s, carry):
        for at, events in TURNS.items():

            @pl.when(s == at)
            def _():
                for e in events:
                    arrive(ORDER[e])

        i = jnp.where(s < MISSED, s, jnp.where(s < PART, s - MISSED, s - PART + PAIRS // 2))

        @pl.when(s < MISSED)
        def _():
            prepare_pair(i)

        @pl.when(s == JOIN)
        def _():
            for t in range(LENT):

                @pl.when(low & (t < count))
                def _():
                    lend(t).wait_recv()

        @pl.when((s == MISSED) & (taken > 0))
        def _():
            def single(k, carry):
                block = last - k
                prepare(block)
                run(taken, lambda t: (TILES + t, block, False), k * TOK)
                return carry

            lax.fori_loop(0, 1 + last % 2, single, 0)

        @pl.when(s == PART)
        def _():
            def rest(k, carry):
                prepare_pair(k)
                return carry

            lax.fori_loop(PAIRS // 2, PAIRS, rest, 0)

            def away(j, carry):
                run(before[-1] + wanted[-1], lambda t: (j, due_at(t), True))
                of_s[j - TILES] = finish(j)
                for f in range(LENT):

                    @pl.when(j == TILES + f)
                    def _():
                        give_back(f).start()

                return carry

            lax.fori_loop(TILES, TILES + taken, away, 0)
            run(own * (g % 2), lambda t: (first + t, g - 1, False))

        two = pair_at(i)
        join = (s >= JOIN) & (s < PART) & (two < last // 2)
        start = jnp.where((two < g // 2) & ((s < MISSED) | (s >= PART)), first, TILES)
        stop = jnp.where(join, TILES + taken, TILES)
        run(jnp.maximum(stop - start, 0), lambda t: (start + t, two, True))
        return carry

    lax.fori_loop(0, ENDS, turn, 0)

    for j in range(TILES):

        @pl.when(j >= first)
        def _():
            pre_out[:, j * HD : (j + 1) * HD] = finish(j)

    mine = NEW_ROWS // GROUPS
    at = pl.ds(pl.multiple_of(g * mine, mine), mine)
    for src in range(GROUPS):
        for half in range(2):
            new_out[half, src * mine : (src + 1) * mine, :] = kv_s[src, half, at, :]

    for t in range(LENT):

        @pl.when((t < count) & low)
        def _():
            give_back(t).wait_send()

        @pl.when((t < count) & jnp.logical_not(low))
        def _():
            lend(t).wait_send()
            give_back(t).wait_recv()

    for k in range(1, 8):
        dec_copy(k).wait_send()
    for number in range(len(SENDS)):
        kv_copy(number).wait_send()


def decode(
    table, lens, dest, pre_in, cache, dq, dkv, new,
    pre_out, dec_out,
    pre_s, pool_s, mix_s, page_s, dq_s, out_s, in_sem, out_sem, pool_sem,
):
    half = TOK // 2

    def take(k):
        rows = pl.ds(k * half, half)
        return pltpu.make_async_copy(pre_in.at[rows, :], pre_s.at[rows, :], in_sem.at[k])

    def hand_on(k):
        rows = pl.ds(k * half, half)
        return pltpu.make_async_copy(pre_s.at[rows, :], pre_out.at[rows, :], out_sem.at[k])

    pool = pltpu.make_async_copy(cache, page_s, pool_sem)
    pool.start()
    for k in range(2):
        take(k).start()

    mix_s[pl.ds(0, NEW_ROWS, stride=2), :] = new[0].astype(F32)
    mix_s[pl.ds(1, NEW_ROWS, stride=2), :] = new[1].astype(F32)
    pool.wait()
    for m in range(TOK // PAGE):
        at = pl.ds(pl.multiple_of(dest[0, m] * 2 * PAGE, 2 * PAGE), 2 * PAGE)
        page_s[at, :] = mix_s[m * 2 * PAGE : (m + 1) * 2 * PAGE, :].astype(BF16)
    dq_s[...] = dq[...].astype(F32)
    for r in range(ROWS):
        for j in range(MAXP):
            at = pl.ds(pl.multiple_of(table[r, j] * 2 * PAGE, 2 * PAGE), 2 * PAGE)
            pool_s[r, j * 2 * PAGE : (j + 1) * 2 * PAGE, :] = page_s[at, :]

    for k in range(2):
        take(k).wait()
        hand_on(k).start()

    wide = 2 * MAXP * PAGE
    queries = HEADS * STEPS
    column = lax.broadcasted_iota(jnp.int32, (queries, wide), 1)
    query = lax.broadcasted_iota(jnp.int32, (queries, DEC), 0)
    token = lax.broadcasted_iota(jnp.int32, (queries, DEC), 1)
    so_far = (token >> 3) <= (query & (STEPS - 1))
    s_old, s_new = [], []
    for r in range(ROWS):
        q = dq_s[pl.ds(r, queries, stride=ROWS), :].astype(BF16)

        def scores(keys):
            return lax.dot_general(q, keys, (((1,), (1,)), ((), ())), preferred_element_type=F32)

        live = ((column & 1) == 0) & (column < 2 * lens[r])
        s_old.append(jnp.where(live, scores(pool_s[r]), LOW))
        s_new.append(jnp.where(so_far & ((token & (ROWS - 1)) == r), scores(dkv[0]), LOW))
    tops = [
        jnp.maximum(jnp.max(a, axis=1, keepdims=True), jnp.max(b, axis=1, keepdims=True))
        for a, b in zip(s_old, s_new)
    ]
    p_old = [jnp.exp2(a - top) for a, top in zip(s_old, tops)]
    p_new = [jnp.exp2(b - top) for b, top in zip(s_new, tops)]
    totals = [
        jnp.sum(a, axis=1, keepdims=True) + jnp.sum(b, axis=1, keepdims=True)
        for a, b in zip(p_old, p_new)
    ]
    p_old = [
        jnp.concatenate(
            [pltpu.roll(a[:, k * HD : (k + 1) * HD], 1, 1) for k in range(wide // HD)], axis=1
        ).astype(BF16)
        for a in p_old
    ]
    for r in range(ROWS):
        mixed = jnp.dot(p_old[r], pool_s[r], preferred_element_type=F32) + jnp.dot(
            p_new[r].astype(BF16), dkv[1], preferred_element_type=F32
        )
        out_s[pl.ds(r, queries, stride=ROWS), :] = mixed / totals[r]
    for h in range(HEADS):
        dec_out[:, h * HD : (h + 1) * HD] = out_s[h * DEC : (h + 1) * DEC, :].astype(BF16)
    for k in range(2):
        hand_on(k).wait()


def per_device(pre_x, w_query, w_key, w_value, dec_x, cache, lengths, page_table, dest_slots):
    hbm = pl.BlockSpec(memory_space=pltpu.MemorySpace.HBM)
    vmem = pl.BlockSpec(memory_space=pltpu.MemorySpace.VMEM)
    smem = pl.BlockSpec(memory_space=pltpu.MemorySpace.SMEM)
    pre, dq, dkv, new = pl.pallas_call(
        prefill,
        out_shape=(
            jax.ShapeDtypeStruct((TOK, HEADS * HD), BF16),
            jax.ShapeDtypeStruct((HEADS * DEC, HD), BF16),
            jax.ShapeDtypeStruct((2, DEC, HD), BF16),
            jax.ShapeDtypeStruct((2, NEW_ROWS, HD), BF16),
        ),
        in_specs=[hbm] * 5,
        out_specs=(vmem,) * 4,
        scratch_shapes=[
            pltpu.VMEM((ALL, D), BF16),
            pltpu.VMEM((D, 2 * HD), BF16),
            pltpu.VMEM((D, HEADS * HD), BF16),
            pltpu.VMEM((GROUPS, 2, TOK, HD), BF16),
            pltpu.VMEM((PAIRS, HD, 2 * TOK), BF16),
            pltpu.VMEM((PAIRS, 2 * TOK, 2 * HD), BF16),
            pltpu.VMEM((LENT, TOK, HD), BF16),
            pltpu.VMEM((TILES + LENT, TILE, HD), BF16),
            pltpu.VMEM((ALL, HEADS * HD // QN), F32),
            pltpu.VMEM((TILES + LENT, TILE, 2 * HD), F32),
            pltpu.VMEM((TILES + LENT, TILE, HD), F32),
            pltpu.VMEM((TILE, 2 * TOK), F32),
            pltpu.VMEM((TILE, 2 * TOK), F32),
            pltpu.VMEM((TILE, 2 * TOK), BF16),
            pltpu.VMEM((TILE, 2 * TOK), BF16),
            pltpu.SemaphoreType.DMA((XC,)),
            pltpu.SemaphoreType.DMA((XC,)),
            pltpu.SemaphoreType.DMA((XC,)),
            pltpu.SemaphoreType.DMA((QN * QK,)),
            pltpu.SemaphoreType.DMA,
            pltpu.SemaphoreType.DMA((7,)),
            pltpu.SemaphoreType.DMA((7,)),
            pltpu.SemaphoreType.DMA((len(SENDS),)),
            pltpu.SemaphoreType.DMA((32,)),
            pltpu.SemaphoreType.DMA((LENT,)),
            pltpu.SemaphoreType.DMA((LENT,)),
            pltpu.SemaphoreType.DMA((LENT,)),
            pltpu.SemaphoreType.DMA((LENT,)),
        ],
        compiler_params=pltpu.CompilerParams(
            collective_id=0, has_side_effects=True, vmem_limit_bytes=63 * 1024 * 1024
        ),
    )(pre_x, w_query, w_key, w_value, dec_x.reshape(DEC, D // 8))
    pre_out, dec_out = pl.pallas_call(
        decode,
        out_shape=(
            jax.ShapeDtypeStruct((TOK, HEADS * HD), BF16),
            jax.ShapeDtypeStruct((DEC, HEADS * HD), BF16),
        ),
        in_specs=[smem] * 3 + [hbm] * 2 + [vmem] * 3,
        out_specs=(hbm, vmem),
        scratch_shapes=[
            pltpu.VMEM((TOK, HEADS * HD), BF16),
            pltpu.VMEM((ROWS, 2 * MAXP * PAGE, HD), BF16),
            pltpu.VMEM((2 * NEW_ROWS, HD), F32),
            pltpu.VMEM((CACHE_ROWS, HD), BF16),
            pltpu.VMEM((HEADS * DEC, HD), F32),
            pltpu.VMEM((HEADS * DEC, HD), F32),
            pltpu.SemaphoreType.DMA((2,)),
            pltpu.SemaphoreType.DMA((2,)),
            pltpu.SemaphoreType.DMA,
        ],
        compiler_params=pltpu.CompilerParams(vmem_limit_bytes=63 * 1024 * 1024),
    )(page_table, lengths, dest_slots, pre, cache.reshape(CACHE_ROWS, HD), dq, dkv, new)
    return pre_out, dec_out.reshape(STEPS, ROWS, HEADS * HD)


def solution(mesh):
    in_specs = (
        P(("seq", "pool"), None),
        P(None, "tensor"),
        P(None, "tensor"),
        P(None, "tensor"),
        P(None, ("seq", "pool"), "tensor"),
        P(("seq", "pool"), None, None, "tensor"),
        P(("seq", "pool")),
        P(("seq", "pool"), None),
        P(("seq", "pool"), None),
    )
    out_specs = (P(("seq", "pool"), "tensor"), P(None, ("seq", "pool"), "tensor"))
    return jax.shard_map(
        per_device, mesh=mesh, in_specs=in_specs, out_specs=out_specs, check_vma=False
    )
```

```python
import functools

import jax
import jax.numpy as jnp
from jax import lax
from jax.experimental import pallas as pl
from jax.experimental.pallas import tpu as pltpu
from jax.sharding import PartitionSpec as P

MESH = pl.DeviceIdType.MESH
BF16 = jnp.bfloat16
F32 = jnp.float32

D = 8192
HD = 128
HEADS = 8
TOK = 512
GROUPS = 16
PAGE = 16
MAXP = 16
PAGES = 128
ROWS = 8
STEPS = 4
DEC = ROWS * STEPS
ALL = TOK + DEC
TILES = HEADS
TILE = TOK
CACHE_ROWS = PAGES * PAGE * 2
NEW_ROWS = 512
SCALE = HD ** (-0.5) * 1.4426950408889634
LOW = -1e30
XC = 4
QK = 2
QN = 4
LENT = 4
TAKES = (3, 3, 2, 2, 1, 1, 1, 0)
PAIRS = GROUPS // 2
CHUNK = 16
POLLS = {2: (1, 2), 3: (3, 4, 5)}
JOIN, MISSED, PART, ENDS = 2, 4, 6, 10
TURNS = {1: (6, 7, 8, 9, 10, 11), PART: (12, 13, 14, 15)}

ORDER = (
    (0, 0), (3, 0), (1, 0), (0, 3), (0, 1), (2, 0), (3, 3), (3, 1),
    (1, 3), (1, 1), (2, 3), (2, 1), (0, 2), (3, 2), (1, 2), (2, 2),
)


def sends_after(event):
    near, far = event
    sends = []
    if near == 0 and far == 0:
        sends += [(0, "A+"), (0, "A-"), (1, "A+"), (1, "A-")]
    elif far == 0 and near == 3:
        sends += [(0, "A+")]
    elif far == 0 and near == 1:
        sends += [(1, "A-")]
    if far == 0:
        sends += [(0, "B+"), (0, "B-"), (1, "B+"), (1, "B-")]
    elif far == 3:
        sends += [(0, "B+")]
    elif far == 1:
        sends += [(1, "B-")]
    return sends


def seen_from(event, direction):
    near, far = event
    step = 1 if direction[1] == "+" else -1
    if direction[0] == "A":
        return ((near - step) % 4, far)
    return (near, (far - step) % 4)


SENDS = [(event, half, way) for event in ORDER for half, way in sends_after(event)]


def prefill(
    px, wq, wk, wv, dx,
    pre_out, dq_out, dkv_out, new_out,
    x_s, wkv_s, wq_s, kv_s, kt_s, va_s, of_s, q_s, pacc, acc, m_s, sa_s, sb_s, pa_s, pb_s,
    xsem, wksem, wvsem, qsem, dsem_own, dsend, drecv, ssem, rsem, qsend, qrecv, osend, orecv,
):
    seq, tensor, pool = lax.axis_index("seq"), lax.axis_index("tensor"), lax.axis_index("pool")
    x, y, core = seq // 2, pool * 2 + seq % 2, tensor % 2
    g = seq * 2 + pool
    low = g < 8
    other = 15 - g
    last = jnp.where(low, other, g)
    pair = jnp.where(low, g, other)
    count = sum(jnp.where(pair == k, TAKES[k], 0) for k in range(8))
    partner = {"seq": 7 - seq, "pool": 1 - pool}

    def place(near, far):
        ax, ay = (x + near) % 4, (y + far) % 4
        bx, by = (x + far) % 4, (y + near) % 4
        return jnp.where(core == 0, ax, bx), jnp.where(core == 0, ay, by)

    def slot_of(near, far):
        px_, py_ = place(near, far)
        return px_ * 4 + (py_ % 2) * 2 + py_ // 2

    def device(near, far):
        px_, py_ = place(near, far)
        return {"seq": px_ * 2 + py_ % 2, "pool": py_ // 2}

    ways = {"A+": device(1, 0), "A-": device(3, 0), "B+": device(0, 1), "B-": device(0, 3)}

    def x_copy(c):
        cols = pl.ds(pl.multiple_of(c * (D // XC), D // XC), D // XC)
        return pltpu.make_async_copy(px.at[:, cols], x_s.at[pl.ds(0, TOK), cols], xsem.at[c])

    def w_copy(c, ref, at, sem):
        rows = pl.ds(pl.multiple_of(c * (D // XC), D // XC), D // XC)
        return pltpu.make_async_copy(ref.at[rows, :], wkv_s.at[rows, pl.ds(at, HD)], sem.at[c])

    def q_copy(n, k):
        rows = pl.ds(k * (D // QK), D // QK)
        cols = pl.ds(pl.multiple_of(n * (HEADS * HD // QN), HEADS * HD // QN), HEADS * HD // QN)
        return pltpu.make_async_copy(wq.at[rows, cols], wq_s.at[rows, cols], qsem.at[n * QK + k])

    my_cols = pl.ds(pl.multiple_of(tensor * (D // 8), D // 8), D // 8)
    dec_own = pltpu.make_async_copy(dx, x_s.at[pl.ds(TOK, DEC), my_cols], dsem_own)

    for c in range(XC):
        x_copy(c).start()
        w_copy(c, wk, 0, wksem).start()
        w_copy(c, wv, HD, wvsem).start()
    dec_own.start()

    barrier = pltpu.get_barrier_semaphore()
    for way in ways.values():
        pl.semaphore_signal(barrier, inc=1, device_id=way, device_id_type=MESH)
    pl.semaphore_signal(barrier, inc=1, device_id=partner, device_id_type=MESH)
    for k in range(1, 8):
        pl.semaphore_signal(
            barrier, inc=1, device_id={"tensor": (tensor + k) % 8}, device_id_type=MESH
        )
    pl.semaphore_wait(barrier, 12)

    def dec_copy(k):
        return pltpu.make_async_remote_copy(
            src_ref=dx,
            dst_ref=x_s.at[pl.ds(TOK, DEC), my_cols],
            send_sem=dsend.at[k - 1],
            recv_sem=drecv.at[k - 1],
            device_id={"tensor": (tensor + k) % 8},
            device_id_type=MESH,
        )

    def dec_arrival(k):
        cols = pl.ds(pl.multiple_of(((tensor + 8 - k) % 8) * (D // 8), D // 8), D // 8)
        return pltpu.make_async_remote_copy(
            src_ref=dx,
            dst_ref=x_s.at[pl.ds(TOK, DEC), cols],
            send_sem=dsend.at[k - 1],
            recv_sem=drecv.at[k - 1],
            device_id={"tensor": (tensor + k) % 8},
            device_id_type=MESH,
        )

    for k in range(1, 8):
        dec_copy(k).start()

    def kv_copy(number):
        event, half, way = SENDS[number]
        slot = slot_of(*event)
        near, far = seen_from(event, way)
        return pltpu.make_async_remote_copy(
            src_ref=kv_s.at[slot, half],
            dst_ref=kv_s.at[slot, half],
            send_sem=ssem.at[number],
            recv_sem=rsem.at[(near * 4 + far) * 2 + half],
            device_id=ways[way],
            device_id_type=MESH,
        )

    def pass_on(event):
        for number, (of, _, _) in enumerate(SENDS):
            if of == event:
                kv_copy(number).start()

    def arrive(event):
        near, far = event
        slot = slot_of(near, far)
        for half in range(2):
            pltpu.make_async_remote_copy(
                src_ref=kv_s.at[slot, half],
                dst_ref=kv_s.at[slot, half],
                send_sem=ssem.at[0],
                recv_sem=rsem.at[(near * 4 + far) * 2 + half],
                device_id=ways["A+"],
                device_id_type=MESH,
            ).wait_recv()
        pass_on(event)

    def lend(t):
        return pltpu.make_async_remote_copy(
            src_ref=q_s.at[t],
            dst_ref=q_s.at[TILES + t],
            send_sem=qsend.at[t],
            recv_sem=qrecv.at[t],
            device_id=partner,
            device_id_type=MESH,
        )

    def give_back(t):
        return pltpu.make_async_remote_copy(
            src_ref=of_s.at[t],
            dst_ref=pre_out.at[:, pl.ds(t * HD, HD)],
            send_sem=osend.at[t],
            recv_sem=orecv.at[t],
            device_id=partner,
            device_id_type=MESH,
        )

    def clear(j, carry):
        acc[j] = jnp.zeros((TILE, 2 * HD), F32)
        m_s[j] = jnp.full((TILE, HD), LOW, F32)
        return carry

    def fill(i, carry):
        va_s[i, :, HD:] = jnp.ones((2 * TOK, HD), BF16)
        return carry

    lax.fori_loop(0, TILES + LENT, clear, 0)
    lax.fori_loop(0, PAIRS, fill, 0)

    def kv_step(c, carry):
        x_copy(c).wait()
        w_copy(c, wk, 0, wksem).wait()
        w_copy(c, wv, HD, wvsem).wait()
        for k in range(QN * QK):

            @pl.when(c == 2 + k // 4)
            def _():
                q_copy(k // QK, k % QK).start()

        at = pl.ds(pl.multiple_of(c * (D // XC), D // XC), D // XC)
        part = jnp.dot(x_s[0:TOK, at], wkv_s[at, :], preferred_element_type=F32)

        @pl.when(c == 0)
        def _():
            pacc[0:TOK, 0:256] = part

        @pl.when(c > 0)
        def _():
            pacc[0:TOK, 0:256] += part

        return carry

    lax.fori_loop(0, XC, kv_step, 0)
    kv_s[g, 0] = pacc[0:TOK, 0:HD].astype(BF16)
    kv_s[g, 1] = pacc[0:TOK, HD : 2 * HD].astype(BF16)
    pass_on(ORDER[0])

    dec_own.wait()
    for k in range(1, 8):
        dec_arrival(k).wait_recv()

    width = HEADS * HD // QN

    def query_step(n, carry):
        for k in range(QK):
            q_copy(n, k).wait()
        part = jnp.dot(
            x_s[...],
            wq_s[:, pl.ds(pl.multiple_of(n * width, width), width)],
            preferred_element_type=F32,
        )
        for hh in range(HEADS // QN):
            h = n * (HEADS // QN) + hh
            scaled = (part[:, hh * HD : (hh + 1) * HD] * SCALE).astype(BF16)
            q_s[h] = scaled[0:TOK]
            dq_out[pl.ds(pl.multiple_of(h * DEC, DEC), DEC), :] = scaled[TOK:ALL]

        @pl.when(n == QN // 2 - 1)
        def _():
            for t in range(LENT):

                @pl.when(jnp.logical_not(low) & (t < count))
                def _():
                    lend(t).start()

        for at, events in POLLS.items():

            @pl.when(n == at)
            def _():
                for e in events:
                    arrive(ORDER[e])

        return carry

    lax.fori_loop(0, QN, query_step, 0)
    dkv = jnp.dot(x_s[TOK:ALL, :], wkv_s[...], preferred_element_type=F32)
    dkv_out[0] = dkv[:, 0:HD].astype(BF16)
    dkv_out[1] = dkv[:, HD : 2 * HD].astype(BF16)

    def prepare(slot):
        side = pl.ds(pl.multiple_of((slot % 2) * TOK, TOK), TOK)
        kt_s[slot // 2, :, side] = kv_s[slot, 0].T
        va_s[slot // 2, side, 0:HD] = kv_s[slot, 1]

    def part_of(item):
        j, block, whole = item
        if whole:
            return j, block, slice(0, 2 * TOK), 2 * TOK
        return j, block // 2, pl.ds(pl.multiple_of((block % 2) * TOK, TOK), TOK), TOK

    def score(item, buf):
        j, two, side, width = part_of(item)
        buf[:, 0:width] = jnp.dot(q_s[j], kt_s[two, :, side], preferred_element_type=F32)

    def absorb(item, buf, weights, ahead):
        j, two, side, width = part_of(item)
        if ahead is not None:
            lead = lax.broadcasted_iota(jnp.int32, (CHUNK, HD), 1) - lax.broadcasted_iota(
                jnp.int32, (CHUNK, HD), 0
            )
        for c in range(TILE // CHUNK):
            rows = slice(c * CHUNK, (c + 1) * CHUNK)
            cuts = [buf[rows, k * HD : (k + 1) * HD] for k in range(width // HD)]
            if ahead is not None:
                cuts = [
                    jnp.where(lead <= c * CHUNK - k * HD + ahead, cut, LOW)
                    for k, cut in enumerate(cuts)
                ]
            if isinstance(ahead, int):
                clear_from = (ahead + (c + 1) * CHUNK - 1) // HD + 1
                for k in range(clear_from, len(cuts)):
                    weights[rows, k * HD : (k + 1) * HD] = jnp.zeros((CHUNK, HD), BF16)
                cuts = cuts[:clear_from]
            old = m_s[j, rows, :]
            best = functools.reduce(jnp.maximum, cuts)
            top = jnp.maximum(
                old, jnp.broadcast_to(jnp.max(best, axis=1, keepdims=True), (CHUNK, HD))
            )
            for k, cut in enumerate(cuts):
                weights[rows, k * HD : (k + 1) * HD] = jnp.exp2(cut - top).astype(BF16)
            shrink = jnp.exp2(old - top)
            m_s[j, rows, :] = top
            acc[j, rows, 0:HD] = acc[j, rows, 0:HD] * shrink
            acc[j, rows, HD:] = acc[j, rows, HD:] * shrink
        acc[j] += jnp.dot(weights[:, 0:width], va_s[two, side, :], preferred_element_type=F32)

    def run(n, item, ahead=None):
        @pl.when(n > 0)
        def _():
            score(item(0), sa_s)

        def two(t, carry):
            score(item(2 * t + 1), sb_s)
            absorb(item(2 * t), sa_s, pa_s, ahead)

            @pl.when(2 * t + 2 < n)
            def _():
                score(item(2 * t + 2), sa_s)

            absorb(item(2 * t + 1), sb_s, pb_s, ahead)
            return carry

        lax.fori_loop(0, n // 2, two, 0)

        @pl.when(n % 2 == 1)
        def _():
            absorb(item(n - 1), sa_s, pa_s, ahead)

    first = jnp.where(low, 0, count)
    own = TILES - first
    taken = jnp.where(low, count, 0)

    prepare(g)
    run(own, lambda t: (first + t, g, False), 0)

    def finish(j):
        return (acc[j, :, 0:HD] / acc[j, :, HD:]).astype(BF16)

    def pair_at(i):
        half = i // 4
        step = jnp.where(core == 0, i % 4, i // 2)
        across = jnp.where(core == 0, 1 - half, 1 - i % 2)
        near = jnp.where(step == 0, 0, jnp.where(step == 1, 3, step - 1))
        return ((x + near) % 4) * 2 + (y + across) % 2

    def prepare_pair(i):
        for side in range(2):
            slot = 2 * pair_at(i) + side

            @pl.when(slot <= last)
            def _():
                prepare(slot)

    due = range(PAIRS // 2, PAIRS)
    wanted = [jnp.where(pair_at(i) < last // 2, 1, 0) for i in due]
    before = [sum(wanted[:k], jnp.int32(0)) for k in range(len(due))]

    def due_at(t):
        return sum(
            jnp.where((wanted[k] == 1) & (before[k] == t), pair_at(due[k]), 0)
            for k in range(len(due))
        )

    def turn(s, carry):
        for at, events in TURNS.items():

            @pl.when(s == at)
            def _():
                for e in events:
                    arrive(ORDER[e])

        i = jnp.where(s < MISSED, s, jnp.where(s < PART, s - MISSED, s - PART + PAIRS // 2))

        @pl.when(s < MISSED)
        def _():
            prepare_pair(i)

        @pl.when(s == JOIN)
        def _():
            for t in range(LENT):

                @pl.when(low & (t < count))
                def _():
                    lend(t).wait_recv()

        @pl.when((s == MISSED) & (taken > 0))
        def _():
            def single(k, carry):
                block = last - k
                prepare(block)
                run(taken, lambda t: (TILES + t, block, False), k * TOK)
                return carry

            lax.fori_loop(0, 1 + last % 2, single, 0)

        @pl.when(s == PART)
        def _():
            def rest(k, carry):
                prepare_pair(k)
                return carry

            lax.fori_loop(PAIRS // 2, PAIRS, rest, 0)

            def away(j, carry):
                run(before[-1] + wanted[-1], lambda t: (j, due_at(t), True))
                of_s[j - TILES] = finish(j)
                for f in range(LENT):

                    @pl.when(j == TILES + f)
                    def _():
                        give_back(f).start()

                return carry

            lax.fori_loop(TILES, TILES + taken, away, 0)
            run(own * (g % 2), lambda t: (first + t, g - 1, False))

        two = pair_at(i)
        join = (s >= JOIN) & (s < PART) & (two < last // 2)
        start = jnp.where((two < g // 2) & ((s < MISSED) | (s >= PART)), first, TILES)
        stop = jnp.where(join, TILES + taken, TILES)
        run(jnp.maximum(stop - start, 0), lambda t: (start + t, two, True))
        return carry

    lax.fori_loop(0, ENDS, turn, 0)

    for j in range(TILES):

        @pl.when(j >= first)
        def _():
            pre_out[:, j * HD : (j + 1) * HD] = finish(j)

    mine = NEW_ROWS // GROUPS
    at = pl.ds(pl.multiple_of(g * mine, mine), mine)
    for src in range(GROUPS):
        for half in range(2):
            new_out[half, src * mine : (src + 1) * mine, :] = kv_s[src, half, at, :]

    for t in range(LENT):

        @pl.when((t < count) & low)
        def _():
            give_back(t).wait_send()

        @pl.when((t < count) & jnp.logical_not(low))
        def _():
            lend(t).wait_send()
            give_back(t).wait_recv()

    for k in range(1, 8):
        dec_copy(k).wait_send()
    for number in range(len(SENDS)):
        kv_copy(number).wait_send()


def decode(
    table, lens, dest, pre_in, cache, dq, dkv, new,
    pre_out, dec_out,
    pre_s, pool_s, mix_s, page_s, dq_s, out_s, in_sem, out_sem, pool_sem,
):
    half = TOK // 2

    def take(k):
        rows = pl.ds(k * half, half)
        return pltpu.make_async_copy(pre_in.at[rows, :], pre_s.at[rows, :], in_sem.at[k])

    def hand_on(k):
        rows = pl.ds(k * half, half)
        return pltpu.make_async_copy(pre_s.at[rows, :], pre_out.at[rows, :], out_sem.at[k])

    pool = pltpu.make_async_copy(cache, page_s, pool_sem)
    pool.start()
    for k in range(2):
        take(k).start()

    mix_s[pl.ds(0, NEW_ROWS, stride=2), :] = new[0].astype(F32)
    mix_s[pl.ds(1, NEW_ROWS, stride=2), :] = new[1].astype(F32)
    pool.wait()
    for m in range(TOK // PAGE):
        at = pl.ds(pl.multiple_of(dest[0, m] * 2 * PAGE, 2 * PAGE), 2 * PAGE)
        page_s[at, :] = mix_s[m * 2 * PAGE : (m + 1) * 2 * PAGE, :].astype(BF16)
    dq_s[...] = dq[...].astype(F32)
    for r in range(ROWS):
        for j in range(MAXP):
            at = pl.ds(pl.multiple_of(table[r, j] * 2 * PAGE, 2 * PAGE), 2 * PAGE)
            pool_s[r, j * 2 * PAGE : (j + 1) * 2 * PAGE, :] = page_s[at, :]

    for k in range(2):
        take(k).wait()
        hand_on(k).start()

    wide = 2 * MAXP * PAGE
    queries = HEADS * STEPS
    column = lax.broadcasted_iota(jnp.int32, (queries, wide), 1)
    query = lax.broadcasted_iota(jnp.int32, (queries, DEC), 0)
    token = lax.broadcasted_iota(jnp.int32, (queries, DEC), 1)
    so_far = (token >> 3) <= (query & (STEPS - 1))
    s_old, s_new = [], []
    for r in range(ROWS):
        q = dq_s[pl.ds(r, queries, stride=ROWS), :].astype(BF16)

        def scores(keys):
            return lax.dot_general(q, keys, (((1,), (1,)), ((), ())), preferred_element_type=F32)

        live = ((column & 1) == 0) & (column < 2 * lens[r])
        s_old.append(jnp.where(live, scores(pool_s[r]), LOW))
        s_new.append(jnp.where(so_far & ((token & (ROWS - 1)) == r), scores(dkv[0]), LOW))
    tops = [
        jnp.maximum(jnp.max(a, axis=1, keepdims=True), jnp.max(b, axis=1, keepdims=True))
        for a, b in zip(s_old, s_new)
    ]
    p_old = [jnp.exp2(a - top) for a, top in zip(s_old, tops)]
    p_new = [jnp.exp2(b - top) for b, top in zip(s_new, tops)]
    totals = [
        jnp.sum(a, axis=1, keepdims=True) + jnp.sum(b, axis=1, keepdims=True)
        for a, b in zip(p_old, p_new)
    ]
    p_old = [
        jnp.concatenate(
            [pltpu.roll(a[:, k * HD : (k + 1) * HD], 1, 1) for k in range(wide // HD)], axis=1
        ).astype(BF16)
        for a in p_old
    ]
    for r in range(ROWS):
        mixed = jnp.dot(p_old[r], pool_s[r], preferred_element_type=F32) + jnp.dot(
            p_new[r].astype(BF16), dkv[1], preferred_element_type=F32
        )
        out_s[pl.ds(r, queries, stride=ROWS), :] = mixed / totals[r]
    for h in range(HEADS):
        dec_out[:, h * HD : (h + 1) * HD] = out_s[h * DEC : (h + 1) * DEC, :].astype(BF16)
    for k in range(2):
        hand_on(k).wait()


def per_device(pre_x, w_query, w_key, w_value, dec_x, cache, lengths, page_table, dest_slots):
    hbm = pl.BlockSpec(memory_space=pltpu.MemorySpace.HBM)
    vmem = pl.BlockSpec(memory_space=pltpu.MemorySpace.VMEM)
    smem = pl.BlockSpec(memory_space=pltpu.MemorySpace.SMEM)
    pre, dq, dkv, new = pl.pallas_call(
        prefill,
        out_shape=(
            jax.ShapeDtypeStruct((TOK, HEADS * HD), BF16),
            jax.ShapeDtypeStruct((HEADS * DEC, HD), BF16),
            jax.ShapeDtypeStruct((2, DEC, HD), BF16),
            jax.ShapeDtypeStruct((2, NEW_ROWS, HD), BF16),
        ),
        in_specs=[hbm] * 5,
        out_specs=(vmem,) * 4,
        scratch_shapes=[
            pltpu.VMEM((ALL, D), BF16),
            pltpu.VMEM((D, 2 * HD), BF16),
            pltpu.VMEM((D, HEADS * HD), BF16),
            pltpu.VMEM((GROUPS, 2, TOK, HD), BF16),
            pltpu.VMEM((PAIRS, HD, 2 * TOK), BF16),
            pltpu.VMEM((PAIRS, 2 * TOK, 2 * HD), BF16),
            pltpu.VMEM((LENT, TOK, HD), BF16),
            pltpu.VMEM((TILES + LENT, TILE, HD), BF16),
            pltpu.VMEM((TOK, 2 * HD), F32),
            pltpu.VMEM((TILES + LENT, TILE, 2 * HD), F32),
            pltpu.VMEM((TILES + LENT, TILE, HD), F32),
            pltpu.VMEM((TILE, 2 * TOK), F32),
            pltpu.VMEM((TILE, 2 * TOK), F32),
            pltpu.VMEM((TILE, 2 * TOK), BF16),
            pltpu.VMEM((TILE, 2 * TOK), BF16),
            pltpu.SemaphoreType.DMA((XC,)),
            pltpu.SemaphoreType.DMA((XC,)),
            pltpu.SemaphoreType.DMA((XC,)),
            pltpu.SemaphoreType.DMA((QN * QK,)),
            pltpu.SemaphoreType.DMA,
            pltpu.SemaphoreType.DMA((7,)),
            pltpu.SemaphoreType.DMA((7,)),
            pltpu.SemaphoreType.DMA((len(SENDS),)),
            pltpu.SemaphoreType.DMA((32,)),
            pltpu.SemaphoreType.DMA((LENT,)),
            pltpu.SemaphoreType.DMA((LENT,)),
            pltpu.SemaphoreType.DMA((LENT,)),
            pltpu.SemaphoreType.DMA((LENT,)),
        ],
        compiler_params=pltpu.CompilerParams(
            collective_id=0, has_side_effects=True, vmem_limit_bytes=63 * 1024 * 1024
        ),
    )(pre_x, w_query, w_key, w_value, dec_x.reshape(DEC, D // 8))
    pre_out, dec_out = pl.pallas_call(
        decode,
        out_shape=(
            jax.ShapeDtypeStruct((TOK, HEADS * HD), BF16),
            jax.ShapeDtypeStruct((DEC, HEADS * HD), BF16),
        ),
        in_specs=[smem] * 3 + [hbm] * 2 + [vmem] * 3,
        out_specs=(hbm, vmem),
        scratch_shapes=[
            pltpu.VMEM((TOK, HEADS * HD), BF16),
            pltpu.VMEM((ROWS, 2 * MAXP * PAGE, HD), BF16),
            pltpu.VMEM((2 * NEW_ROWS, HD), F32),
            pltpu.VMEM((CACHE_ROWS, HD), BF16),
            pltpu.VMEM((HEADS * DEC, HD), F32),
            pltpu.VMEM((HEADS * DEC, HD), F32),
            pltpu.SemaphoreType.DMA((2,)),
            pltpu.SemaphoreType.DMA((2,)),
            pltpu.SemaphoreType.DMA,
        ],
        compiler_params=pltpu.CompilerParams(vmem_limit_bytes=63 * 1024 * 1024),
    )(page_table, lengths, dest_slots, pre, cache.reshape(CACHE_ROWS, HD), dq, dkv, new)
    return pre_out, dec_out.reshape(STEPS, ROWS, HEADS * HD)


def solution(mesh):
    in_specs = (
        P(("seq", "pool"), None),
        P(None, "tensor"),
        P(None, "tensor"),
        P(None, "tensor"),
        P(None, ("seq", "pool"), "tensor"),
        P(("seq", "pool"), None, None, "tensor"),
        P(("seq", "pool")),
        P(("seq", "pool"), None),
        P(("seq", "pool"), None),
    )
    out_specs = (P(("seq", "pool"), "tensor"), P(None, ("seq", "pool"), "tensor"))
    return jax.shard_map(
        per_device, mesh=mesh, in_specs=in_specs, out_specs=out_specs, check_vma=False
    )
```

```python
import functools

import jax
import jax.numpy as jnp
from jax import lax
from jax.experimental import pallas as pl
from jax.experimental.pallas import tpu as pltpu
from jax.sharding import PartitionSpec as P

MESH = pl.DeviceIdType.MESH
BF16 = jnp.bfloat16
F32 = jnp.float32

D = 8192
HD = 128
HEADS = 8
TOK = 512
GROUPS = 16
PAGE = 16
MAXP = 16
PAGES = 128
ROWS = 8
STEPS = 4
DEC = ROWS * STEPS
ALL = TOK + DEC
TILES = HEADS
TILE = TOK
CACHE_ROWS = PAGES * PAGE * 2
NEW_ROWS = 512
SCALE = HD ** (-0.5) * 1.4426950408889634
LOW = -1e30
XC = 4
QK = 2
QN = 4
LENT = 4
TAKES = (3, 3, 3, 2, 2, 1, 1, 0)
PAIRS = GROUPS // 2
CHUNK = 16
POLLS = {2: (1, 2), 3: (3, 4, 5)}
JOIN, MISSED, PART, ENDS = 2, 4, 6, 10
TURNS = {1: (6, 7, 8, 9, 10, 11), PART: (12, 13, 14, 15)}

ORDER = (
    (0, 0), (3, 0), (1, 0), (0, 3), (0, 1), (2, 0), (3, 3), (3, 1),
    (1, 3), (1, 1), (2, 3), (2, 1), (0, 2), (3, 2), (1, 2), (2, 2),
)


def sends_after(event):
    near, far = event
    sends = []
    if near == 0 and far == 0:
        sends += [(0, "A+"), (0, "A-"), (1, "A+"), (1, "A-")]
    elif far == 0 and near == 3:
        sends += [(0, "A+")]
    elif far == 0 and near == 1:
        sends += [(1, "A-")]
    if far == 0:
        sends += [(0, "B+"), (0, "B-"), (1, "B+"), (1, "B-")]
    elif far == 3:
        sends += [(0, "B+")]
    elif far == 1:
        sends += [(1, "B-")]
    return sends


def seen_from(event, direction):
    near, far = event
    step = 1 if direction[1] == "+" else -1
    if direction[0] == "A":
        return ((near - step) % 4, far)
    return (near, (far - step) % 4)


SENDS = [(event, half, way) for event in ORDER for half, way in sends_after(event)]


def prefill(
    px, wq, wk, wv, dx,
    pre_out, dq_out, dkv_out, new_out,
    x_s, wkv_s, wq_s, kv_s, kt_s, va_s, of_s, q_s, pacc, acc, m_s, sa_s, sb_s, pa_s, pb_s,
    xsem, wksem, wvsem, qsem, dsem_own, dsend, drecv, ssem, rsem, qsend, qrecv, osend, orecv,
):
    seq, tensor, pool = lax.axis_index("seq"), lax.axis_index("tensor"), lax.axis_index("pool")
    x, y, core = seq // 2, pool * 2 + seq % 2, tensor % 2
    g = seq * 2 + pool
    low = g < 8
    other = 15 - g
    last = jnp.where(low, other, g)
    pair = jnp.where(low, g, other)
    count = sum(jnp.where(pair == k, TAKES[k], 0) for k in range(8))
    partner = {"seq": 7 - seq, "pool": 1 - pool}

    def place(near, far):
        ax, ay = (x + near) % 4, (y + far) % 4
        bx, by = (x + far) % 4, (y + near) % 4
        return jnp.where(core == 0, ax, bx), jnp.where(core == 0, ay, by)

    def slot_of(near, far):
        px_, py_ = place(near, far)
        return px_ * 4 + (py_ % 2) * 2 + py_ // 2

    def device(near, far):
        px_, py_ = place(near, far)
        return {"seq": px_ * 2 + py_ % 2, "pool": py_ // 2}

    ways = {"A+": device(1, 0), "A-": device(3, 0), "B+": device(0, 1), "B-": device(0, 3)}

    def x_copy(c):
        cols = pl.ds(pl.multiple_of(c * (D // XC), D // XC), D // XC)
        return pltpu.make_async_copy(px.at[:, cols], x_s.at[pl.ds(0, TOK), cols], xsem.at[c])

    def w_copy(c, ref, at, sem):
        rows = pl.ds(pl.multiple_of(c * (D // XC), D // XC), D // XC)
        return pltpu.make_async_copy(ref.at[rows, :], wkv_s.at[rows, pl.ds(at, HD)], sem.at[c])

    def q_copy(n, k):
        rows = pl.ds(k * (D // QK), D // QK)
        cols = pl.ds(pl.multiple_of(n * (HEADS * HD // QN), HEADS * HD // QN), HEADS * HD // QN)
        return pltpu.make_async_copy(wq.at[rows, cols], wq_s.at[rows, cols], qsem.at[n * QK + k])

    my_cols = pl.ds(pl.multiple_of(tensor * (D // 8), D // 8), D // 8)
    dec_own = pltpu.make_async_copy(dx, x_s.at[pl.ds(TOK, DEC), my_cols], dsem_own)

    for c in range(XC):
        x_copy(c).start()
        w_copy(c, wk, 0, wksem).start()
        w_copy(c, wv, HD, wvsem).start()
    dec_own.start()

    barrier = pltpu.get_barrier_semaphore()
    for way in ways.values():
        pl.semaphore_signal(barrier, inc=1, device_id=way, device_id_type=MESH)
    pl.semaphore_signal(barrier, inc=1, device_id=partner, device_id_type=MESH)
    for k in range(1, 8):
        pl.semaphore_signal(
            barrier, inc=1, device_id={"tensor": (tensor + k) % 8}, device_id_type=MESH
        )
    pl.semaphore_wait(barrier, 12)

    def dec_copy(k):
        return pltpu.make_async_remote_copy(
            src_ref=dx,
            dst_ref=x_s.at[pl.ds(TOK, DEC), my_cols],
            send_sem=dsend.at[k - 1],
            recv_sem=drecv.at[k - 1],
            device_id={"tensor": (tensor + k) % 8},
            device_id_type=MESH,
        )

    def dec_arrival(k):
        cols = pl.ds(pl.multiple_of(((tensor + 8 - k) % 8) * (D // 8), D // 8), D // 8)
        return pltpu.make_async_remote_copy(
            src_ref=dx,
            dst_ref=x_s.at[pl.ds(TOK, DEC), cols],
            send_sem=dsend.at[k - 1],
            recv_sem=drecv.at[k - 1],
            device_id={"tensor": (tensor + k) % 8},
            device_id_type=MESH,
        )

    for k in range(1, 8):
        dec_copy(k).start()

    def kv_copy(number):
        event, half, way = SENDS[number]
        slot = slot_of(*event)
        near, far = seen_from(event, way)
        return pltpu.make_async_remote_copy(
            src_ref=kv_s.at[slot, half],
            dst_ref=kv_s.at[slot, half],
            send_sem=ssem.at[number],
            recv_sem=rsem.at[(near * 4 + far) * 2 + half],
            device_id=ways[way],
            device_id_type=MESH,
        )

    def pass_on(event):
        for number, (of, _, _) in enumerate(SENDS):
            if of == event:
                kv_copy(number).start()

    def arrive(event):
        near, far = event
        slot = slot_of(near, far)
        for half in range(2):
            pltpu.make_async_remote_copy(
                src_ref=kv_s.at[slot, half],
                dst_ref=kv_s.at[slot, half],
                send_sem=ssem.at[0],
                recv_sem=rsem.at[(near * 4 + far) * 2 + half],
                device_id=ways["A+"],
                device_id_type=MESH,
            ).wait_recv()
        pass_on(event)

    def lend(t):
        return pltpu.make_async_remote_copy(
            src_ref=q_s.at[t],
            dst_ref=q_s.at[TILES + t],
            send_sem=qsend.at[t],
            recv_sem=qrecv.at[t],
            device_id=partner,
            device_id_type=MESH,
        )

    def give_back(t):
        return pltpu.make_async_remote_copy(
            src_ref=of_s.at[t],
            dst_ref=pre_out.at[:, pl.ds(t * HD, HD)],
            send_sem=osend.at[t],
            recv_sem=orecv.at[t],
            device_id=partner,
            device_id_type=MESH,
        )

    def clear(j, carry):
        acc[j] = jnp.zeros((TILE, 2 * HD), F32)
        m_s[j] = jnp.full((TILE, HD), LOW, F32)
        return carry

    def fill(i, carry):
        va_s[i, :, HD:] = jnp.ones((2 * TOK, HD), BF16)
        return carry

    lax.fori_loop(0, TILES + LENT, clear, 0)
    lax.fori_loop(0, PAIRS, fill, 0)

    def kv_step(c, carry):
        x_copy(c).wait()
        w_copy(c, wk, 0, wksem).wait()
        w_copy(c, wv, HD, wvsem).wait()
        for k in range(QN * QK):

            @pl.when(c == 2 + k // 4)
            def _():
                q_copy(k // QK, k % QK).start()

        at = pl.ds(pl.multiple_of(c * (D // XC), D // XC), D // XC)
        part = jnp.dot(x_s[0:TOK, at], wkv_s[at, :], preferred_element_type=F32)

        @pl.when(c == 0)
        def _():
            pacc[0:TOK, 0:256] = part

        @pl.when(c > 0)
        def _():
            pacc[0:TOK, 0:256] += part

        return carry

    lax.fori_loop(0, XC, kv_step, 0)
    kv_s[g, 0] = pacc[0:TOK, 0:HD].astype(BF16)
    kv_s[g, 1] = pacc[0:TOK, HD : 2 * HD].astype(BF16)
    pass_on(ORDER[0])

    dec_own.wait()
    for k in range(1, 8):
        dec_arrival(k).wait_recv()

    width = HEADS * HD // QN

    def query_step(n, carry):
        for k in range(QK):
            q_copy(n, k).wait()
        part = jnp.dot(
            x_s[...],
            wq_s[:, pl.ds(pl.multiple_of(n * width, width), width)],
            preferred_element_type=F32,
        )
        for hh in range(HEADS // QN):
            h = n * (HEADS // QN) + hh
            scaled = (part[:, hh * HD : (hh + 1) * HD] * SCALE).astype(BF16)
            q_s[h] = scaled[0:TOK]
            dq_out[pl.ds(pl.multiple_of(h * DEC, DEC), DEC), :] = scaled[TOK:ALL]

        @pl.when(n == QN // 2 - 1)
        def _():
            for t in range(LENT):

                @pl.when(jnp.logical_not(low) & (t < count))
                def _():
                    lend(t).start()

        for at, events in POLLS.items():

            @pl.when(n == at)
            def _():
                for e in events:
                    arrive(ORDER[e])

        return carry

    lax.fori_loop(0, QN, query_step, 0)
    dkv = jnp.dot(x_s[TOK:ALL, :], wkv_s[...], preferred_element_type=F32)
    dkv_out[0] = dkv[:, 0:HD].astype(BF16)
    dkv_out[1] = dkv[:, HD : 2 * HD].astype(BF16)

    def prepare(slot):
        side = pl.ds(pl.multiple_of((slot % 2) * TOK, TOK), TOK)
        kt_s[slot // 2, :, side] = kv_s[slot, 0].T
        va_s[slot // 2, side, 0:HD] = kv_s[slot, 1]

    def part_of(item):
        j, block, whole = item
        if whole:
            return j, block, slice(0, 2 * TOK), 2 * TOK
        return j, block // 2, pl.ds(pl.multiple_of((block % 2) * TOK, TOK), TOK), TOK

    def score(item, buf):
        j, two, side, width = part_of(item)
        at = 0 if width == 2 * TOK else pl.multiple_of((item[1] % 2) * TOK, TOK)

        def step(n):
            keys = kt_s[two, :, pl.ds(at + n * 2 * HD, 2 * HD)]
            buf[:, n * 2 * HD : (n + 1) * 2 * HD] = jnp.dot(
                q_s[j], keys, preferred_element_type=F32
            )

        return [functools.partial(step, n) for n in range(width // (2 * HD))]

    def absorb(item, buf, weights, ahead, beside=()):
        j, two, side, width = part_of(item)
        if ahead is not None:
            lead = lax.broadcasted_iota(jnp.int32, (CHUNK, HD), 1) - lax.broadcasted_iota(
                jnp.int32, (CHUNK, HD), 0
            )
        for c in range(TILE // CHUNK):
            if beside and c % (TILE // CHUNK // len(beside)) == 0:
                beside[c // (TILE // CHUNK // len(beside))]()
            rows = slice(c * CHUNK, (c + 1) * CHUNK)
            cuts = [buf[rows, k * HD : (k + 1) * HD] for k in range(width // HD)]
            if ahead is not None:
                cuts = [
                    jnp.where(lead <= c * CHUNK - k * HD + ahead, cut, LOW)
                    for k, cut in enumerate(cuts)
                ]
            if isinstance(ahead, int):
                clear_from = (ahead + (c + 1) * CHUNK - 1) // HD + 1
                for k in range(clear_from, len(cuts)):
                    weights[rows, k * HD : (k + 1) * HD] = jnp.zeros((CHUNK, HD), BF16)
                cuts = cuts[:clear_from]
            old = m_s[j, rows, :]
            best = functools.reduce(jnp.maximum, cuts)
            top = jnp.maximum(
                old, jnp.broadcast_to(jnp.max(best, axis=1, keepdims=True), (CHUNK, HD))
            )
            for k, cut in enumerate(cuts):
                weights[rows, k * HD : (k + 1) * HD] = jnp.exp2(cut - top).astype(BF16)
            shrink = jnp.exp2(old - top)
            m_s[j, rows, :] = top
            acc[j, rows, 0:HD] = acc[j, rows, 0:HD] * shrink
            acc[j, rows, HD:] = acc[j, rows, HD:] * shrink
        acc[j] += jnp.dot(weights[:, 0:width], va_s[two, side, :], preferred_element_type=F32)

    def run(n, item, ahead=None):
        @pl.when(n > 0)
        def _():
            for step in score(item(0), sa_s):
                step()

        def two(t, carry):
            now, later, last_one = item(2 * t), item(2 * t + 1), item(jnp.minimum(2 * t + 2, n - 1))
            absorb(now, sa_s, pa_s, ahead, score(later, sb_s))
            absorb(later, sb_s, pb_s, ahead, score(last_one, sa_s))
            return carry

        lax.fori_loop(0, n // 2, two, 0)

        @pl.when(n % 2 == 1)
        def _():
            absorb(item(n - 1), sa_s, pa_s, ahead)

    first = jnp.where(low, 0, count)
    own = TILES - first
    taken = jnp.where(low, count, 0)

    prepare(g)
    run(own, lambda t: (first + t, g, False), 0)

    def finish(j):
        return (acc[j, :, 0:HD] / acc[j, :, HD:]).astype(BF16)

    def pair_at(i):
        half = i // 4
        step = jnp.where(core == 0, i % 4, i // 2)
        across = jnp.where(core == 0, 1 - half, 1 - i % 2)
        near = jnp.where(step == 0, 0, jnp.where(step == 1, 3, step - 1))
        return ((x + near) % 4) * 2 + (y + across) % 2

    def prepare_pair(i):
        for side in range(2):
            slot = 2 * pair_at(i) + side

            @pl.when(slot <= last)
            def _():
                prepare(slot)

    due = range(PAIRS // 2, PAIRS)
    wanted = [jnp.where(pair_at(i) < last // 2, 1, 0) for i in due]
    before = [sum(wanted[:k], jnp.int32(0)) for k in range(len(due))]

    def due_at(t):
        return sum(
            jnp.where((wanted[k] == 1) & (before[k] == t), pair_at(due[k]), 0)
            for k in range(len(due))
        )

    def turn(s, carry):
        for at, events in TURNS.items():

            @pl.when(s == at)
            def _():
                for e in events:
                    arrive(ORDER[e])

        i = jnp.where(s < MISSED, s, jnp.where(s < PART, s - MISSED, s - PART + PAIRS // 2))

        @pl.when(s < MISSED)
        def _():
            prepare_pair(i)

        @pl.when(s == JOIN)
        def _():
            for t in range(LENT):

                @pl.when(low & (t < count))
                def _():
                    lend(t).wait_recv()

        @pl.when((s == MISSED) & (taken > 0))
        def _():
            def single(k, carry):
                block = last - k
                prepare(block)
                run(taken, lambda t: (TILES + t, block, False), k * TOK)
                return carry

            lax.fori_loop(0, 1 + last % 2, single, 0)

        @pl.when(s == PART)
        def _():
            def rest(k, carry):
                prepare_pair(k)
                return carry

            lax.fori_loop(PAIRS // 2, PAIRS, rest, 0)

            def away(j, carry):
                run(before[-1] + wanted[-1], lambda t: (j, due_at(t), True))
                of_s[j - TILES] = finish(j)
                for f in range(LENT):

                    @pl.when(j == TILES + f)
                    def _():
                        give_back(f).start()

                return carry

            lax.fori_loop(TILES, TILES + taken, away, 0)
            run(own * (g % 2), lambda t: (first + t, g - 1, False))

        two = pair_at(i)
        join = (s >= JOIN) & (s < PART) & (two < last // 2)
        start = jnp.where((two < g // 2) & ((s < MISSED) | (s >= PART)), first, TILES)
        stop = jnp.where(join, TILES + taken, TILES)
        run(jnp.maximum(stop - start, 0), lambda t: (start + t, two, True))
        return carry

    lax.fori_loop(0, ENDS, turn, 0)

    for j in range(TILES):

        @pl.when(j >= first)
        def _():
            pre_out[:, j * HD : (j + 1) * HD] = finish(j)

    mine = NEW_ROWS // GROUPS
    at = pl.ds(pl.multiple_of(g * mine, mine), mine)
    for src in range(GROUPS):
        for half in range(2):
            new_out[half, src * mine : (src + 1) * mine, :] = kv_s[src, half, at, :]

    for t in range(LENT):

        @pl.when((t < count) & low)
        def _():
            give_back(t).wait_send()

        @pl.when((t < count) & jnp.logical_not(low))
        def _():
            lend(t).wait_send()
            give_back(t).wait_recv()

    for k in range(1, 8):
        dec_copy(k).wait_send()
    for number in range(len(SENDS)):
        kv_copy(number).wait_send()


def decode(
    table, lens, dest, pre_in, cache, dq, dkv, new,
    pre_out, dec_out,
    pre_s, pool_s, mix_s, page_s, dq_s, out_s, in_sem, out_sem, pool_sem,
):
    half = TOK // 2

    def take(k):
        rows = pl.ds(k * half, half)
        return pltpu.make_async_copy(pre_in.at[rows, :], pre_s.at[rows, :], in_sem.at[k])

    def hand_on(k):
        rows = pl.ds(k * half, half)
        return pltpu.make_async_copy(pre_s.at[rows, :], pre_out.at[rows, :], out_sem.at[k])

    pool = pltpu.make_async_copy(cache, page_s, pool_sem)
    pool.start()
    for k in range(2):
        take(k).start()

    mix_s[pl.ds(0, NEW_ROWS, stride=2), :] = new[0].astype(F32)
    mix_s[pl.ds(1, NEW_ROWS, stride=2), :] = new[1].astype(F32)
    pool.wait()
    for m in range(TOK // PAGE):
        at = pl.ds(pl.multiple_of(dest[0, m] * 2 * PAGE, 2 * PAGE), 2 * PAGE)
        page_s[at, :] = mix_s[m * 2 * PAGE : (m + 1) * 2 * PAGE, :].astype(BF16)
    dq_s[...] = dq[...].astype(F32)
    for r in range(ROWS):
        for j in range(MAXP):
            at = pl.ds(pl.multiple_of(table[r, j] * 2 * PAGE, 2 * PAGE), 2 * PAGE)
            pool_s[r, j * 2 * PAGE : (j + 1) * 2 * PAGE, :] = page_s[at, :]

    for k in range(2):
        take(k).wait()
        hand_on(k).start()

    wide = 2 * MAXP * PAGE
    queries = HEADS * STEPS
    column = lax.broadcasted_iota(jnp.int32, (queries, wide), 1)
    query = lax.broadcasted_iota(jnp.int32, (queries, DEC), 0)
    token = lax.broadcasted_iota(jnp.int32, (queries, DEC), 1)
    so_far = (token >> 3) <= (query & (STEPS - 1))
    s_old, s_new = [], []
    for r in range(ROWS):
        q = dq_s[pl.ds(r, queries, stride=ROWS), :].astype(BF16)

        def scores(keys):
            return lax.dot_general(q, keys, (((1,), (1,)), ((), ())), preferred_element_type=F32)

        live = ((column & 1) == 0) & (column < 2 * lens[r])
        s_old.append(jnp.where(live, scores(pool_s[r]), LOW))
        s_new.append(jnp.where(so_far & ((token & (ROWS - 1)) == r), scores(dkv[0]), LOW))
    tops = [
        jnp.maximum(jnp.max(a, axis=1, keepdims=True), jnp.max(b, axis=1, keepdims=True))
        for a, b in zip(s_old, s_new)
    ]
    p_old = [jnp.exp2(a - top) for a, top in zip(s_old, tops)]
    p_new = [jnp.exp2(b - top) for b, top in zip(s_new, tops)]
    totals = [
        jnp.sum(a, axis=1, keepdims=True) + jnp.sum(b, axis=1, keepdims=True)
        for a, b in zip(p_old, p_new)
    ]
    p_old = [
        jnp.concatenate(
            [pltpu.roll(a[:, k * HD : (k + 1) * HD], 1, 1) for k in range(wide // HD)], axis=1
        ).astype(BF16)
        for a in p_old
    ]
    for r in range(ROWS):
        mixed = jnp.dot(p_old[r], pool_s[r], preferred_element_type=F32) + jnp.dot(
            p_new[r].astype(BF16), dkv[1], preferred_element_type=F32
        )
        out_s[pl.ds(r, queries, stride=ROWS), :] = mixed / totals[r]
    for h in range(HEADS):
        dec_out[:, h * HD : (h + 1) * HD] = out_s[h * DEC : (h + 1) * DEC, :].astype(BF16)
    for k in range(2):
        hand_on(k).wait()


def per_device(pre_x, w_query, w_key, w_value, dec_x, cache, lengths, page_table, dest_slots):
    hbm = pl.BlockSpec(memory_space=pltpu.MemorySpace.HBM)
    vmem = pl.BlockSpec(memory_space=pltpu.MemorySpace.VMEM)
    smem = pl.BlockSpec(memory_space=pltpu.MemorySpace.SMEM)
    pre, dq, dkv, new = pl.pallas_call(
        prefill,
        out_shape=(
            jax.ShapeDtypeStruct((TOK, HEADS * HD), BF16),
            jax.ShapeDtypeStruct((HEADS * DEC, HD), BF16),
            jax.ShapeDtypeStruct((2, DEC, HD), BF16),
            jax.ShapeDtypeStruct((2, NEW_ROWS, HD), BF16),
        ),
        in_specs=[hbm] * 5,
        out_specs=(vmem,) * 4,
        scratch_shapes=[
            pltpu.VMEM((ALL, D), BF16),
            pltpu.VMEM((D, 2 * HD), BF16),
            pltpu.VMEM((D, HEADS * HD), BF16),
            pltpu.VMEM((GROUPS, 2, TOK, HD), BF16),
            pltpu.VMEM((PAIRS, HD, 2 * TOK), BF16),
            pltpu.VMEM((PAIRS, 2 * TOK, 2 * HD), BF16),
            pltpu.VMEM((LENT, TOK, HD), BF16),
            pltpu.VMEM((TILES + LENT, TILE, HD), BF16),
            pltpu.VMEM((TOK, 2 * HD), F32),
            pltpu.VMEM((TILES + LENT, TILE, 2 * HD), F32),
            pltpu.VMEM((TILES + LENT, TILE, HD), F32),
            pltpu.VMEM((TILE, 2 * TOK), F32),
            pltpu.VMEM((TILE, 2 * TOK), F32),
            pltpu.VMEM((TILE, 2 * TOK), BF16),
            pltpu.VMEM((TILE, 2 * TOK), BF16),
            pltpu.SemaphoreType.DMA((XC,)),
            pltpu.SemaphoreType.DMA((XC,)),
            pltpu.SemaphoreType.DMA((XC,)),
            pltpu.SemaphoreType.DMA((QN * QK,)),
            pltpu.SemaphoreType.DMA,
            pltpu.SemaphoreType.DMA((7,)),
            pltpu.SemaphoreType.DMA((7,)),
            pltpu.SemaphoreType.DMA((len(SENDS),)),
            pltpu.SemaphoreType.DMA((32,)),
            pltpu.SemaphoreType.DMA((LENT,)),
            pltpu.SemaphoreType.DMA((LENT,)),
            pltpu.SemaphoreType.DMA((LENT,)),
            pltpu.SemaphoreType.DMA((LENT,)),
        ],
        compiler_params=pltpu.CompilerParams(
            collective_id=0, has_side_effects=True, vmem_limit_bytes=63 * 1024 * 1024
        ),
    )(pre_x, w_query, w_key, w_value, dec_x.reshape(DEC, D // 8))
    pre_out, dec_out = pl.pallas_call(
        decode,
        out_shape=(
            jax.ShapeDtypeStruct((TOK, HEADS * HD), BF16),
            jax.ShapeDtypeStruct((DEC, HEADS * HD), BF16),
        ),
        in_specs=[smem] * 3 + [hbm] * 2 + [vmem] * 3,
        out_specs=(hbm, vmem),
        scratch_shapes=[
            pltpu.VMEM((TOK, HEADS * HD), BF16),
            pltpu.VMEM((ROWS, 2 * MAXP * PAGE, HD), BF16),
            pltpu.VMEM((2 * NEW_ROWS, HD), F32),
            pltpu.VMEM((CACHE_ROWS, HD), BF16),
            pltpu.VMEM((HEADS * DEC, HD), F32),
            pltpu.VMEM((HEADS * DEC, HD), F32),
            pltpu.SemaphoreType.DMA((2,)),
            pltpu.SemaphoreType.DMA((2,)),
            pltpu.SemaphoreType.DMA,
        ],
        compiler_params=pltpu.CompilerParams(vmem_limit_bytes=63 * 1024 * 1024),
    )(page_table, lengths, dest_slots, pre, cache.reshape(CACHE_ROWS, HD), dq, dkv, new)
    return pre_out, dec_out.reshape(STEPS, ROWS, HEADS * HD)


def solution(mesh):
    in_specs = (
        P(("seq", "pool"), None),
        P(None, "tensor"),
        P(None, "tensor"),
        P(None, "tensor"),
        P(None, ("seq", "pool"), "tensor"),
        P(("seq", "pool"), None, None, "tensor"),
        P(("seq", "pool")),
        P(("seq", "pool"), None),
        P(("seq", "pool"), None),
    )
    out_specs = (P(("seq", "pool"), "tensor"), P(None, ("seq", "pool"), "tensor"))
    return jax.shard_map(
        per_device, mesh=mesh, in_specs=in_specs, out_specs=out_specs, check_vma=False
    )
```

```python
import functools

import jax
import jax.numpy as jnp
from jax import lax
from jax.experimental import pallas as pl
from jax.experimental.pallas import tpu as pltpu
from jax.sharding import PartitionSpec as P

MESH = pl.DeviceIdType.MESH
BF16 = jnp.bfloat16
F32 = jnp.float32

D = 8192
HD = 128
HEADS = 8
TOK = 512
GROUPS = 16
PAGE = 16
MAXP = 16
PAGES = 128
ROWS = 8
STEPS = 4
DEC = ROWS * STEPS
ALL = TOK + DEC
TILES = HEADS
TILE = TOK
CACHE_ROWS = PAGES * PAGE * 2
NEW_ROWS = 512
SCALE = HD ** (-0.5) * 1.4426950408889634
LOW = -1e30
XC = 4
QK = 2
QN = 4
LENT = 4
TAKES = (3, 3, 3, 2, 2, 1, 1, 0)
PAIRS = GROUPS // 2
CHUNK = 16
POLLS = {2: (1, 2), 3: (3, 4, 5)}
JOIN, MISSED, PART, ENDS = 2, 4, 6, 10
TURNS = {1: (6, 7, 8, 9, 10, 11), PART: (12, 13, 14, 15)}

ORDER = (
    (0, 0), (3, 0), (1, 0), (0, 3), (0, 1), (2, 0), (3, 3), (3, 1),
    (1, 3), (1, 1), (2, 3), (2, 1), (0, 2), (3, 2), (1, 2), (2, 2),
)


def sends_after(event):
    near, far = event
    sends = []
    if near == 0 and far == 0:
        sends += [(0, "A+"), (0, "A-"), (1, "A+"), (1, "A-")]
    elif far == 0 and near == 3:
        sends += [(0, "A+")]
    elif far == 0 and near == 1:
        sends += [(1, "A-")]
    if far == 0:
        sends += [(0, "B+"), (0, "B-"), (1, "B+"), (1, "B-")]
    elif far == 3:
        sends += [(0, "B+")]
    elif far == 1:
        sends += [(1, "B-")]
    return sends


def seen_from(event, direction):
    near, far = event
    step = 1 if direction[1] == "+" else -1
    if direction[0] == "A":
        return ((near - step) % 4, far)
    return (near, (far - step) % 4)


SENDS = [(event, half, way) for event in ORDER for half, way in sends_after(event)]


def prefill(
    px, wq, wk, wv, dx,
    pre_out, dq_out, dkv_out, new_out,
    x_s, wkv_s, wq_s, kv_s, kt_s, va_s, of_s, q_s, pacc, acc, m_s, sa_s, sb_s, pa_s, pb_s,
    xsem, wksem, wvsem, qsem, dsem_own, dsend, drecv, ssem, rsem, qsend, qrecv, osend, orecv,
):
    seq, tensor, pool = lax.axis_index("seq"), lax.axis_index("tensor"), lax.axis_index("pool")
    x, y, core = seq // 2, pool * 2 + seq % 2, tensor % 2
    g = seq * 2 + pool
    low = g < 8
    other = 15 - g
    last = jnp.where(low, other, g)
    pair = jnp.where(low, g, other)
    count = sum(jnp.where(pair == k, TAKES[k], 0) for k in range(8))
    partner = {"seq": 7 - seq, "pool": 1 - pool}

    def place(near, far):
        ax, ay = (x + near) % 4, (y + far) % 4
        bx, by = (x + far) % 4, (y + near) % 4
        return jnp.where(core == 0, ax, bx), jnp.where(core == 0, ay, by)

    def slot_of(near, far):
        px_, py_ = place(near, far)
        return px_ * 4 + (py_ % 2) * 2 + py_ // 2

    def device(near, far):
        px_, py_ = place(near, far)
        return {"seq": px_ * 2 + py_ % 2, "pool": py_ // 2}

    ways = {"A+": device(1, 0), "A-": device(3, 0), "B+": device(0, 1), "B-": device(0, 3)}

    def x_copy(c):
        cols = pl.ds(pl.multiple_of(c * (D // XC), D // XC), D // XC)
        return pltpu.make_async_copy(px.at[:, cols], x_s.at[pl.ds(0, TOK), cols], xsem.at[c])

    def w_copy(c, ref, at, sem):
        rows = pl.ds(pl.multiple_of(c * (D // XC), D // XC), D // XC)
        return pltpu.make_async_copy(ref.at[rows, :], wkv_s.at[rows, pl.ds(at, HD)], sem.at[c])

    def q_copy(n, k):
        rows = pl.ds(k * (D // QK), D // QK)
        cols = pl.ds(pl.multiple_of(n * (HEADS * HD // QN), HEADS * HD // QN), HEADS * HD // QN)
        return pltpu.make_async_copy(wq.at[rows, cols], wq_s.at[rows, cols], qsem.at[n * QK + k])

    my_cols = pl.ds(pl.multiple_of(tensor * (D // 8), D // 8), D // 8)
    dec_own = pltpu.make_async_copy(dx, x_s.at[pl.ds(TOK, DEC), my_cols], dsem_own)

    for c in range(XC):
        x_copy(c).start()
        w_copy(c, wk, 0, wksem).start()
        w_copy(c, wv, HD, wvsem).start()
    dec_own.start()

    barrier = pltpu.get_barrier_semaphore()
    for way in ways.values():
        pl.semaphore_signal(barrier, inc=1, device_id=way, device_id_type=MESH)
    pl.semaphore_signal(barrier, inc=1, device_id=partner, device_id_type=MESH)
    for k in range(1, 8):
        pl.semaphore_signal(
            barrier, inc=1, device_id={"tensor": (tensor + k) % 8}, device_id_type=MESH
        )
    pl.semaphore_wait(barrier, 12)

    def dec_copy(k):
        return pltpu.make_async_remote_copy(
            src_ref=dx,
            dst_ref=x_s.at[pl.ds(TOK, DEC), my_cols],
            send_sem=dsend.at[k - 1],
            recv_sem=drecv.at[k - 1],
            device_id={"tensor": (tensor + k) % 8},
            device_id_type=MESH,
        )

    def dec_arrival(k):
        cols = pl.ds(pl.multiple_of(((tensor + 8 - k) % 8) * (D // 8), D // 8), D // 8)
        return pltpu.make_async_remote_copy(
            src_ref=dx,
            dst_ref=x_s.at[pl.ds(TOK, DEC), cols],
            send_sem=dsend.at[k - 1],
            recv_sem=drecv.at[k - 1],
            device_id={"tensor": (tensor + k) % 8},
            device_id_type=MESH,
        )

    for k in range(1, 8):
        dec_copy(k).start()

    def kv_copy(number):
        event, half, way = SENDS[number]
        slot = slot_of(*event)
        near, far = seen_from(event, way)
        return pltpu.make_async_remote_copy(
            src_ref=kv_s.at[slot, half],
            dst_ref=kv_s.at[slot, half],
            send_sem=ssem.at[number],
            recv_sem=rsem.at[(near * 4 + far) * 2 + half],
            device_id=ways[way],
            device_id_type=MESH,
        )

    def pass_on(event):
        for number, (of, _, _) in enumerate(SENDS):
            if of == event:
                kv_copy(number).start()

    def arrive(event):
        near, far = event
        slot = slot_of(near, far)
        for half in range(2):
            pltpu.make_async_remote_copy(
                src_ref=kv_s.at[slot, half],
                dst_ref=kv_s.at[slot, half],
                send_sem=ssem.at[0],
                recv_sem=rsem.at[(near * 4 + far) * 2 + half],
                device_id=ways["A+"],
                device_id_type=MESH,
            ).wait_recv()
        pass_on(event)

    def lend(t):
        return pltpu.make_async_remote_copy(
            src_ref=q_s.at[t],
            dst_ref=q_s.at[TILES + t],
            send_sem=qsend.at[t],
            recv_sem=qrecv.at[t],
            device_id=partner,
            device_id_type=MESH,
        )

    def give_back(t):
        return pltpu.make_async_remote_copy(
            src_ref=of_s.at[t],
            dst_ref=pre_out.at[:, pl.ds(t * HD, HD)],
            send_sem=osend.at[t],
            recv_sem=orecv.at[t],
            device_id=partner,
            device_id_type=MESH,
        )

    def clear(j, carry):
        acc[j] = jnp.zeros((TILE, 2 * HD), F32)
        m_s[j] = jnp.full((TILE, HD), LOW, F32)
        return carry

    def fill(i, carry):
        va_s[i, :, HD:] = jnp.ones((2 * TOK, HD), BF16)
        return carry

    lax.fori_loop(0, TILES + LENT, clear, 0)
    lax.fori_loop(0, PAIRS, fill, 0)

    def kv_step(c, carry):
        x_copy(c).wait()
        w_copy(c, wk, 0, wksem).wait()
        w_copy(c, wv, HD, wvsem).wait()
        for k in range(QN * QK):

            @pl.when(c == 2 + k // 4)
            def _():
                q_copy(k // QK, k % QK).start()

        at = pl.ds(pl.multiple_of(c * (D // XC), D // XC), D // XC)
        part = jnp.dot(x_s[0:TOK, at], wkv_s[at, :], preferred_element_type=F32)

        @pl.when(c == 0)
        def _():
            pacc[0:TOK, 0:256] = part

        @pl.when(c > 0)
        def _():
            pacc[0:TOK, 0:256] += part

        return carry

    lax.fori_loop(0, XC, kv_step, 0)
    kv_s[g, 0] = pacc[0:TOK, 0:HD].astype(BF16)
    kv_s[g, 1] = pacc[0:TOK, HD : 2 * HD].astype(BF16)
    pass_on(ORDER[0])

    dec_own.wait()
    for k in range(1, 8):
        dec_arrival(k).wait_recv()

    width = HEADS * HD // QN

    def query_step(n, carry):
        for k in range(QK):
            q_copy(n, k).wait()
        part = jnp.dot(
            x_s[...],
            wq_s[:, pl.ds(pl.multiple_of(n * width, width), width)],
            preferred_element_type=F32,
        )
        for hh in range(HEADS // QN):
            h = n * (HEADS // QN) + hh
            scaled = (part[:, hh * HD : (hh + 1) * HD] * SCALE).astype(BF16)
            q_s[h] = scaled[0:TOK]
            dq_out[pl.ds(pl.multiple_of(h * DEC, DEC), DEC), :] = scaled[TOK:ALL]

        @pl.when(n == QN // 2 - 1)
        def _():
            for t in range(LENT):

                @pl.when(jnp.logical_not(low) & (t < count))
                def _():
                    lend(t).start()

        for at, events in POLLS.items():

            @pl.when(n == at)
            def _():
                for e in events:
                    arrive(ORDER[e])

        return carry

    lax.fori_loop(0, QN, query_step, 0)
    dkv = jnp.dot(x_s[TOK:ALL, :], wkv_s[...], preferred_element_type=F32)
    dkv_out[0] = dkv[:, 0:HD].astype(BF16)
    dkv_out[1] = dkv[:, HD : 2 * HD].astype(BF16)

    def prepare(slot):
        side = pl.ds(pl.multiple_of((slot % 2) * TOK, TOK), TOK)
        kt_s[slot // 2, :, side] = kv_s[slot, 0].T
        va_s[slot // 2, side, 0:HD] = kv_s[slot, 1]

    def part_of(item):
        j, block, whole = item
        if whole:
            return j, block, slice(0, 2 * TOK), 2 * TOK
        return j, block // 2, pl.ds(pl.multiple_of((block % 2) * TOK, TOK), TOK), TOK

    def score(item, buf):
        j, two, side, width = part_of(item)
        at = 0 if width == 2 * TOK else pl.multiple_of((item[1] % 2) * TOK, TOK)

        def step(n):
            keys = kt_s[two, :, pl.ds(at + n * 2 * HD, 2 * HD)]
            buf[:, n * 2 * HD : (n + 1) * 2 * HD] = jnp.dot(
                q_s[j], keys, preferred_element_type=F32
            )

        return [functools.partial(step, n) for n in range(width // (2 * HD))]

    def absorb(item, buf, weights, ahead, beside=()):
        j, two, side, width = part_of(item)
        if ahead is not None:
            lead = lax.broadcasted_iota(jnp.int32, (CHUNK, HD), 1) - lax.broadcasted_iota(
                jnp.int32, (CHUNK, HD), 0
            )
        for c in range(TILE // CHUNK):
            if beside and c % (TILE // CHUNK // len(beside)) == 0:
                beside[c // (TILE // CHUNK // len(beside))]()
            rows = slice(c * CHUNK, (c + 1) * CHUNK)
            cuts = [buf[rows, k * HD : (k + 1) * HD] for k in range(width // HD)]
            if ahead is not None:
                cuts = [
                    jnp.where(lead <= c * CHUNK - k * HD + ahead, cut, LOW)
                    for k, cut in enumerate(cuts)
                ]
            if isinstance(ahead, int):
                clear_from = (ahead + (c + 1) * CHUNK - 1) // HD + 1
                for k in range(clear_from, len(cuts)):
                    weights[rows, k * HD : (k + 1) * HD] = jnp.zeros((CHUNK, HD), BF16)
                cuts = cuts[:clear_from]
            old = m_s[j, rows, :]
            best = functools.reduce(jnp.maximum, cuts)
            top = jnp.maximum(
                old, jnp.broadcast_to(jnp.max(best, axis=1, keepdims=True), (CHUNK, HD))
            )
            for k, cut in enumerate(cuts):
                weights[rows, k * HD : (k + 1) * HD] = jnp.exp2(cut - top).astype(BF16)
            shrink = jnp.exp2(old - top)
            m_s[j, rows, :] = top
            acc[j, rows, 0:HD] = acc[j, rows, 0:HD] * shrink
            acc[j, rows, HD:] = acc[j, rows, HD:] * shrink
        acc[j] += jnp.dot(weights[:, 0:width], va_s[two, side, :], preferred_element_type=F32)

    def run(n, item, ahead=None):
        @pl.when(n > 0)
        def _():
            for step in score(item(0), sa_s):
                step()

        def two(t, carry):
            now, later, last_one = item(2 * t), item(2 * t + 1), item(jnp.minimum(2 * t + 2, n - 1))
            absorb(now, sa_s, pa_s, ahead, score(later, sb_s))
            absorb(later, sb_s, pb_s, ahead, score(last_one, sa_s))
            return carry

        lax.fori_loop(0, n // 2, two, 0)

        @pl.when(n % 2 == 1)
        def _():
            absorb(item(n - 1), sa_s, pa_s, ahead)

    first = jnp.where(low, 0, count)
    own = TILES - first
    taken = jnp.where(low, count, 0)

    prepare(g)
    run(own, lambda t: (first + t, g, False), 0)

    def finish(j):
        return (acc[j, :, 0:HD] / acc[j, :, HD:]).astype(BF16)

    def pair_at(i):
        half = i // 4
        step = jnp.where(core == 0, i % 4, i // 2)
        across = jnp.where(core == 0, 1 - half, 1 - i % 2)
        near = jnp.where(step == 0, 0, jnp.where(step == 1, 3, step - 1))
        return ((x + near) % 4) * 2 + (y + across) % 2

    def prepare_pair(i):
        for side in range(2):
            slot = 2 * pair_at(i) + side

            @pl.when(slot <= last)
            def _():
                prepare(slot)

    due = range(PAIRS // 2, PAIRS)
    wanted = [jnp.where(pair_at(i) < last // 2, 1, 0) for i in due]
    before = [sum(wanted[:k], jnp.int32(0)) for k in range(len(due))]

    def due_at(t):
        return sum(
            jnp.where((wanted[k] == 1) & (before[k] == t), pair_at(due[k]), 0)
            for k in range(len(due))
        )

    def turn(s, carry):
        for at, events in TURNS.items():

            @pl.when(s == at)
            def _():
                for e in events:
                    arrive(ORDER[e])

        i = jnp.where(s < MISSED, s, jnp.where(s < PART, s - MISSED, s - PART + PAIRS // 2))

        @pl.when(s < MISSED)
        def _():
            prepare_pair(i)

        @pl.when(s == JOIN)
        def _():
            for t in range(LENT):

                @pl.when(low & (t < count))
                def _():
                    lend(t).wait_recv()

        @pl.when((s == MISSED) & (taken > 0))
        def _():
            def single(k, carry):
                block = last - k
                prepare(block)
                run(taken, lambda t: (TILES + t, block, False), k * TOK)
                return carry

            lax.fori_loop(0, 1 + last % 2, single, 0)

        @pl.when(s == PART)
        def _():
            def rest(k, carry):
                prepare_pair(k)
                return carry

            lax.fori_loop(PAIRS // 2, PAIRS, rest, 0)

            def away(j, carry):
                run(before[-1] + wanted[-1], lambda t: (j, due_at(t), True))
                of_s[j - TILES] = finish(j)
                for f in range(LENT):

                    @pl.when(j == TILES + f)
                    def _():
                        give_back(f).start()

                return carry

            lax.fori_loop(TILES, TILES + taken, away, 0)
            run(own * (g % 2), lambda t: (first + t, g - 1, False))

        two = pair_at(i)
        join = (s >= JOIN) & (s < PART) & (two < last // 2)
        start = jnp.where((two < g // 2) & ((s < MISSED) | (s >= PART)), first, TILES)
        stop = jnp.where(join, TILES + taken, TILES)
        run(jnp.maximum(stop - start, 0), lambda t: (start + t, two, True))
        return carry

    lax.fori_loop(0, ENDS, turn, 0)

    for j in range(TILES):

        @pl.when(j >= first)
        def _():
            pre_out[:, j * HD : (j + 1) * HD] = finish(j)

    mine = NEW_ROWS // GROUPS
    at = pl.ds(pl.multiple_of(g * mine, mine), mine)
    for src in range(GROUPS):
        for half in range(2):
            new_out[half, src * mine : (src + 1) * mine, :] = kv_s[src, half, at, :]

    for t in range(LENT):

        @pl.when((t < count) & low)
        def _():
            give_back(t).wait_send()

        @pl.when((t < count) & jnp.logical_not(low))
        def _():
            lend(t).wait_send()
            give_back(t).wait_recv()

    for k in range(1, 8):
        dec_copy(k).wait_send()
    for number in range(len(SENDS)):
        kv_copy(number).wait_send()


def decode(
    table, lens, dest, pre_in, cache, dq_in, dkv_in, new_in,
    pre_out, dec_out,
    dq, dkv, new, pre_s, pool_s, mix_s, page_s, dq_s, out_s, in_sem, out_sem, pool_sem, small_sem,
):
    half = TOK // 2

    def take(k):
        rows = pl.ds(k * half, half)
        return pltpu.make_async_copy(pre_in.at[rows, :], pre_s.at[rows, :], in_sem.at[k])

    def hand_on(k):
        rows = pl.ds(k * half, half)
        return pltpu.make_async_copy(pre_s.at[rows, :], pre_out.at[rows, :], out_sem.at[k])

    pool = pltpu.make_async_copy(cache, page_s, pool_sem)
    small = [
        pltpu.make_async_copy(src, dst, small_sem.at[k])
        for k, (src, dst) in enumerate(((new_in, new), (dq_in, dq), (dkv_in, dkv)))
    ]
    small[0].start()
    pool.start()
    small[1].start()
    small[2].start()
    for k in range(2):
        take(k).start()

    small[0].wait()
    mix_s[pl.ds(0, NEW_ROWS, stride=2), :] = new[0].astype(F32)
    mix_s[pl.ds(1, NEW_ROWS, stride=2), :] = new[1].astype(F32)
    pool.wait()
    for m in range(TOK // PAGE):
        at = pl.ds(pl.multiple_of(dest[0, m] * 2 * PAGE, 2 * PAGE), 2 * PAGE)
        page_s[at, :] = mix_s[m * 2 * PAGE : (m + 1) * 2 * PAGE, :].astype(BF16)
    small[1].wait()
    small[2].wait()
    dq_s[...] = dq[...].astype(F32)
    for r in range(ROWS):
        for j in range(MAXP):
            at = pl.ds(pl.multiple_of(table[r, j] * 2 * PAGE, 2 * PAGE), 2 * PAGE)
            pool_s[r, j * 2 * PAGE : (j + 1) * 2 * PAGE, :] = page_s[at, :]

    for k in range(2):
        take(k).wait()
        hand_on(k).start()

    wide = 2 * MAXP * PAGE
    queries = HEADS * STEPS
    column = lax.broadcasted_iota(jnp.int32, (queries, wide), 1)
    query = lax.broadcasted_iota(jnp.int32, (queries, DEC), 0)
    token = lax.broadcasted_iota(jnp.int32, (queries, DEC), 1)
    so_far = (token >> 3) <= (query & (STEPS - 1))
    s_old, s_new = [], []
    for r in range(ROWS):
        q = dq_s[pl.ds(r, queries, stride=ROWS), :].astype(BF16)

        def scores(keys):
            return lax.dot_general(q, keys, (((1,), (1,)), ((), ())), preferred_element_type=F32)

        live = ((column & 1) == 0) & (column < 2 * lens[r])
        s_old.append(jnp.where(live, scores(pool_s[r]), LOW))
        s_new.append(jnp.where(so_far & ((token & (ROWS - 1)) == r), scores(dkv[0]), LOW))
    tops = [
        jnp.maximum(jnp.max(a, axis=1, keepdims=True), jnp.max(b, axis=1, keepdims=True))
        for a, b in zip(s_old, s_new)
    ]
    p_old = [jnp.exp2(a - top) for a, top in zip(s_old, tops)]
    p_new = [jnp.exp2(b - top) for b, top in zip(s_new, tops)]
    totals = [
        jnp.sum(a, axis=1, keepdims=True) + jnp.sum(b, axis=1, keepdims=True)
        for a, b in zip(p_old, p_new)
    ]
    p_old = [
        jnp.concatenate(
            [pltpu.roll(a[:, k * HD : (k + 1) * HD], 1, 1) for k in range(wide // HD)], axis=1
        ).astype(BF16)
        for a in p_old
    ]
    for r in range(ROWS):
        mixed = jnp.dot(p_old[r], pool_s[r], preferred_element_type=F32) + jnp.dot(
            p_new[r].astype(BF16), dkv[1], preferred_element_type=F32
        )
        out_s[pl.ds(r, queries, stride=ROWS), :] = mixed / totals[r]
    for h in range(HEADS):
        dec_out[:, h * HD : (h + 1) * HD] = out_s[h * DEC : (h + 1) * DEC, :].astype(BF16)
    for k in range(2):
        hand_on(k).wait()


def per_device(pre_x, w_query, w_key, w_value, dec_x, cache, lengths, page_table, dest_slots):
    hbm = pl.BlockSpec(memory_space=pltpu.MemorySpace.HBM)
    vmem = pl.BlockSpec(memory_space=pltpu.MemorySpace.VMEM)
    smem = pl.BlockSpec(memory_space=pltpu.MemorySpace.SMEM)
    pre, dq, dkv, new = pl.pallas_call(
        prefill,
        out_shape=(
            jax.ShapeDtypeStruct((TOK, HEADS * HD), BF16),
            jax.ShapeDtypeStruct((HEADS * DEC, HD), BF16),
            jax.ShapeDtypeStruct((2, DEC, HD), BF16),
            jax.ShapeDtypeStruct((2, NEW_ROWS, HD), BF16),
        ),
        in_specs=[hbm] * 5,
        out_specs=(vmem,) * 4,
        scratch_shapes=[
            pltpu.VMEM((ALL, D), BF16),
            pltpu.VMEM((D, 2 * HD), BF16),
            pltpu.VMEM((D, HEADS * HD), BF16),
            pltpu.VMEM((GROUPS, 2, TOK, HD), BF16),
            pltpu.VMEM((PAIRS, HD, 2 * TOK), BF16),
            pltpu.VMEM((PAIRS, 2 * TOK, 2 * HD), BF16),
            pltpu.VMEM((LENT, TOK, HD), BF16),
            pltpu.VMEM((TILES + LENT, TILE, HD), BF16),
            pltpu.VMEM((TOK, 2 * HD), F32),
            pltpu.VMEM((TILES + LENT, TILE, 2 * HD), F32),
            pltpu.VMEM((TILES + LENT, TILE, HD), F32),
            pltpu.VMEM((TILE, 2 * TOK), F32),
            pltpu.VMEM((TILE, 2 * TOK), F32),
            pltpu.VMEM((TILE, 2 * TOK), BF16),
            pltpu.VMEM((TILE, 2 * TOK), BF16),
            pltpu.SemaphoreType.DMA((XC,)),
            pltpu.SemaphoreType.DMA((XC,)),
            pltpu.SemaphoreType.DMA((XC,)),
            pltpu.SemaphoreType.DMA((QN * QK,)),
            pltpu.SemaphoreType.DMA,
            pltpu.SemaphoreType.DMA((7,)),
            pltpu.SemaphoreType.DMA((7,)),
            pltpu.SemaphoreType.DMA((len(SENDS),)),
            pltpu.SemaphoreType.DMA((32,)),
            pltpu.SemaphoreType.DMA((LENT,)),
            pltpu.SemaphoreType.DMA((LENT,)),
            pltpu.SemaphoreType.DMA((LENT,)),
            pltpu.SemaphoreType.DMA((LENT,)),
        ],
        compiler_params=pltpu.CompilerParams(
            collective_id=0, has_side_effects=True, vmem_limit_bytes=63 * 1024 * 1024
        ),
    )(pre_x, w_query, w_key, w_value, dec_x.reshape(DEC, D // 8))
    pre_out, dec_out = pl.pallas_call(
        decode,
        out_shape=(
            jax.ShapeDtypeStruct((TOK, HEADS * HD), BF16),
            jax.ShapeDtypeStruct((DEC, HEADS * HD), BF16),
        ),
        in_specs=[smem] * 3 + [hbm] * 5,
        out_specs=(hbm, vmem),
        scratch_shapes=[
            pltpu.VMEM((HEADS * DEC, HD), BF16),
            pltpu.VMEM((2, DEC, HD), BF16),
            pltpu.VMEM((2, NEW_ROWS, HD), BF16),
            pltpu.VMEM((TOK, HEADS * HD), BF16),
            pltpu.VMEM((ROWS, 2 * MAXP * PAGE, HD), BF16),
            pltpu.VMEM((2 * NEW_ROWS, HD), F32),
            pltpu.VMEM((CACHE_ROWS, HD), BF16),
            pltpu.VMEM((HEADS * DEC, HD), F32),
            pltpu.VMEM((HEADS * DEC, HD), F32),
            pltpu.SemaphoreType.DMA((2,)),
            pltpu.SemaphoreType.DMA((2,)),
            pltpu.SemaphoreType.DMA,
            pltpu.SemaphoreType.DMA((3,)),
        ],
        compiler_params=pltpu.CompilerParams(vmem_limit_bytes=63 * 1024 * 1024),
    )(page_table, lengths, dest_slots, pre, cache.reshape(CACHE_ROWS, HD), dq, dkv, new)
    return pre_out, dec_out.reshape(STEPS, ROWS, HEADS * HD)


def solution(mesh):
    in_specs = (
        P(("seq", "pool"), None),
        P(None, "tensor"),
        P(None, "tensor"),
        P(None, "tensor"),
        P(None, ("seq", "pool"), "tensor"),
        P(("seq", "pool"), None, None, "tensor"),
        P(("seq", "pool")),
        P(("seq", "pool"), None),
        P(("seq", "pool"), None),
    )
    out_specs = (P(("seq", "pool"), "tensor"), P(None, ("seq", "pool"), "tensor"))
    return jax.shard_map(
        per_device, mesh=mesh, in_specs=in_specs, out_specs=out_specs, check_vma=False
    )
```
